512 devices in a mesh: tm: 32 (over x, y_lo, core), seq: 16 (over z, y_hi).
Axes of the slice: x: 4, y: 8 (y_hi: 2, y_lo: 4; y = y_hi * 4 + y_lo), z: 8, core: 2. Of those that a mesh axis runs over, the one named last changes fastest.
Arguments:
- query_in: bfloat16 [65536, 1024], P(('tm', 'seq')), may hold values from -6 to 6
- key_in: bfloat16 [65536, 1024], P(('tm', 'seq')), may hold values from -6 to 6
- value_in: bfloat16 [65536, 1024], P(('tm', 'seq')), may hold values from -6 to 6
- residual: bfloat16 [65536, 1024], P(('tm', 'seq')), may hold values from -6 to 6
- layer_gain: float32 [1024], replicated, may hold values from 0.5 to 1.5
- proj_weight: bfloat16 [1024, 2048], P(None, 'seq'), may hold values from -0.1875 to 0.1875
- conv_kernel: float32 [31, 1024], replicated, may hold values from -1 to 1
- batch_gamma: float32 [1024], replicated, may hold values from 0.25 to 1.75
- batch_beta: float32 [1024], replicated, may hold values from -3 to 3
- stale_mean: float32 [1024], replicated, may hold values from -1 to 1
- stale_variance: float32 [1024], replicated, may hold values from 0.05 to 0.5
- grad_conv: bfloat16 [65536, 1024], P(('tm', 'seq')), may hold values from -6 to 6
- grad_stream_in: bfloat16 [65536, 1024], P(('tm', 'seq')), may hold values from -6 to 6
Outputs:
- grad_query: bfloat16 [65536, 1024], P(('tm', 'seq'))
- grad_key: bfloat16 [65536, 1024], P(('tm', 'seq'))
- grad_value: bfloat16 [65536, 1024], P(('tm', 'seq'))
- grad_stream: bfloat16 [65536, 1024], P(('tm', 'seq'))
- grad_kernel: float32 [31, 1024], replicated
- grad_affine: float32 [2, 1024], replicated
- moments: float32 [2, 1024], replicated
The draws below stay inside these ranges and needn't reach their ends.
All inputs are finite; a program needn't handle non-finite values.
Results may differ from the reference program's by a relative error of at most 0.019.
Values may be sent and summed in bfloat16 or wider, within the bound.
No kernel may reach another device: no remote copies, remote signals or barrier semaphores. Data moves between devices by JAX's collectives and lax.ppermute only.
A program may use at most 64 MiB of HBM per device.

```python
import math
import jax
import jax.numpy as jnp
from jax import lax

D = 1024
HEADS = 16
HD = 64
KW = 31
FR_DEV = 128
FRAMES = 65536
N_TM = 32
N_SEQ = 16


def draw_query_in(key, part):
    key = jax.random.fold_in(key, 11)
    values = jnp.clip(jax.random.normal(key, (FRAMES, D), jnp.float32), -6.0, 6.0)
    return values.astype(jnp.bfloat16)


def draw_key_in(key, part):
    key = jax.random.fold_in(key, 13)
    values = jnp.clip(jax.random.normal(key, (FRAMES, D), jnp.float32), -6.0, 6.0)
    return values.astype(jnp.bfloat16)


def block_levels(own_key, shape, pieces, least, largest):
    level, own = 1.0, jax.random.fold_in(own_key, 6)
    for position, blocks in pieces:
        heights = jnp.exp(jax.random.uniform(jax.random.fold_in(own, position), (blocks,), jnp.float32, least / len(pieces), largest / len(pieces)))
        level = level * jnp.repeat(heights, shape[position] // blocks).reshape([-1 if axis == position else 1 for axis in range(len(shape))])
    return level


def bell_draw(own_key, extent, spread, reach, shards=(), kind=jnp.bfloat16):
    values = spread * jax.random.normal(own_key, extent, jnp.float32)
    if shards:
        values = values * block_levels(own_key, extent, shards, -0.22, 0.18)
    return jnp.clip(values, -reach, reach).astype(kind)


def setup_inputs(seed: int = 0) -> dict:
    key_of = jax.random.split(jax.random.key(seed), 14)
    query_in = draw_query_in(jax.random.fold_in(key_of[13], 71), 0)
    key_in = draw_key_in(jax.random.fold_in(key_of[13], 71), 0)
    value_in = bell_draw(key_of[2], (FRAMES, D), 1.0, 6.0, ((0, 512),))
    residual = bell_draw(key_of[3], (FRAMES, D), 1.0, 6.0, ((0, 512),))
    layer_gain = jnp.clip(1.0 + 0.1 * jax.random.normal(key_of[4], (D,), jnp.float32), 0.5, 1.5)
    proj_weight = bell_draw(key_of[5], (D, 2 * D), D ** -0.5, 0.1875, ((1, 16),))
    conv_kernel = bell_draw(key_of[6], (KW, D), KW ** -0.5, 1.0, (), jnp.float32)
    batch_gamma = jnp.clip(1.0 + 0.15 * jax.random.normal(key_of[7], (D,), jnp.float32), 0.25, 1.75)
    batch_beta = bell_draw(key_of[8], (D,), 0.5, 3.0, (), jnp.float32)
    stale_mean = bell_draw(key_of[9], (D,), 0.2, 1.0, (), jnp.float32)
    stale_variance = jnp.clip(jnp.exp(jax.random.uniform(key_of[10], (D,), jnp.float32, math.log(0.05), math.log(0.5))), 0.05, 0.5)
    grad_conv = bell_draw(key_of[11], (FRAMES, D), 1.0, 6.0, ((0, 512),))
    grad_stream_in = bell_draw(key_of[12], (FRAMES, D), 1.0, 6.0, ((0, 512),))
    return {"query_in": query_in, "key_in": key_in, "value_in": value_in, "residual": residual, "layer_gain": layer_gain, "proj_weight": proj_weight, "conv_kernel": conv_kernel, "batch_gamma": batch_gamma, "batch_beta": batch_beta, "stale_mean": stale_mean, "stale_variance": stale_variance, "grad_conv": grad_conv, "grad_stream_in": grad_stream_in}


epsilon = 1e-05

def stretch_forward(items):
    query_stretch, key_stretch, value_stretch = items
    score_scale = HD ** (-0.5)
    scores = jnp.einsum('qhd,khd->hqk', query_stretch.astype(jnp.float32), key_stretch.astype(jnp.float32)) * score_scale
    row_peak = lax.optimization_barrier(jnp.max(scores, axis=-1))
    logsum = row_peak + jnp.log(lax.optimization_barrier(jnp.sum(jnp.exp(scores - row_peak[..., None]), axis=-1)))
    weights = jnp.exp(scores - logsum[..., None]).astype(jnp.bfloat16)
    attended = jnp.einsum('hqk,khd->qhd', weights.astype(jnp.float32), value_stretch.astype(jnp.float32))
    return (attended.astype(jnp.bfloat16), logsum)

def stretch_backward(items):
    query_stretch, key_stretch, value_stretch, attended, logsum, grad_stretch = items
    score_scale = HD ** (-0.5)
    query_wide = query_stretch.astype(jnp.float32)
    key_wide = key_stretch.astype(jnp.float32)
    grad_wide = grad_stretch.astype(jnp.float32)
    scores = jnp.einsum('qhd,khd->hqk', query_wide, key_wide) * score_scale
    probs = jnp.exp(scores - logsum[..., None])
    weights = probs.astype(jnp.bfloat16)
    value_grad = jnp.einsum('hqk,qhd->khd', weights.astype(jnp.float32), grad_wide)
    grad_probs = jnp.einsum('qhd,khd->hqk', grad_wide, value_stretch.astype(jnp.float32))
    row_delta = lax.optimization_barrier(jnp.sum(grad_wide * attended.astype(jnp.float32), axis=-1)).T
    grad_scores = (probs * (grad_probs - row_delta[..., None])).astype(jnp.bfloat16)
    score_wide = grad_scores.astype(jnp.float32)
    query_grad = jnp.einsum('hqk,khd->qhd', score_wide, key_wide) * score_scale
    key_grad = jnp.einsum('hqk,qhd->khd', score_wide, query_wide) * score_scale
    return (query_grad.astype(jnp.bfloat16), key_grad.astype(jnp.bfloat16), value_grad.astype(jnp.bfloat16))

def reference(query_in, key_in, value_in, residual, layer_gain, proj_weight, conv_kernel, batch_gamma, batch_beta, stale_mean, stale_variance, grad_conv, grad_stream_in):
    stretch_len = FR_DEV * N_SEQ

    def stretched(matrix):
        return matrix.reshape(N_TM, stretch_len, HEADS, HD)
    attended, logsums = lax.map(stretch_forward, (stretched(query_in), stretched(key_in), stretched(value_in)))
    attn_out = attended.reshape(FRAMES, D)
    stream = residual.astype(jnp.float32) + attn_out.astype(jnp.float32)
    row_mean = lax.optimization_barrier(jnp.mean(stream, axis=1, keepdims=True))
    centred = stream - row_mean
    inv_std = lax.rsqrt(lax.optimization_barrier(jnp.mean(centred * centred, axis=1, keepdims=True)) + epsilon)
    normed = centred * inv_std
    normed_low = (normed * layer_gain).astype(jnp.bfloat16)
    projected = jnp.dot(normed_low, proj_weight, preferred_element_type=jnp.float32)
    linear_half = projected[:, :D]
    gate_sig = jax.nn.sigmoid(projected[:, D:])
    glu_out = (linear_half * gate_sig).astype(jnp.bfloat16)
    half_span = KW // 2
    glu_ext = jnp.pad(glu_out, ((half_span, half_span), (0, 0)))
    conv_sum = jnp.zeros((FRAMES, D), jnp.float32)
    for offset in range(KW):
        conv_sum = conv_sum + conv_kernel[offset] * glu_ext[offset:offset + FRAMES].astype(jnp.float32)
    inv_scale = lax.rsqrt(stale_variance + epsilon)
    zhat = (conv_sum - stale_mean) * inv_scale
    shifted = batch_gamma * zhat + batch_beta
    moments = jnp.stack([lax.optimization_barrier(jnp.sum(conv_sum, axis=0)), lax.optimization_barrier(jnp.sum(conv_sum * conv_sum, axis=0))]) / FRAMES
    sig_shift = jax.nn.sigmoid(shifted)
    grad_shift = grad_conv.astype(jnp.float32) * sig_shift * (1.0 + shifted * (1.0 - sig_shift))
    grad_affine = jnp.stack([lax.optimization_barrier(jnp.sum(grad_shift * zhat, axis=0)), lax.optimization_barrier(jnp.sum(grad_shift, axis=0))])
    grad_conv_out = (grad_shift * batch_gamma * inv_scale).astype(jnp.bfloat16)
    grad_wide = grad_conv_out.astype(jnp.float32)
    kernel_rows = []
    for offset in range(KW):
        kernel_rows.append(lax.optimization_barrier(jnp.sum(grad_wide * glu_ext[offset:offset + FRAMES].astype(jnp.float32), axis=0)))
    grad_kernel = jnp.stack(kernel_rows)
    grad_ext = jnp.pad(grad_conv_out, ((half_span, half_span), (0, 0)))
    grad_glu = jnp.zeros((FRAMES, D), jnp.float32)
    for offset in range(KW):
        begin = 2 * half_span - offset
        grad_glu = grad_glu + conv_kernel[offset] * grad_ext[begin:begin + FRAMES].astype(jnp.float32)
    grad_proj = jnp.concatenate([grad_glu * gate_sig, grad_glu * linear_half * gate_sig * (1.0 - gate_sig)], axis=1).astype(jnp.bfloat16)
    grad_normed = jnp.dot(grad_proj, proj_weight.T, preferred_element_type=jnp.float32)
    grad_hat = grad_normed * layer_gain
    grad_centre = inv_std * (grad_hat - lax.optimization_barrier(jnp.mean(grad_hat, axis=1, keepdims=True)) - normed * lax.optimization_barrier(jnp.mean(grad_hat * normed, axis=1, keepdims=True)))
    grad_stream = (grad_centre + grad_stream_in.astype(jnp.float32)).astype(jnp.bfloat16)
    query_grad, key_grad, value_grad = lax.map(stretch_backward, (stretched(query_in), stretched(key_in), stretched(value_in), attended, logsums, stretched(grad_stream)))
    return (query_grad.reshape(FRAMES, D), key_grad.reshape(FRAMES, D), value_grad.reshape(FRAMES, D), grad_stream, grad_kernel, grad_affine, moments)
```

```python
import math

import jax
import jax.numpy as jnp
from jax import lax
from jax.experimental import pallas as pl
from jax.experimental.pallas import tpu as pltpu
from jax.sharding import PartitionSpec as P

HEADS = 16
HD = 64
D = 1024
FR = 128
KW = 31
HALF = KW // 2
STRETCH = FR * HEADS
epsilon = 1e-05
LOG2E = math.log2(math.e)
SCALE = HD ** (-0.5)
BLOCK = 256
PART_ROWS = 24

f32 = jnp.float32
bf16 = jnp.bfloat16
NT = (((1,), (1,)), ((), ()))


def params(megabytes=48):
    return pltpu.CompilerParams(vmem_limit_bytes=megabytes * 1024 * 1024)


def dot(left, right):
    return jnp.dot(left, right, preferred_element_type=f32)


def dot_nt(left, right):
    return lax.dot_general(left, right, NT, preferred_element_type=f32)


def two_parts(value):
    high = value.astype(bf16)
    low = (value - high.astype(f32)).astype(bf16)
    return high, low


def three_parts(value):
    high = value.astype(bf16)
    rest = value - high.astype(f32)
    mid = rest.astype(bf16)
    low = (rest - mid.astype(f32)).astype(bf16)
    return high, mid, low


def pack_kernel(query_ref, key_ref, value_ref, out_ref):
    for item, ref in enumerate((query_ref, key_ref, value_ref)):
        for pair in range(HEADS // 2):
            turned = ref[:, 128 * pair : 128 * (pair + 1)].T
            out_ref[2 * pair, HD * item : HD * (item + 1), :] = turned[:HD]
            out_ref[2 * pair + 1, HD * item : HD * (item + 1), :] = turned[HD:]


def forward_kernel(qkv_ref, out_ref, log_ref, keys_ref, query_ref, value_ref, score_ref):
    for source in range(HEADS):
        span = slice(FR * source, FR * (source + 1))
        key_block = qkv_ref[source, HD : 2 * HD, :]
        keys_ref[span, :] = jnp.concatenate([key_block, key_block], axis=0).T
        high, low = two_parts(qkv_ref[source, 0:HD, :].astype(f32) * (SCALE * LOG2E))
        query_ref[0:HD, span] = high
        query_ref[HD : 2 * HD, span] = low
        value_ref[0:HD, span] = qkv_ref[source, 2 * HD : 3 * HD, :]
    extra = lax.broadcasted_iota(jnp.int32, (16, STRETCH), 0)
    value_ref[HD : HD + 16, :] = jnp.where(extra == 0, 1.0, 0.0).astype(bf16)
    chunks = STRETCH // BLOCK

    def scores(block, slot):
        queries = query_ref[:, pl.ds(pl.multiple_of(block * BLOCK, BLOCK), BLOCK)]
        peak = None
        for chunk in range(chunks):
            rows = slice(BLOCK * chunk, BLOCK * (chunk + 1))
            part = dot(keys_ref[rows, :], queries)
            score_ref[slot, rows, :] = part
            part = jnp.max(part.reshape(BLOCK // 8, 8, BLOCK), axis=0)
            peak = part if peak is None else jnp.maximum(peak, part)
        return jnp.max(peak, axis=0, keepdims=True)

    def step(block, peak):
        slot = lax.rem(block, 2)
        following = scores(jnp.minimum(block + 1, chunks - 1), 1 - slot)
        total = jnp.zeros((HD + 16, BLOCK), f32)
        for chunk in range(chunks):
            rows = slice(BLOCK * chunk, BLOCK * (chunk + 1))
            weights = jnp.exp2(score_ref[slot, rows, :] - peak).astype(bf16)
            total = total + dot(value_ref[:, rows], weights)
        norm = total[HD : HD + 1]
        attended = (total[:HD] / norm).astype(bf16)
        out_ref[2 * block] = attended[:, :FR]
        out_ref[2 * block + 1] = attended[:, FR:]
        log_ref[:, pl.ds(pl.multiple_of(block * BLOCK, BLOCK), BLOCK)] = peak + jnp.log2(norm)
        return following

    lax.fori_loop(0, chunks, step, scores(0, 0))


def project_kernel(
    att_ref, residual_ref, gain_ref, weight_ref, normed_ref, inv_ref, linear_ref, gate_ref, glu_ref, first_ref, last_ref
):
    for pair in range(HEADS // 2):
        cols = slice(128 * pair, 128 * (pair + 1))
        turned = att_ref[2 * pair : 2 * pair + 2].reshape(128, FR).T
        normed_ref[:, cols] = residual_ref[:, cols].astype(f32) + turned.astype(f32)
    stream = normed_ref[...]
    centred = stream - jnp.mean(stream, axis=1, keepdims=True)
    inv_std = lax.rsqrt(jnp.mean(centred * centred, axis=1, keepdims=True) + epsilon)
    normed = centred * inv_std
    normed_ref[...] = normed
    inv_ref[...] = jnp.broadcast_to(inv_std, (FR, 128))
    low = (normed * gain_ref[...]).astype(bf16)
    for part in range(8):
        cols = slice(128 * part, 128 * (part + 1))
        weights = jnp.concatenate(
            [weight_ref[:, part].reshape(D, 128), weight_ref[:, part + 8].reshape(D, 128)], axis=1
        )
        projected = dot(low, weights)
        linear = projected[:, :128]
        gate = jax.nn.sigmoid(projected[:, 128:])
        linear_ref[:, cols] = linear
        gate_ref[:, cols] = gate
        glu = (linear * gate).astype(bf16)
        glu_ref[:, cols] = glu
        first_ref[:, cols] = glu[:16]
        last_ref[:, cols] = glu[FR - 16 :]


def fill_extended(ext_ref, before_ref, own_ref, after_ref):
    for part in range(8):
        cols = slice(128 * part, 128 * (part + 1))
        ext_ref[part, 0:16, :] = before_ref[:, cols].astype(f32)
        ext_ref[part, 16 : 16 + FR, :] = own_ref[:, cols].astype(f32)
        ext_ref[part, 16 + FR : 32 + FR, :] = after_ref[:, cols].astype(f32)


def conv_kernel_body(
    glu_ref, before_ref, after_ref, taps_ref, vec_ref, grad_ref, out_ref, first_ref, last_ref, sums_ref, ext_ref
):
    fill_extended(ext_ref, before_ref, glu_ref, after_ref)
    for part in range(8):
        cols = slice(128 * part, 128 * (part + 1))
        conv = jnp.zeros((FR, 128), f32)
        for tap in range(KW):
            conv = conv + taps_ref[tap : tap + 1, cols] * ext_ref[part, tap + 1 : tap + 1 + FR, :]
        gamma = vec_ref[0:1, cols]
        inv_scale = lax.rsqrt(vec_ref[3:4, cols] + epsilon)
        zhat = (conv - vec_ref[2:3, cols]) * inv_scale
        shifted = gamma * zhat + vec_ref[1:2, cols]
        sig = jax.nn.sigmoid(shifted)
        grad_shift = grad_ref[:, cols].astype(f32) * sig * (1.0 + shifted * (1.0 - sig))
        grad_out = (grad_shift * (gamma * inv_scale)).astype(bf16)
        out_ref[:, cols] = grad_out
        first_ref[:, cols] = grad_out[:16]
        last_ref[:, cols] = grad_out[FR - 16 :]
        sums_ref[0:1, cols] = jnp.sum(grad_shift * zhat, axis=0, keepdims=True)
        sums_ref[1:2, cols] = jnp.sum(grad_shift, axis=0, keepdims=True)
        sums_ref[2:3, cols] = jnp.sum(conv, axis=0, keepdims=True)
        sums_ref[3:4, cols] = jnp.sum(conv * conv, axis=0, keepdims=True)


def taps_kernel(glu_ref, before_ref, after_ref, grad_ref, sums_ref, part_ref, ext_ref):
    fill_extended(ext_ref, before_ref, glu_ref, after_ref)
    part_ref[...] = jnp.zeros_like(part_ref)
    for part in range(8):
        cols = slice(128 * part, 128 * (part + 1))
        grad = grad_ref[:, cols].astype(f32)
        for tap in range(KW):
            total = jnp.sum(grad * ext_ref[part, tap + 1 : tap + 1 + FR, :], axis=0, keepdims=True)
            place = (tap % 3) * 8 + part
            part_ref[tap // 3, place : place + 1, :] = total
        for row in range(4):
            tap = KW + row
            place = (tap % 3) * 8 + part
            part_ref[tap // 3, place : place + 1, :] = sums_ref[row : row + 1, cols]


def back_kernel(
    grad_ref,
    before_ref,
    after_ref,
    taps_ref,
    linear_ref,
    gate_ref,
    normed_ref,
    inv_ref,
    gain_ref,
    weight_ref,
    skip_ref,
    part_ref,
    stream_ref,
    payload_ref,
    ext_ref,
    proj_ref,
    hat_ref,
):
    fill_extended(ext_ref, before_ref, grad_ref, after_ref)
    high, low = two_parts(part_ref[...])
    payload_ref[:, 0:PART_ROWS, :] = high
    payload_ref[:, PART_ROWS : 2 * PART_ROWS, :] = low
    for part in range(8):
        cols = slice(128 * part, 128 * (part + 1))
        grad_glu = jnp.zeros((FR, 128), f32)
        for tap in range(KW):
            begin = 2 * HALF - tap + 1
            grad_glu = grad_glu + taps_ref[tap : tap + 1, cols] * ext_ref[part, begin : begin + FR, :]
        gate = gate_ref[:, cols]
        half = grad_glu * gate
        proj_ref[:, cols] = half.astype(bf16)
        proj_ref[:, 1024 + 128 * part : 1024 + 128 * (part + 1)] = (
            half * linear_ref[:, cols] * (1.0 - gate)
        ).astype(bf16)
    proj = proj_ref[...]
    for part in range(4):
        cols = slice(256 * part, 256 * (part + 1))
        rows = [
            jnp.concatenate([weight_ref[2 * part + half, s] for s in range(16)], axis=1) for half in range(2)
        ]
        hat_ref[:, cols] = dot_nt(proj, jnp.concatenate(rows, axis=0)) * gain_ref[:, cols]
    hat = hat_ref[...]
    normed = normed_ref[...]
    mean = jnp.mean(hat, axis=1, keepdims=True)
    mean_normed = jnp.mean(hat * normed, axis=1, keepdims=True)
    centre = inv_ref[:, 0:1] * (hat - mean - normed * mean_normed)
    stream = (centre + skip_ref[...].astype(f32)).astype(bf16)
    stream_ref[...] = stream
    for pair in range(HEADS // 2):
        turned = stream[:, 128 * pair : 128 * (pair + 1)].T
        payload_ref[2 * pair, 2 * PART_ROWS :, :] = turned[:HD]
        payload_ref[2 * pair + 1, 2 * PART_ROWS :, :] = turned[HD:]


def spread_kernel(payload_ref, out_ref):
    both = payload_ref[...].astype(f32)
    total = jnp.sum(both[:, :PART_ROWS] + both[:, PART_ROWS:], axis=0)
    out_ref[...] = jnp.broadcast_to(total[None], out_ref.shape)


def backward_kernel(
    qkv_ref,
    att_ref,
    log_ref,
    payload_ref,
    out_ref,
    keys_ref,
    values_ref,
    query_ref,
    grad_ref,
    turned_ref,
    key_total_ref,
    value_total_ref,
):
    pad_rows = lax.broadcasted_iota(jnp.int32, (HD, FR), 0)
    ones = jnp.where(pad_rows < 3, 1.0, 0.0).astype(bf16)
    for source in range(HEADS):
        span = slice(FR * source, FR * (source + 1))
        key_block = qkv_ref[source, HD : 2 * HD, :]
        turned_ref[:, span] = key_block
        keys_ref[span, :] = jnp.concatenate([key_block, ones], axis=0).T
        values_ref[span, :] = jnp.concatenate([qkv_ref[source, 2 * HD :, :], ones], axis=0).T
        query_ref[0:HD, span] = qkv_ref[source, 0:HD, :]
        grads = payload_ref[source, 2 * PART_ROWS :, :]
        grad_ref[0:HD, span] = grads
        delta = jnp.sum(grads.astype(f32) * att_ref[source].astype(f32), axis=0, keepdims=True)
        logs = log_ref[:, span] * (1.0 / (SCALE * LOG2E))
        for ref, row in ((query_ref, logs), (grad_ref, delta)):
            parts = three_parts(jnp.broadcast_to(-row, (HD, FR)))
            tail = jnp.where(
                pad_rows == 0,
                parts[0].astype(f32),
                jnp.where(
                    pad_rows == 1, parts[1].astype(f32), jnp.where(pad_rows == 2, parts[2].astype(f32), 0.0)
                ),
            )
            ref[HD : 2 * HD, span] = tail.astype(bf16)
    key_total_ref[...] = jnp.zeros_like(key_total_ref)
    value_total_ref[...] = jnp.zeros_like(value_total_ref)
    chunks = STRETCH // BLOCK

    def step(block, carry):
        cols = pl.ds(pl.multiple_of(block * BLOCK, BLOCK), BLOCK)
        queries = query_ref[:, cols]
        grads = grad_ref[:, cols]
        query_total = jnp.zeros((HD, BLOCK), f32)
        for chunk in range(chunks):
            rows = slice(BLOCK * chunk, BLOCK * (chunk + 1))
            probs = jnp.exp2(dot(keys_ref[rows, :], queries) * (SCALE * LOG2E))
            grad_scores = (probs * dot(values_ref[rows, :], grads)).astype(bf16)
            query_total = query_total + dot(turned_ref[:, rows], grad_scores)
            value_total_ref[:, rows] += dot_nt(grads[:HD], probs.astype(bf16))
            key_total_ref[:, rows] += dot_nt(queries[:HD], grad_scores)
        query_grad = (query_total * SCALE).astype(bf16)
        out_ref[2 * block, 0:HD, :] = query_grad[:, :FR]
        out_ref[2 * block + 1, 0:HD, :] = query_grad[:, FR:]
        return carry

    lax.fori_loop(0, chunks, step, 0)
    for source in range(HEADS):
        span = slice(FR * source, FR * (source + 1))
        out_ref[source, HD : 2 * HD, :] = (key_total_ref[:, span] * SCALE).astype(bf16)
        out_ref[source, 2 * HD : 3 * HD, :] = value_total_ref[:, span].astype(bf16)


def finish_kernel(parts_ref, payload_ref, out_ref):
    total = jnp.sum(parts_ref[...], axis=0)
    high, low = two_parts(total)
    both = jnp.concatenate([high.astype(f32), low.astype(f32)], axis=0).astype(bf16)
    out_ref[...] = jnp.broadcast_to(both[None], out_ref.shape)


def unpack_kernel(frame_total, back_ref, query_ref, key_ref, value_ref, taps_ref, affine_ref, moments_ref):
    for item, ref in enumerate((query_ref, key_ref, value_ref)):
        for pair in range(HEADS // 2):
            turned = back_ref[2 * pair : 2 * pair + 2, HD * item : HD * (item + 1), :].reshape(128, FR)
            ref[:, 128 * pair : 128 * (pair + 1)] = turned.T
    for source in range(12):
        both = back_ref[source, 3 * HD :, :].astype(f32)
        total = both[:PART_ROWS] + both[PART_ROWS:]
        for local_row in range(3):
            row = 3 * source + local_row
            if row >= KW + 4:
                continue
            if row < KW:
                ref, place, factor = taps_ref, row, 1.0
            elif row < KW + 2:
                ref, place, factor = affine_ref, row - KW, 1.0
            else:
                ref, place, factor = moments_ref, row - KW - 2, 1.0 / frame_total
            for part in range(8):
                position = 8 * local_row + part
                ref[place : place + 1, 128 * part : 128 * (part + 1)] = total[position : position + 1] * factor


def call(kernel, out_shape, *args, scratch=(), **extra):
    return pl.pallas_call(
        kernel, out_shape=out_shape, scratch_shapes=list(scratch), compiler_params=params(), **extra
    )(*args)


def shape(dims, dtype):
    return jax.ShapeDtypeStruct(dims, dtype)


def gather_weights(proj_weight):
    place = lax.axis_index("tm")
    chunk = lax.rem(place, 2) * 4 + place // 8
    own = lax.dynamic_slice_in_dim(proj_weight, chunk * 128, 128, axis=0)
    rows = lax.all_gather(own, "seq", axis=0)
    along_x = [[x * 8 + low for x in range(4)] for low in range(8)]
    rows = lax.all_gather(rows, "tm", axis=0, axis_index_groups=along_x)
    cores = [[2 * chip, 2 * chip + 1] for chip in range(16)]
    rows = lax.all_gather(rows, "tm", axis=0, axis_index_groups=cores)
    return rows.reshape(8, 16, 128, 128)


def halo(first, last):
    size = lax.axis_size("tm") * lax.axis_size("seq")
    up = [(i, i + 1) for i in range(size - 1)]
    down = [(i + 1, i) for i in range(size - 1)]
    axes = ("tm", "seq")
    return lax.ppermute(last, axes, up), lax.ppermute(first, axes, down)


def local(
    query_in,
    key_in,
    value_in,
    residual,
    layer_gain,
    proj_weight,
    conv_kernel,
    batch_gamma,
    batch_beta,
    stale_mean,
    stale_variance,
    grad_conv,
    grad_stream_in,
):
    frame_total = FR * lax.axis_size("tm") * lax.axis_size("seq")
    weights = gather_weights(proj_weight)
    gain = layer_gain.reshape(1, D)
    vectors = jnp.stack([batch_gamma, batch_beta, stale_mean, stale_variance])

    packed = call(pack_kernel, shape((HEADS, 3 * HD, FR), bf16), query_in, key_in, value_in)
    qkv = lax.all_to_all(packed, "seq", 0, 0, tiled=True)
    attended, logs = call(
        forward_kernel,
        (shape((HEADS, HD, FR), bf16), shape((1, STRETCH), f32)),
        qkv,
        scratch=(
            pltpu.VMEM((STRETCH, 2 * HD), bf16),
            pltpu.VMEM((2 * HD, STRETCH), bf16),
            pltpu.VMEM((HD + 16, STRETCH), bf16),
            pltpu.VMEM((2, STRETCH, BLOCK), f32),
        ),
    )
    att_rows = lax.all_to_all(attended, "seq", 0, 0, tiled=True)
    wide = shape((FR, D), f32)
    narrow = shape((FR, D), bf16)
    edge = shape((16, D), bf16)
    ext = pltpu.VMEM((8, 32 + FR, 128), f32)
    normed, inv_std, linear, gate, glu, first, last = call(
        project_kernel,
        (wide, shape((FR, 128), f32), wide, wide, narrow, edge, edge),
        att_rows,
        residual,
        gain,
        weights,
    )
    before, after = halo(first, last)
    grad_out, first, last, sums = call(
        conv_kernel_body,
        (narrow, edge, edge, shape((4, D), f32)),
        glu,
        before,
        after,
        conv_kernel,
        vectors,
        grad_conv,
        scratch=(ext,),
    )
    grad_before, grad_after = halo(first, last)
    parts = call(
        taps_kernel,
        shape((HEADS, PART_ROWS, 128), f32),
        glu,
        before,
        after,
        grad_out,
        sums,
        scratch=(ext,),
    )
    grad_stream, payload = call(
        back_kernel,
        (narrow, shape((HEADS, 2 * PART_ROWS + HD, FR), bf16)),
        grad_out,
        grad_before,
        grad_after,
        conv_kernel,
        linear,
        gate,
        normed,
        inv_std,
        gain,
        weights,
        grad_stream_in,
        parts,
        scratch=(ext, pltpu.VMEM((FR, 2 * D), bf16), pltpu.VMEM((FR, D), f32)),
    )
    payload = lax.all_to_all(payload, "seq", 0, 0, tiled=True)
    groups = lax.axis_size("tm")
    spread = call(
        spread_kernel,
        shape((groups, PART_ROWS, 128), f32),
        payload,
        grid=(1,),
        in_specs=[pl.BlockSpec((HEADS, 2 * PART_ROWS, 128), lambda i: (0, 0, 0))],
        out_specs=pl.BlockSpec((groups, PART_ROWS, 128), lambda i: (0, 0, 0)),
    )
    totals = lax.all_to_all(spread, "tm", 0, 0, tiled=True)
    back = call(
        backward_kernel,
        shape((HEADS, 3 * HD + 2 * PART_ROWS, FR), bf16),
        qkv,
        attended,
        logs,
        payload,
        scratch=(
            pltpu.VMEM((STRETCH, 2 * HD), bf16),
            pltpu.VMEM((STRETCH, 2 * HD), bf16),
            pltpu.VMEM((2 * HD, STRETCH), bf16),
            pltpu.VMEM((2 * HD, STRETCH), bf16),
            pltpu.VMEM((HD, STRETCH), bf16),
            pltpu.VMEM((HD, STRETCH), f32),
            pltpu.VMEM((HD, STRETCH), f32),
        ),
    )
    back = call(
        finish_kernel,
        shape(back.shape, bf16),
        totals,
        back,
        grid=(1,),
        in_specs=[
            pl.BlockSpec((groups, PART_ROWS, 128), lambda i: (0, 0, 0)),
            pl.BlockSpec(memory_space=pl.ANY),
        ],
        out_specs=pl.BlockSpec((HEADS, 2 * PART_ROWS, 128), lambda i: (0, 4, 0)),
        input_output_aliases={1: 0},
    )
    back = lax.all_to_all(back, "seq", 0, 0, tiled=True)
    query_grad, key_grad, value_grad, kernel_sum, affine_sum, moments = call(
        lambda *refs: unpack_kernel(frame_total, *refs),
        (narrow, narrow, narrow, shape((KW, D), f32), shape((2, D), f32), shape((2, D), f32)),
        back,
    )
    return (query_grad, key_grad, value_grad, grad_stream, kernel_sum, affine_sum, moments)


def solution(mesh):
    rows = P(("tm", "seq"), None)
    in_specs = (rows, rows, rows, rows, P(), P(None, "seq"), P(), P(), P(), P(), P(), rows, rows)
    out_specs = (rows, rows, rows, rows, P(), P(), P())
    return jax.shard_map(local, mesh=mesh, in_specs=in_specs, out_specs=out_specs, check_vma=False)
```

```python
import math

import jax
import jax.numpy as jnp
from jax import lax
from jax.experimental import pallas as pl
from jax.experimental.pallas import tpu as pltpu
from jax.sharding import PartitionSpec as P

HEADS = 16
HD = 64
D = 1024
FR = 128
KW = 31
HALF = KW // 2
STRETCH = FR * HEADS
epsilon = 1e-05
LOG2E = math.log2(math.e)
SCALE = HD ** (-0.5)
BLOCK = 256
PART_ROWS = 32
EDGE = 32
ROWS = FR + 2 * EDGE
WIDE = FR + EDGE

f32 = jnp.float32
bf16 = jnp.bfloat16
NT = (((1,), (1,)), ((), ()))


def params(megabytes=48):
    return pltpu.CompilerParams(vmem_limit_bytes=megabytes * 1024 * 1024)


def dot(left, right):
    return jnp.dot(left, right, preferred_element_type=f32)


def dot_nt(left, right):
    return lax.dot_general(left, right, NT, preferred_element_type=f32)


def two_parts(value):
    high = value.astype(bf16)
    low = (value - high.astype(f32)).astype(bf16)
    return high, low


def three_parts(value):
    high = value.astype(bf16)
    rest = value - high.astype(f32)
    mid = rest.astype(bf16)
    low = (rest - mid.astype(f32)).astype(bf16)
    return high, mid, low


def pack_kernel(
    query_ref,
    key_ref,
    value_ref,
    res_first_ref,
    res_last_ref,
    grad_first_ref,
    grad_last_ref,
    out_ref,
    first_ref,
    last_ref,
):
    for item, ref in enumerate((query_ref, key_ref, value_ref)):
        for pair in range(HEADS // 2):
            turned = ref[:, 128 * pair : 128 * (pair + 1)].T
            out_ref[2 * pair, HD * item : HD * (item + 1), :] = turned[:HD]
            out_ref[2 * pair + 1, HD * item : HD * (item + 1), :] = turned[HD:]
    first_ref[:EDGE] = res_first_ref[...]
    first_ref[EDGE:] = grad_first_ref[...]
    last_ref[:EDGE] = res_last_ref[...]
    last_ref[EDGE:] = grad_last_ref[...]


CHUNKS = STRETCH // BLOCK


def block_rows(block):
    if isinstance(block, int):
        return slice(block * BLOCK, (block + 1) * BLOCK)
    return pl.ds(pl.multiple_of(block * BLOCK, BLOCK), BLOCK)


def low_lanes(rows):
    return lax.broadcasted_iota(jnp.int32, (rows, 128), 1) < HD


def soft_stage(keys_ref, query_ref, value_ref, following, current):
    queries = peak = total = None
    if following is not None:
        block, next_ref = following
        queries = query_ref[block_rows(block), :]
    for chunk in range(CHUNKS):
        rows = slice(BLOCK * chunk, BLOCK * (chunk + 1))
        if following is not None:
            part = dot(queries, keys_ref[:, rows])
            next_ref[:, rows] = part
            part = jnp.maximum(part[:, :128], part[:, 128:])
            peak = part if peak is None else jnp.maximum(peak, part)
        if current is not None:
            score_ref, top = current
            weights = jnp.exp2(score_ref[:, rows] - jnp.concatenate([top, top], axis=1)).astype(bf16)
            part = dot(weights, value_ref[rows, :])
            total = part if total is None else total + part
    if peak is not None:
        peak = jnp.broadcast_to(jnp.max(peak, axis=1, keepdims=True), (BLOCK, 128))
    return peak, total


def store_attended(total, peak, nat_ref, rows, turned_ref, log_ref, place):
    norm = jnp.broadcast_to(total[:, HD : HD + 1], (BLOCK, 128))
    attended = (total / norm).astype(bf16).astype(f32)
    low = low_lanes(BLOCK)
    nat_ref[rows, :] = jnp.where(low, attended, pltpu.roll(attended, HD, 1)).astype(bf16)
    turned = jnp.where(low, attended, peak + jnp.log2(norm)).T
    turned_ref[place] = turned[:HD].astype(bf16)
    log_ref[place] = turned[HD : HD + 8]


def edge_forward_kernel(
    qkv_ref,
    keys_ref,
    query_ref,
    value_ref,
    nat_ref,
    turned_ref,
    log_ref,
    first_ref,
    last_ref,
    score_ref,
    other_ref,
):
    pad_rows = lax.broadcasted_iota(jnp.int32, (HD, FR), 0)
    ones = jnp.where(pad_rows == 0, 1.0, 0.0).astype(bf16)
    for source in range(HEADS):
        span = slice(FR * source, FR * (source + 1))
        key_block = qkv_ref[source, HD : 2 * HD, :]
        keys_ref[0:HD, span] = key_block
        keys_ref[HD : 2 * HD, span] = key_block
        high, low = two_parts(qkv_ref[source, 0:HD, :].astype(f32) * (SCALE * LOG2E))
        query_ref[span, :] = jnp.concatenate([high, low], axis=0).T
        value_ref[span, :] = jnp.concatenate([qkv_ref[source, 2 * HD : 3 * HD, :], ones], axis=0).T
    stage = lambda *pair: soft_stage(keys_ref, query_ref, value_ref, *pair)
    top, _ = stage((0, score_ref), None)
    final_top, total = stage((CHUNKS - 1, other_ref), (score_ref, top))
    store_attended(total, top, nat_ref, slice(0, BLOCK), turned_ref, log_ref, 0)
    _, total = stage(None, (other_ref, final_top))
    store_attended(total, final_top, nat_ref, slice(BLOCK, 2 * BLOCK), turned_ref, log_ref, 1)
    first_ref[...] = nat_ref[0:EDGE, :]
    last_ref[...] = nat_ref[2 * BLOCK - EDGE : 2 * BLOCK, :]


def middle_forward_kernel(
    keys_ref, query_ref, value_ref, nat_ref, turned_ref, log_ref, score_ref, other_ref
):
    stage = lambda *pair: soft_stage(keys_ref, query_ref, value_ref, *pair)

    def store(total, top, place):
        store_attended(total, top, nat_ref, block_rows(place), turned_ref, log_ref, place)

    def two(index, top):
        place = 2 * index
        next_top, total = stage((place + 2, other_ref), (score_ref, top))
        store(total, top, place)
        last_top, total = stage((place + 3, score_ref), (other_ref, next_top))
        store(total, next_top, place + 1)
        return last_top

    top, _ = stage((1, score_ref), None)
    top = lax.fori_loop(0, 2, two, top)
    next_top, total = stage((6, other_ref), (score_ref, top))
    store(total, top, 4)
    _, total = stage(None, (other_ref, next_top))
    store(total, next_top, 5)


def assemble_kernel(edge_ref, middle_ref, before_ref, after_ref, out_ref):
    def frames(begin, count):
        if begin < 0:
            return before_ref[...]
        if begin >= STRETCH:
            return after_ref[...]
        if begin < BLOCK:
            return edge_ref[begin : begin + count, :]
        if begin < STRETCH - BLOCK:
            return middle_ref[begin - BLOCK : begin - BLOCK + count, :]
        begin -= STRETCH - 2 * BLOCK
        return edge_ref[begin : begin + count, :]

    for dest in range(HEADS):
        begin = FR * dest
        low = low_lanes(64)
        out_ref[dest, 0:64, :] = jnp.where(
            low, frames(begin, 64).astype(f32), frames(begin + 64, 64).astype(f32)
        ).astype(bf16)
        low = low_lanes(EDGE)
        out_ref[dest, 64 : 64 + EDGE, :] = jnp.where(
            low, frames(begin - EDGE, EDGE).astype(f32), frames(begin + FR, EDGE).astype(f32)
        ).astype(bf16)


def middle_kernel(
    core_ref,
    att_ref,
    residual_ref,
    before_ref,
    after_ref,
    gain_ref,
    own_ref,
    swapped_ref,
    taps_ref,
    vec_ref,
    grad_ref,
    skip_ref,
    stream_ref,
    payload_ref,
    weight_ref,
    normed_ref,
    low_ref,
    linear_ref,
    gate_ref,
    glu_ref,
    grad_ext_ref,
    sums_ref,
    proj_ref,
    hat_ref,
    copy_sem,
):
    core = core_ref[0]

    def copies(column):
        out = []
        for index, (ref, side) in enumerate(((own_ref, core), (swapped_ref, 1 - core))):
            out.append(
                pltpu.make_async_copy(
                    ref.at[:, column],
                    weight_ref.at[pl.ds(side * 16, 16), column],
                    copy_sem.at[2 * column + index],
                )
            )
        return out

    order = [column for part in range(8) for column in (part, part + 8)]
    for column in order:
        for copy in copies(column):
            copy.start()
    lanes = low_lanes(64 + EDGE)
    for pair in range(HEADS // 2):
        cols = slice(128 * pair, 128 * (pair + 1))
        even = att_ref[2 * pair].astype(f32)
        odd = att_ref[2 * pair + 1].astype(f32)
        low = jnp.where(lanes, even, pltpu.roll(odd, HD, 1))
        high = jnp.where(lanes, pltpu.roll(even, HD, 1), odd)
        normed_ref[0:EDGE, cols] = low[64:] + before_ref[0:EDGE, cols].astype(f32)
        normed_ref[EDGE : EDGE + 64, cols] = low[:64] + residual_ref[0:64, cols].astype(f32)
        normed_ref[EDGE + 64 : EDGE + FR, cols] = high[:64] + residual_ref[64:FR, cols].astype(f32)
        normed_ref[EDGE + FR :, cols] = high[64:] + after_ref[0:EDGE, cols].astype(f32)
    stream = normed_ref[...]
    centred = stream - jnp.mean(stream, axis=1, keepdims=True)
    inv_std = lax.rsqrt(jnp.mean(centred * centred, axis=1, keepdims=True) + epsilon)
    normed = centred * inv_std
    normed_ref[...] = normed
    inv_own = inv_std[EDGE : EDGE + FR]
    low_ref[...] = (normed * gain_ref[...]).astype(bf16)
    sums_ref[...] = jnp.zeros_like(sums_ref)
    for part in range(8):
        for column in (part, part + 8):
            for copy in copies(column):
                copy.wait()
        weights = jnp.concatenate(
            [weight_ref[:, part].reshape(D, 128), weight_ref[:, part + 8].reshape(D, 128)], axis=1
        )
        projected = dot(low_ref[...], weights)
        linear = projected[:, :128]
        gate = jax.nn.sigmoid(projected[:, 128:])
        linear_ref[part] = linear[EDGE : EDGE + FR]
        gate_ref[part] = gate[EDGE : EDGE + FR]
        glu_ref[part] = (linear * gate).astype(bf16).astype(f32)
    for part in range(8):
        cols = slice(128 * part, 128 * (part + 1))

        def put(row, total):
            place = (row % 4) * 8 + part
            sums_ref[row // 4, place : place + 1, :] = total

        conv = jnp.zeros((WIDE, 128), f32)
        for tap in range(KW):
            conv = conv + taps_ref[tap : tap + 1, cols] * glu_ref[part, tap + 1 : tap + 1 + WIDE, :]
        gamma = vec_ref[0:1, cols]
        inv_scale = lax.rsqrt(vec_ref[3:4, cols] + epsilon)
        zhat = (conv - vec_ref[2:3, cols]) * inv_scale
        shifted = gamma * zhat + vec_ref[1:2, cols]
        sig = jax.nn.sigmoid(shifted)
        grads = jnp.concatenate(
            [before_ref[EDGE:, cols], grad_ref[:, cols], after_ref[EDGE:, cols]], axis=0
        ).astype(f32)
        grad_shift = grads * sig * (1.0 + shifted * (1.0 - sig))
        grad_ext_ref[...] = (grad_shift * (gamma * inv_scale)).astype(bf16).astype(f32)
        own = slice(EDGE // 2, EDGE // 2 + FR)
        conv, zhat, grad_shift = conv[own], zhat[own], grad_shift[own]
        for row, value in enumerate((grad_shift * zhat, grad_shift, conv, conv * conv)):
            total = jnp.sum(value, axis=0, keepdims=True)
            put(KW + row, total)
            put(KW + 4 + row, total - total.astype(bf16).astype(f32))
        grad_own = grad_ext_ref[own, :]
        for tap in range(KW):
            begin = EDGE + tap - HALF
            put(tap, jnp.sum(grad_own * glu_ref[part, begin : begin + FR, :], axis=0, keepdims=True))
        grad_glu = jnp.zeros((FR, 128), f32)
        for tap in range(KW):
            begin = EDGE // 2 + HALF - tap
            grad_glu = grad_glu + taps_ref[tap : tap + 1, cols] * grad_ext_ref[begin : begin + FR, :]
        gate = gate_ref[part]
        half = grad_glu * gate
        proj_ref[:, cols] = half.astype(bf16)
        proj_ref[:, D + 128 * part : D + 128 * (part + 1)] = (half * linear_ref[part] * (1.0 - gate)).astype(bf16)
    payload_ref[:, 0:PART_ROWS, :] = sums_ref[...].astype(bf16)
    proj = proj_ref[...]
    for part in range(4):
        cols = slice(256 * part, 256 * (part + 1))
        columns = [weight_ref[8 * part : 8 * (part + 1), s].reshape(256, 128) for s in range(16)]
        hat_ref[:, cols] = dot_nt(proj, jnp.concatenate(columns, axis=1)) * gain_ref[:, cols]
    hat = hat_ref[...]
    normed = normed_ref[EDGE : EDGE + FR, :]
    mean = jnp.mean(hat, axis=1, keepdims=True)
    mean_normed = jnp.mean(hat * normed, axis=1, keepdims=True)
    centre = inv_own * (hat - mean - normed * mean_normed)
    stream = (centre + skip_ref[...].astype(f32)).astype(bf16)
    stream_ref[...] = stream
    for pair in range(HEADS // 2):
        turned = stream[:, 128 * pair : 128 * (pair + 1)].T
        payload_ref[2 * pair, PART_ROWS:, :] = turned[:HD]
        payload_ref[2 * pair + 1, PART_ROWS:, :] = turned[HD:]


def spread_kernel(payload_ref, out_ref):
    total = jnp.sum(payload_ref[...].astype(f32), axis=0)
    out_ref[...] = jnp.broadcast_to(total[None], out_ref.shape)


def backward_kernel(
    qkv_ref,
    edge_att_ref,
    mid_att_ref,
    edge_log_ref,
    mid_log_ref,
    payload_ref,
    out_ref,
    keys_ref,
    values_ref,
    query_ref,
    grad_ref,
    query_rows_ref,
    grad_rows_ref,
    turned_ref,
    total_ref,
):
    pad_rows = lax.broadcasted_iota(jnp.int32, (HD, FR), 0)
    ones = jnp.where(pad_rows < 3, 1.0, 0.0).astype(bf16)
    for source in range(HEADS):
        span = slice(FR * source, FR * (source + 1))
        key_block = qkv_ref[source, HD : 2 * HD, :]
        turned_ref[:, span] = key_block
        keys_ref[span, :] = jnp.concatenate([key_block, ones], axis=0).T
        values_ref[span, :] = jnp.concatenate([qkv_ref[source, 2 * HD :, :], ones], axis=0).T
        grads = payload_ref[source, PART_ROWS:, :]
        block, side = divmod(source, 2)
        if 0 < block < CHUNKS - 1:
            att, log, block = mid_att_ref, mid_log_ref, block - 1
        else:
            att, log, block = edge_att_ref, edge_log_ref, min(block, 1)
        lanes = slice(FR * side, FR * (side + 1))
        delta = jnp.sum(grads.astype(f32) * att[block, :, lanes].astype(f32), axis=0, keepdims=True)
        logs = log[block, 0:1, lanes] * (1.0 / (SCALE * LOG2E))
        for ref, rows_ref, body, row in (
            (query_ref, query_rows_ref, qkv_ref[source, 0:HD, :], logs),
            (grad_ref, grad_rows_ref, grads, delta),
        ):
            parts = three_parts(jnp.broadcast_to(-row, (HD, FR)))
            tail = jnp.zeros((HD, FR), f32)
            for place in range(3):
                tail = jnp.where(pad_rows == place, parts[place].astype(f32), tail)
            both = jnp.concatenate([body, tail.astype(bf16)], axis=0)
            ref[:, span] = both
            rows_ref[span, :] = both.T
    total_ref[...] = jnp.zeros_like(total_ref)

    def step(block, carry):
        rows = block_rows(block)
        keys, values, turned = keys_ref[rows, :], values_ref[rows, :], turned_ref[:, rows]

        def products(chunk):
            cols = block_rows(chunk)
            return dot(keys, query_ref[:, cols]), dot(values, grad_ref[:, cols])

        key_total = jnp.zeros((BLOCK, 128), f32)
        value_total = jnp.zeros((BLOCK, 128), f32)
        ready = products(0)
        for chunk in range(CHUNKS):
            cols = block_rows(chunk)
            scores, grad_probs = ready
            if chunk + 1 < CHUNKS:
                ready = products(chunk + 1)
            probs = jnp.exp2(scores * (SCALE * LOG2E))
            grad_scores = (probs * grad_probs).astype(bf16)
            value_total = value_total + dot(probs.astype(bf16), grad_rows_ref[cols, :])
            key_total = key_total + dot(grad_scores, query_rows_ref[cols, :])
            total_ref[:, cols] += dot(turned, grad_scores)
        for place, total in ((1, key_total * SCALE), (2, value_total)):
            turned_total = total.T[:HD].astype(bf16)
            out_ref[2 * block, HD * place : HD * (place + 1), :] = turned_total[:, :FR]
            out_ref[2 * block + 1, HD * place : HD * (place + 1), :] = turned_total[:, FR:]
        return carry

    lax.fori_loop(0, CHUNKS, step, 0)
    for source in range(HEADS):
        span = slice(FR * source, FR * (source + 1))
        out_ref[source, 0:HD, :] = (total_ref[:, span] * SCALE).astype(bf16)


def finish_kernel(parts_ref, payload_ref, out_ref):
    total = jnp.sum(parts_ref[...], axis=0).astype(bf16)
    out_ref[...] = jnp.broadcast_to(total[None], out_ref.shape)


def unpack_kernel(frame_total, back_ref, query_ref, key_ref, value_ref, taps_ref, affine_ref, moments_ref):
    for item, ref in enumerate((query_ref, key_ref, value_ref)):
        for pair in range(HEADS // 2):
            turned = back_ref[2 * pair : 2 * pair + 2, HD * item : HD * (item + 1), :].reshape(128, FR)
            ref[:, 128 * pair : 128 * (pair + 1)] = turned.T
    totals = [back_ref[source, 3 * HD :, :].astype(f32) for source in range(10)]

    def fetch(row, part):
        place = (row % 4) * 8 + part
        return totals[row // 4][place : place + 1]

    for part in range(8):
        cols = slice(128 * part, 128 * (part + 1))
        for row in range(KW):
            taps_ref[row : row + 1, cols] = fetch(row, part)
        for row in range(4):
            ref, factor = (affine_ref, 1.0) if row < 2 else (moments_ref, 1.0 / frame_total)
            total = fetch(KW + row, part) + fetch(KW + 4 + row, part)
            ref[row % 2 : row % 2 + 1, cols] = total * factor


def call(kernel, out_shape, *args, scratch=(), gflops=0, **extra):
    if gflops:
        extra["cost_estimate"] = pl.CostEstimate(
            flops=gflops * 10**9, bytes_accessed=4 * 2**20, transcendentals=STRETCH * STRETCH
        )
    return pl.pallas_call(
        kernel, out_shape=out_shape, scratch_shapes=list(scratch), compiler_params=params(), **extra
    )(*args)


def shape(dims, dtype):
    return jax.ShapeDtypeStruct(dims, dtype)


def whole(*dims):
    return pl.BlockSpec(dims, lambda i: (0,) * len(dims))


def rows_at(count, index):
    return pl.BlockSpec((count, D), lambda i: (index, 0))


def gather_half(proj_weight):
    place = lax.axis_index("tm")
    chunk = lax.rem(place, 2) * 16 + place // 2
    own = lax.dynamic_slice_in_dim(proj_weight, chunk * 32, 32, axis=0)
    own = jnp.broadcast_to(own[None], (HEADS, 32, 128))
    rows = lax.all_to_all(own, "seq", 0, 0, tiled=True)
    chips = [[2 * chip + core for chip in range(16)] for core in range(2)]
    return lax.all_gather(rows, "tm", axis=0, axis_index_groups=chips)


def swap_half(half):
    pairs = [(place, place ^ 1) for place in range(lax.axis_size("tm"))]
    return lax.ppermute(half, "tm", pairs)


def neighbours(axes, first, last):
    size = lax.axis_size(axes)
    up = [(i, i + 1) for i in range(size - 1)]
    down = [(i + 1, i) for i in range(size - 1)]
    return lax.ppermute(last, axes, up), lax.ppermute(first, axes, down)


def local(
    query_in,
    key_in,
    value_in,
    residual,
    layer_gain,
    proj_weight,
    conv_kernel,
    batch_gamma,
    batch_beta,
    stale_mean,
    stale_variance,
    grad_conv,
    grad_stream_in,
):
    groups = lax.axis_size("tm")
    frame_total = FR * groups * lax.axis_size("seq")
    half = gather_half(proj_weight)
    gain = layer_gain.reshape(1, D)
    vectors = jnp.stack([batch_gamma, batch_beta, stale_mean, stale_variance])
    core = lax.rem(lax.axis_index("tm"), 2).reshape(1)

    edge_rows = EDGE + EDGE // 2
    packed, first, last = call(
        pack_kernel,
        (shape((HEADS, 3 * HD, FR), bf16), shape((edge_rows, D), bf16), shape((edge_rows, D), bf16)),
        query_in,
        key_in,
        value_in,
        residual,
        residual,
        grad_conv,
        grad_conv,
        grid=(1,),
        in_specs=[whole(FR, D)] * 3 + [rows_at(EDGE, 0), rows_at(EDGE, 3), rows_at(16, 0), rows_at(16, 7)],
        out_specs=(whole(HEADS, 3 * HD, FR), whole(edge_rows, D), whole(edge_rows, D)),
    )
    qkv = lax.all_to_all(packed, "seq", 0, 0, tiled=True)
    before, after = neighbours(("tm", "seq"), first, last)
    square = shape((STRETCH, 128), bf16)
    scores = [pltpu.VMEM((BLOCK, STRETCH), f32)] * 2
    keys, queries, values, edge_nat, edge_att, edge_log, first, last = call(
        edge_forward_kernel,
        (
            shape((128, STRETCH), bf16),
            square,
            square,
            shape((2 * BLOCK, 128), bf16),
            shape((2, HD, BLOCK), bf16),
            shape((2, 8, BLOCK), f32),
            shape((EDGE, 128), bf16),
            shape((EDGE, 128), bf16),
        ),
        qkv,
        scratch=scores,
    )
    edge_before, edge_after = neighbours("tm", first, last)
    mid_nat, mid_att, mid_log = call(
        middle_forward_kernel,
        (
            shape((STRETCH - 2 * BLOCK, 128), bf16),
            shape((CHUNKS - 2, HD, BLOCK), bf16),
            shape((CHUNKS - 2, 8, BLOCK), f32),
        ),
        keys,
        queries,
        values,
        scratch=scores,
        gflops=6,
    )
    att_payload = call(
        assemble_kernel,
        shape((HEADS, 64 + EDGE, 128), bf16),
        edge_nat,
        mid_nat,
        edge_before,
        edge_after,
    )
    half, _ = lax.optimization_barrier((half, att_payload))
    swapped = swap_half(half)
    att_rows = lax.all_to_all(att_payload, "seq", 0, 0, tiled=True)
    in_vmem = pl.BlockSpec(memory_space=pltpu.VMEM)
    in_place = pl.BlockSpec(memory_space=pl.ANY)
    grad_stream, payload = call(
        middle_kernel,
        (shape((FR, D), bf16), shape((HEADS, PART_ROWS + HD, FR), bf16)),
        core,
        att_rows,
        residual,
        before,
        after,
        gain,
        half,
        swapped,
        conv_kernel,
        vectors,
        grad_conv,
        grad_stream_in,
        in_specs=[pl.BlockSpec(memory_space=pltpu.SMEM)]
        + [in_vmem] * 5
        + [in_place] * 2
        + [in_vmem] * 4,
        scratch=(
            pltpu.VMEM((32, HEADS, 32, 128), bf16),
            pltpu.VMEM((ROWS, D), f32),
            pltpu.VMEM((ROWS, D), bf16),
            pltpu.VMEM((8, FR, 128), f32),
            pltpu.VMEM((8, FR, 128), f32),
            pltpu.VMEM((8, ROWS, 128), f32),
            pltpu.VMEM((WIDE, 128), f32),
            pltpu.VMEM((HEADS, PART_ROWS, 128), f32),
            pltpu.VMEM((FR, 2 * D), bf16),
            pltpu.VMEM((FR, D), f32),
            pltpu.SemaphoreType.DMA((2 * HEADS,)),
        ),
    )
    payload = lax.all_to_all(payload, "seq", 0, 0, tiled=True)
    spread = call(
        spread_kernel,
        shape((groups, PART_ROWS, 128), f32),
        payload,
        grid=(1,),
        in_specs=[whole(HEADS, PART_ROWS, 128)],
        out_specs=whole(groups, PART_ROWS, 128),
    )
    totals = lax.all_to_all(spread, "tm", 0, 0, tiled=True)
    tall = pltpu.VMEM((STRETCH, 128), bf16)
    flat = pltpu.VMEM((128, STRETCH), bf16)
    back = call(
        backward_kernel,
        shape((HEADS, 3 * HD + PART_ROWS, FR), bf16),
        qkv,
        edge_att,
        mid_att,
        edge_log,
        mid_log,
        payload,
        gflops=12,
        scratch=(
            tall,
            tall,
            flat,
            flat,
            tall,
            tall,
            pltpu.VMEM((HD, STRETCH), bf16),
            pltpu.VMEM((HD, STRETCH), f32),
        ),
    )
    back = call(
        finish_kernel,
        shape(back.shape, bf16),
        totals,
        back,
        grid=(1,),
        in_specs=[whole(groups, PART_ROWS, 128), in_place],
        out_specs=pl.BlockSpec((HEADS, PART_ROWS, 128), lambda i: (0, 6, 0)),
        input_output_aliases={1: 0},
    )
    back = lax.all_to_all(back, "seq", 0, 0, tiled=True)
    narrow = shape((FR, D), bf16)
    query_grad, key_grad, value_grad, kernel_sum, affine_sum, moments = call(
        lambda *refs: unpack_kernel(frame_total, *refs),
        (narrow, narrow, narrow, shape((KW, D), f32), shape((2, D), f32), shape((2, D), f32)),
        back,
    )
    return (query_grad, key_grad, value_grad, grad_stream, kernel_sum, affine_sum, moments)


def solution(mesh):
    rows = P(("tm", "seq"), None)
    in_specs = (rows, rows, rows, rows, P(), P(None, "seq"), P(), P(), P(), P(), P(), rows, rows)
    out_specs = (rows, rows, rows, rows, P(), P(), P())
    return jax.shard_map(local, mesh=mesh, in_specs=in_specs, out_specs=out_specs, check_vma=False)
```

```python
import math

import jax
import jax.numpy as jnp
from jax import lax
from jax.experimental import pallas as pl
from jax.experimental.pallas import tpu as pltpu
from jax.sharding import PartitionSpec as P

HEADS = 16
HD = 64
D = 1024
FR = 128
KW = 31
HALF = KW // 2
STRETCH = FR * HEADS
epsilon = 1e-05
LOG2E = math.log2(math.e)
SCALE = HD ** (-0.5)
BLOCK = 256
PART_ROWS = 32
EDGE = 32
ROWS = FR + 2 * EDGE
WIDE = FR + EDGE

f32 = jnp.float32
bf16 = jnp.bfloat16
NT = (((1,), (1,)), ((), ()))


def params(megabytes=48):
    return pltpu.CompilerParams(vmem_limit_bytes=megabytes * 1024 * 1024)


def dot(left, right):
    return jnp.dot(left, right, preferred_element_type=f32)


def dot_nt(left, right):
    return lax.dot_general(left, right, NT, preferred_element_type=f32)


def two_parts(value):
    high = value.astype(bf16)
    low = (value - high.astype(f32)).astype(bf16)
    return high, low


def three_parts(value):
    high = value.astype(bf16)
    rest = value - high.astype(f32)
    mid = rest.astype(bf16)
    low = (rest - mid.astype(f32)).astype(bf16)
    return high, mid, low


def pack_kernel(
    chunk_ref,
    query_hbm,
    key_hbm,
    value_hbm,
    weight_hbm,
    res_hbm,
    grad_hbm,
    out_ref,
    first_ref,
    last_ref,
    query_ref,
    key_ref,
    value_ref,
    weight_ref,
    copy_sem,
):
    weight_rows = weight_hbm.at[pl.ds(pl.multiple_of(chunk_ref[0] * 128, 128), 128)]
    pairs = (
        (query_hbm, query_ref),
        (key_hbm, key_ref),
        (value_hbm, value_ref),
        (weight_rows, weight_ref),
        (res_hbm.at[0:EDGE], first_ref.at[0:EDGE]),
        (res_hbm.at[FR - EDGE : FR], last_ref.at[0:EDGE]),
        (grad_hbm.at[0:16], first_ref.at[EDGE : EDGE + 16]),
        (grad_hbm.at[FR - 16 : FR], last_ref.at[EDGE : EDGE + 16]),
    )
    copies = [pltpu.make_async_copy(src, dst, copy_sem.at[i]) for i, (src, dst) in enumerate(pairs)]
    for copy in copies:
        copy.start()
    for item, ref in enumerate((query_ref, key_ref, value_ref)):
        copies[item].wait()
        for pair in range(HEADS // 2):
            turned = ref[:, 128 * pair : 128 * (pair + 1)].T
            out_ref[2 * pair, HD * item : HD * (item + 1), :] = turned[:HD]
            out_ref[2 * pair + 1, HD * item : HD * (item + 1), :] = turned[HD:]
    copies[3].wait()
    for dest in range(HEADS):
        out_ref[dest, 3 * HD :, :] = weight_ref[...]
    for copy in copies[4:]:
        copy.wait()


CHUNKS = STRETCH // BLOCK


def block_rows(block):
    if isinstance(block, int):
        return slice(block * BLOCK, (block + 1) * BLOCK)
    return pl.ds(pl.multiple_of(block * BLOCK, BLOCK), BLOCK)


def low_lanes(rows):
    return lax.broadcasted_iota(jnp.int32, (rows, 128), 1) < HD


def soft_stage(keys_ref, query_ref, value_ref, following, current):
    queries = peak = total = None
    if following is not None:
        block, next_ref = following
        queries = query_ref[block_rows(block), :]
    for chunk in range(CHUNKS):
        rows = slice(BLOCK * chunk, BLOCK * (chunk + 1))
        if following is not None:
            part = dot(queries, keys_ref[:, rows])
            next_ref[:, rows] = part
            part = jnp.maximum(part[:, :128], part[:, 128:])
            peak = part if peak is None else jnp.maximum(peak, part)
        if current is not None:
            score_ref, top = current
            weights = jnp.exp2(score_ref[:, rows] - jnp.concatenate([top, top], axis=1)).astype(bf16)
            part = dot(weights, value_ref[rows, :])
            total = part if total is None else total + part
    if peak is not None:
        peak = jnp.broadcast_to(jnp.max(peak, axis=1, keepdims=True), (BLOCK, 128))
    return peak, total


def store_attended(total, peak, nat_ref, rows, turned_ref, log_ref, place):
    norm = jnp.broadcast_to(total[:, HD : HD + 1], (BLOCK, 128))
    attended = (total / norm).astype(bf16).astype(f32)
    low = low_lanes(BLOCK)
    nat_ref[rows, :] = jnp.where(low, attended, pltpu.roll(attended, HD, 1)).astype(bf16)
    turned = jnp.where(low, attended, peak + jnp.log2(norm)).T
    turned_ref[place] = turned[:HD].astype(bf16)
    log_ref[place] = turned[HD : HD + 8]


def edge_forward_kernel(
    qkv_ref,
    keys_ref,
    query_ref,
    value_ref,
    nat_ref,
    turned_ref,
    log_ref,
    first_ref,
    last_ref,
    score_ref,
    other_ref,
):
    pad_rows = lax.broadcasted_iota(jnp.int32, (HD, FR), 0)
    ones = jnp.where(pad_rows == 0, 1.0, 0.0).astype(bf16)
    for source in range(HEADS):
        span = slice(FR * source, FR * (source + 1))
        key_block = qkv_ref[source, HD : 2 * HD, :]
        keys_ref[0:HD, span] = key_block
        keys_ref[HD : 2 * HD, span] = key_block
        high, low = two_parts(qkv_ref[source, 0:HD, :].astype(f32) * (SCALE * LOG2E))
        query_ref[span, :] = jnp.concatenate([high, low], axis=0).T
        value_ref[span, :] = jnp.concatenate([qkv_ref[source, 2 * HD : 3 * HD, :], ones], axis=0).T
    stage = lambda *pair: soft_stage(keys_ref, query_ref, value_ref, *pair)
    top, _ = stage((0, score_ref), None)
    final_top, total = stage((CHUNKS - 1, other_ref), (score_ref, top))
    store_attended(total, top, nat_ref, slice(0, BLOCK), turned_ref, log_ref, 0)
    _, total = stage(None, (other_ref, final_top))
    store_attended(total, final_top, nat_ref, slice(BLOCK, 2 * BLOCK), turned_ref, log_ref, 1)
    first_ref[...] = nat_ref[0:EDGE, :]
    last_ref[...] = nat_ref[2 * BLOCK - EDGE : 2 * BLOCK, :]


def middle_forward_kernel(
    keys_ref, query_ref, value_ref, nat_ref, turned_ref, log_ref, score_ref, other_ref
):
    stage = lambda *pair: soft_stage(keys_ref, query_ref, value_ref, *pair)

    def store(total, top, place):
        store_attended(total, top, nat_ref, block_rows(place), turned_ref, log_ref, place)

    def two(index, top):
        place = 2 * index
        next_top, total = stage((place + 2, other_ref), (score_ref, top))
        store(total, top, place)
        last_top, total = stage((place + 3, score_ref), (other_ref, next_top))
        store(total, next_top, place + 1)
        return last_top

    top, _ = stage((1, score_ref), None)
    top = lax.fori_loop(0, 2, two, top)
    next_top, total = stage((6, other_ref), (score_ref, top))
    store(total, top, 4)
    _, total = stage(None, (other_ref, next_top))
    store(total, next_top, 5)


def assemble_kernel(edge_ref, middle_ref, before_ref, after_ref, out_ref):
    def frames(begin, count):
        if begin < 0:
            return before_ref[...]
        if begin >= STRETCH:
            return after_ref[...]
        if begin < BLOCK:
            return edge_ref[begin : begin + count, :]
        if begin < STRETCH - BLOCK:
            return middle_ref[begin - BLOCK : begin - BLOCK + count, :]
        begin -= STRETCH - 2 * BLOCK
        return edge_ref[begin : begin + count, :]

    for dest in range(HEADS):
        begin = FR * dest
        low = low_lanes(64)
        out_ref[dest, 0:64, :] = jnp.where(
            low, frames(begin, 64).astype(f32), frames(begin + 64, 64).astype(f32)
        ).astype(bf16)
        low = low_lanes(EDGE)
        out_ref[dest, 64 : 64 + EDGE, :] = jnp.where(
            low, frames(begin - EDGE, EDGE).astype(f32), frames(begin + FR, EDGE).astype(f32)
        ).astype(bf16)


def middle_kernel(
    att_ref,
    residual_ref,
    before_ref,
    after_ref,
    gain_ref,
    weight_hbm,
    taps_ref,
    vec_ref,
    grad_ref,
    skip_ref,
    stream_ref,
    payload_ref,
    weight_ref,
    normed_ref,
    low_ref,
    linear_ref,
    gate_ref,
    glu_ref,
    grad_ext_ref,
    sums_ref,
    proj_ref,
    hat_ref,
    copy_sem,
):
    def fetch(column):
        return pltpu.make_async_copy(weight_hbm.at[:, column], weight_ref.at[:, column], copy_sem.at[column])

    for part in range(8):
        fetch(part).start()
        fetch(part + 8).start()
    lanes = low_lanes(64 + EDGE)
    for pair in range(HEADS // 2):
        cols = slice(128 * pair, 128 * (pair + 1))
        even = att_ref[2 * pair].astype(f32)
        odd = att_ref[2 * pair + 1].astype(f32)
        low = jnp.where(lanes, even, pltpu.roll(odd, HD, 1))
        high = jnp.where(lanes, pltpu.roll(even, HD, 1), odd)
        normed_ref[0:EDGE, cols] = low[64:] + before_ref[0:EDGE, cols].astype(f32)
        normed_ref[EDGE : EDGE + 64, cols] = low[:64] + residual_ref[0:64, cols].astype(f32)
        normed_ref[EDGE + 64 : EDGE + FR, cols] = high[:64] + residual_ref[64:FR, cols].astype(f32)
        normed_ref[EDGE + FR :, cols] = high[64:] + after_ref[0:EDGE, cols].astype(f32)
    stream = normed_ref[...]
    centred = stream - jnp.mean(stream, axis=1, keepdims=True)
    inv_std = lax.rsqrt(jnp.mean(centred * centred, axis=1, keepdims=True) + epsilon)
    normed = centred * inv_std
    normed_ref[...] = normed
    inv_own = inv_std[EDGE : EDGE + FR]
    low_ref[...] = (normed * gain_ref[...]).astype(bf16)
    sums_ref[...] = jnp.zeros_like(sums_ref)
    for part in range(8):
        fetch(part).wait()
        fetch(part + 8).wait()
        weights = jnp.concatenate(
            [weight_ref[:, part].reshape(D, 128), weight_ref[:, part + 8].reshape(D, 128)], axis=1
        )
        projected = dot(low_ref[...], weights)
        linear = projected[:, :128]
        gate = jax.nn.sigmoid(projected[:, 128:])
        linear_ref[part] = linear[EDGE : EDGE + FR]
        gate_ref[part] = gate[EDGE : EDGE + FR]
        glu_ref[part] = (linear * gate).astype(bf16).astype(f32)
    for part in range(8):
        cols = slice(128 * part, 128 * (part + 1))

        def put(row, total):
            place = (row % 4) * 8 + part
            sums_ref[row // 4, place : place + 1, :] = total

        conv = jnp.zeros((WIDE, 128), f32)
        for tap in range(KW):
            conv = conv + taps_ref[tap : tap + 1, cols] * glu_ref[part, tap + 1 : tap + 1 + WIDE, :]
        gamma = vec_ref[0:1, cols]
        inv_scale = lax.rsqrt(vec_ref[3:4, cols] + epsilon)
        zhat = (conv - vec_ref[2:3, cols]) * inv_scale
        shifted = gamma * zhat + vec_ref[1:2, cols]
        sig = jax.nn.sigmoid(shifted)
        grads = jnp.concatenate(
            [before_ref[EDGE:, cols], grad_ref[:, cols], after_ref[EDGE:, cols]], axis=0
        ).astype(f32)
        grad_shift = grads * sig * (1.0 + shifted * (1.0 - sig))
        grad_ext_ref[...] = (grad_shift * (gamma * inv_scale)).astype(bf16).astype(f32)
        own = slice(EDGE // 2, EDGE // 2 + FR)
        conv, zhat, grad_shift = conv[own], zhat[own], grad_shift[own]
        for row, value in enumerate((grad_shift * zhat, grad_shift, conv, conv * conv)):
            total = jnp.sum(value, axis=0, keepdims=True)
            put(KW + row, total)
            put(KW + 4 + row, total - total.astype(bf16).astype(f32))
        grad_own = grad_ext_ref[own, :]
        for tap in range(KW):
            begin = EDGE + tap - HALF
            put(tap, jnp.sum(grad_own * glu_ref[part, begin : begin + FR, :], axis=0, keepdims=True))
        grad_glu = jnp.zeros((FR, 128), f32)
        for tap in range(KW):
            begin = EDGE // 2 + HALF - tap
            grad_glu = grad_glu + taps_ref[tap : tap + 1, cols] * grad_ext_ref[begin : begin + FR, :]
        gate = gate_ref[part]
        half = grad_glu * gate
        proj_ref[:, cols] = half.astype(bf16)
        proj_ref[:, D + 128 * part : D + 128 * (part + 1)] = (half * linear_ref[part] * (1.0 - gate)).astype(bf16)
    payload_ref[:, 0:PART_ROWS, :] = sums_ref[...].astype(bf16)
    proj = proj_ref[...]
    for part in range(4):
        cols = slice(256 * part, 256 * (part + 1))
        columns = [weight_ref[2 * part : 2 * (part + 1), s].reshape(256, 128) for s in range(16)]
        hat_ref[:, cols] = dot_nt(proj, jnp.concatenate(columns, axis=1)) * gain_ref[:, cols]
    hat = hat_ref[...]
    normed = normed_ref[EDGE : EDGE + FR, :]
    mean = jnp.mean(hat, axis=1, keepdims=True)
    mean_normed = jnp.mean(hat * normed, axis=1, keepdims=True)
    centre = inv_own * (hat - mean - normed * mean_normed)
    stream = (centre + skip_ref[...].astype(f32)).astype(bf16)
    stream_ref[...] = stream
    for pair in range(HEADS // 2):
        turned = stream[:, 128 * pair : 128 * (pair + 1)].T
        payload_ref[2 * pair, PART_ROWS:, :] = turned[:HD]
        payload_ref[2 * pair + 1, PART_ROWS:, :] = turned[HD:]


def spread_kernel(payload_ref, out_ref):
    total = jnp.sum(payload_ref[...].astype(f32), axis=0)
    out_ref[...] = jnp.broadcast_to(total[None], out_ref.shape)


def backward_kernel(
    qkv_ref,
    edge_att_ref,
    mid_att_ref,
    edge_log_ref,
    mid_log_ref,
    payload_ref,
    out_ref,
    keys_ref,
    values_ref,
    query_ref,
    grad_ref,
    query_rows_ref,
    grad_rows_ref,
    turned_ref,
    total_ref,
):
    pad_rows = lax.broadcasted_iota(jnp.int32, (HD, FR), 0)
    ones = jnp.where(pad_rows < 3, 1.0, 0.0).astype(bf16)
    for source in range(HEADS):
        span = slice(FR * source, FR * (source + 1))
        key_block = qkv_ref[source, HD : 2 * HD, :]
        turned_ref[:, span] = key_block
        keys_ref[span, :] = jnp.concatenate([key_block, ones], axis=0).T
        values_ref[span, :] = jnp.concatenate([qkv_ref[source, 2 * HD : 3 * HD, :], ones], axis=0).T
        grads = payload_ref[source, PART_ROWS:, :]
        block, side = divmod(source, 2)
        if 0 < block < CHUNKS - 1:
            att, log, block = mid_att_ref, mid_log_ref, block - 1
        else:
            att, log, block = edge_att_ref, edge_log_ref, min(block, 1)
        lanes = slice(FR * side, FR * (side + 1))
        delta = jnp.sum(grads.astype(f32) * att[block, :, lanes].astype(f32), axis=0, keepdims=True)
        logs = log[block, 0:1, lanes] * (1.0 / (SCALE * LOG2E))
        for ref, rows_ref, body, row in (
            (query_ref, query_rows_ref, qkv_ref[source, 0:HD, :], logs),
            (grad_ref, grad_rows_ref, grads, delta),
        ):
            parts = three_parts(jnp.broadcast_to(-row, (HD, FR)))
            tail = jnp.zeros((HD, FR), f32)
            for place in range(3):
                tail = jnp.where(pad_rows == place, parts[place].astype(f32), tail)
            both = jnp.concatenate([body, tail.astype(bf16)], axis=0)
            ref[:, span] = both
            rows_ref[span, :] = both.T
    total_ref[...] = jnp.zeros_like(total_ref)

    def step(block, carry):
        rows = block_rows(block)
        keys, values, turned = keys_ref[rows, :], values_ref[rows, :], turned_ref[:, rows]

        def products(chunk):
            cols = block_rows(chunk)
            return dot(keys, query_ref[:, cols]), dot(values, grad_ref[:, cols])

        key_total = jnp.zeros((BLOCK, 128), f32)
        value_total = jnp.zeros((BLOCK, 128), f32)
        ready = products(0)
        for chunk in range(CHUNKS):
            cols = block_rows(chunk)
            scores, grad_probs = ready
            if chunk + 1 < CHUNKS:
                ready = products(chunk + 1)
            probs = jnp.exp2(scores * (SCALE * LOG2E))
            grad_scores = (probs * grad_probs).astype(bf16)
            value_total = value_total + dot(probs.astype(bf16), grad_rows_ref[cols, :])
            key_total = key_total + dot(grad_scores, query_rows_ref[cols, :])
            total_ref[:, cols] += dot(turned, grad_scores)
        for place, total in ((1, key_total * SCALE), (2, value_total)):
            turned_total = total.T[:HD].astype(bf16)
            out_ref[2 * block, HD * place : HD * (place + 1), :] = turned_total[:, :FR]
            out_ref[2 * block + 1, HD * place : HD * (place + 1), :] = turned_total[:, FR:]
        return carry

    lax.fori_loop(0, CHUNKS, step, 0)
    for source in range(HEADS):
        span = slice(FR * source, FR * (source + 1))
        out_ref[source, 0:HD, :] = (total_ref[:, span] * SCALE).astype(bf16)


def finish_kernel(parts_ref, payload_ref, out_ref):
    total = jnp.sum(parts_ref[...], axis=0).astype(bf16)
    out_ref[...] = jnp.broadcast_to(total[None], out_ref.shape)


def unpack_kernel(frame_total, back_ref, query_ref, key_ref, value_ref, taps_ref, affine_ref, moments_ref):
    for item, ref in enumerate((query_ref, key_ref, value_ref)):
        for pair in range(HEADS // 2):
            turned = back_ref[2 * pair : 2 * pair + 2, HD * item : HD * (item + 1), :].reshape(128, FR)
            ref[:, 128 * pair : 128 * (pair + 1)] = turned.T
    totals = [back_ref[source, 3 * HD :, :].astype(f32) for source in range(10)]

    def fetch(row, part):
        place = (row % 4) * 8 + part
        return totals[row // 4][place : place + 1]

    for part in range(8):
        cols = slice(128 * part, 128 * (part + 1))
        for row in range(KW):
            taps_ref[row : row + 1, cols] = fetch(row, part)
        for row in range(4):
            ref, factor = (affine_ref, 1.0) if row < 2 else (moments_ref, 1.0 / frame_total)
            total = fetch(KW + row, part) + fetch(KW + 4 + row, part)
            ref[row % 2 : row % 2 + 1, cols] = total * factor


def call(kernel, out_shape, *args, scratch=(), gflops=0, **extra):
    if gflops:
        extra["cost_estimate"] = pl.CostEstimate(
            flops=gflops * 10**9, bytes_accessed=4 * 2**20, transcendentals=STRETCH * STRETCH
        )
    return pl.pallas_call(
        kernel, out_shape=out_shape, scratch_shapes=list(scratch), compiler_params=params(), **extra
    )(*args)


def shape(dims, dtype):
    return jax.ShapeDtypeStruct(dims, dtype)


def in_high_memory(array):
    return pltpu.with_memory_space_constraint(array, pltpu.HBM)


def whole(*dims):
    return pl.BlockSpec(dims, lambda i: (0,) * len(dims))


def weight_chunk():
    place = lax.axis_index("tm")
    return (place // 8) * 2 + lax.rem(place, 2)


def gather_weights(rows):
    peers = [[8 * x + 2 * low + core for x in range(4) for core in range(2)] for low in range(4)]
    return lax.all_gather(rows, "tm", axis=0, axis_index_groups=peers)


def neighbours(axes, first, last):
    size = lax.axis_size(axes)
    up = [(i, i + 1) for i in range(size - 1)]
    down = [(i + 1, i) for i in range(size - 1)]
    return lax.ppermute(last, axes, up), lax.ppermute(first, axes, down)


def local(
    query_in,
    key_in,
    value_in,
    residual,
    layer_gain,
    proj_weight,
    conv_kernel,
    batch_gamma,
    batch_beta,
    stale_mean,
    stale_variance,
    grad_conv,
    grad_stream_in,
):
    groups = lax.axis_size("tm")
    frame_total = FR * groups * lax.axis_size("seq")
    gain = layer_gain.reshape(1, D)
    vectors = jnp.stack([batch_gamma, batch_beta, stale_mean, stale_variance])
    in_hbm = pl.BlockSpec(memory_space=pltpu.HBM)
    in_vmem = pl.BlockSpec(memory_space=pltpu.VMEM)

    edge_rows = EDGE + EDGE // 2
    block = pltpu.VMEM((FR, D), bf16)
    packed, first, last = call(
        pack_kernel,
        (shape((HEADS, 3 * HD + 128, FR), bf16), shape((edge_rows, D), bf16), shape((edge_rows, D), bf16)),
        weight_chunk().reshape(1),
        *map(in_high_memory, (query_in, key_in, value_in, proj_weight, residual, grad_conv)),
        in_specs=[pl.BlockSpec(memory_space=pltpu.SMEM)] + [in_hbm] * 6,
        scratch=(block, block, block, pltpu.VMEM((128, 128), bf16), pltpu.SemaphoreType.DMA((8,))),
    )
    qkv = lax.all_to_all(packed, "seq", 0, 0, tiled=True)
    before, after = neighbours(("tm", "seq"), first, last)
    qkv, before, after = lax.optimization_barrier((qkv, before, after))
    weights = gather_weights(qkv[:, 3 * HD :])
    square = shape((STRETCH, 128), bf16)
    scores = [pltpu.VMEM((BLOCK, STRETCH), f32)] * 2
    keys, queries, values, edge_nat, edge_att, edge_log, first, last = call(
        edge_forward_kernel,
        (
            shape((128, STRETCH), bf16),
            square,
            square,
            shape((2 * BLOCK, 128), bf16),
            shape((2, HD, BLOCK), bf16),
            shape((2, 8, BLOCK), f32),
            shape((EDGE, 128), bf16),
            shape((EDGE, 128), bf16),
        ),
        qkv,
        scratch=scores,
    )
    edge_before, edge_after = neighbours("tm", first, last)
    mid_nat, mid_att, mid_log = call(
        middle_forward_kernel,
        (
            shape((STRETCH - 2 * BLOCK, 128), bf16),
            shape((CHUNKS - 2, HD, BLOCK), bf16),
            shape((CHUNKS - 2, 8, BLOCK), f32),
        ),
        keys,
        queries,
        values,
        scratch=scores,
        gflops=6,
    )
    att_payload = call(
        assemble_kernel,
        shape((HEADS, 64 + EDGE, 128), bf16),
        edge_nat,
        mid_nat,
        edge_before,
        edge_after,
    )
    att_rows = lax.all_to_all(att_payload, "seq", 0, 0, tiled=True)
    grad_stream, payload = call(
        middle_kernel,
        (shape((FR, D), bf16), shape((HEADS, PART_ROWS + HD, FR), bf16)),
        att_rows,
        residual,
        before,
        after,
        gain,
        in_high_memory(weights),
        conv_kernel,
        vectors,
        grad_conv,
        grad_stream_in,
        in_specs=[in_vmem] * 5 + [in_hbm] + [in_vmem] * 4,
        scratch=(
            pltpu.VMEM((8, HEADS, 128, 128), bf16),
            pltpu.VMEM((ROWS, D), f32),
            pltpu.VMEM((ROWS, D), bf16),
            pltpu.VMEM((8, FR, 128), f32),
            pltpu.VMEM((8, FR, 128), f32),
            pltpu.VMEM((8, ROWS, 128), f32),
            pltpu.VMEM((WIDE, 128), f32),
            pltpu.VMEM((HEADS, PART_ROWS, 128), f32),
            pltpu.VMEM((FR, 2 * D), bf16),
            pltpu.VMEM((FR, D), f32),
            pltpu.SemaphoreType.DMA((HEADS,)),
        ),
    )
    payload = lax.all_to_all(payload, "seq", 0, 0, tiled=True)
    spread = call(
        spread_kernel,
        shape((groups, PART_ROWS, 128), f32),
        payload,
        grid=(1,),
        in_specs=[whole(HEADS, PART_ROWS, 128)],
        out_specs=whole(groups, PART_ROWS, 128),
    )
    totals = lax.all_to_all(spread, "tm", 0, 0, tiled=True)
    tall = pltpu.VMEM((STRETCH, 128), bf16)
    flat = pltpu.VMEM((128, STRETCH), bf16)
    back = call(
        backward_kernel,
        shape((HEADS, 3 * HD + PART_ROWS, FR), bf16),
        qkv,
        edge_att,
        mid_att,
        edge_log,
        mid_log,
        payload,
        gflops=12,
        scratch=(
            tall,
            tall,
            flat,
            flat,
            tall,
            tall,
            pltpu.VMEM((HD, STRETCH), bf16),
            pltpu.VMEM((HD, STRETCH), f32),
        ),
    )
    back = call(
        finish_kernel,
        shape(back.shape, bf16),
        totals,
        back,
        grid=(1,),
        in_specs=[whole(groups, PART_ROWS, 128), pl.BlockSpec(memory_space=pl.ANY)],
        out_specs=pl.BlockSpec((HEADS, PART_ROWS, 128), lambda i: (0, 6, 0)),
        input_output_aliases={1: 0},
    )
    back = lax.all_to_all(back, "seq", 0, 0, tiled=True)
    narrow = shape((FR, D), bf16)
    query_grad, key_grad, value_grad, kernel_sum, affine_sum, moments = call(
        lambda *refs: unpack_kernel(frame_total, *refs),
        (narrow, narrow, narrow, shape((KW, D), f32), shape((2, D), f32), shape((2, D), f32)),
        back,
    )
    return (query_grad, key_grad, value_grad, grad_stream, kernel_sum, affine_sum, moments)


def solution(mesh):
    rows = P(("tm", "seq"), None)
    in_specs = (rows, rows, rows, rows, P(), P(None, "seq"), P(), P(), P(), P(), P(), rows, rows)
    out_specs = (rows, rows, rows, rows, P(), P(), P())
    return jax.shard_map(local, mesh=mesh, in_specs=in_specs, out_specs=out_specs, check_vma=False)
```

```python
import math

import jax
import jax.numpy as jnp
from jax import lax
from jax.experimental import pallas as pl
from jax.experimental.pallas import tpu as pltpu
from jax.sharding import PartitionSpec as P

HEADS = 16
HD = 64
D = 1024
FR = 128
KW = 31
HALF = KW // 2
STRETCH = FR * HEADS
epsilon = 1e-05
LOG2E = math.log2(math.e)
SCALE = HD ** (-0.5)
BLOCK = 256
PART_ROWS = 32
EDGE = 32
ROWS = FR + 2 * EDGE
WIDE = FR + EDGE

f32 = jnp.float32
bf16 = jnp.bfloat16
NT = (((1,), (1,)), ((), ()))


def params(megabytes=48):
    return pltpu.CompilerParams(vmem_limit_bytes=megabytes * 1024 * 1024)


def dot(left, right):
    return jnp.dot(left, right, preferred_element_type=f32)


def dot_nt(left, right):
    return lax.dot_general(left, right, NT, preferred_element_type=f32)


def two_parts(value):
    high = value.astype(bf16)
    low = (value - high.astype(f32)).astype(bf16)
    return high, low


def three_parts(value):
    high = value.astype(bf16)
    rest = value - high.astype(f32)
    mid = rest.astype(bf16)
    low = (rest - mid.astype(f32)).astype(bf16)
    return high, mid, low


def chunk_kernel(chunk_ref, weight_hbm, out_ref, weight_ref, copy_sem):
    rows = pl.ds(pl.multiple_of(chunk_ref[0] * 128, 128), 128)
    copy = pltpu.make_async_copy(weight_hbm.at[rows], weight_ref, copy_sem)
    copy.start()
    copy.wait()
    for dest in range(HEADS):
        out_ref[dest] = weight_ref[...]


def pack_kernel(
    query_hbm,
    key_hbm,
    value_hbm,
    res_hbm,
    grad_hbm,
    out_ref,
    first_ref,
    last_ref,
    query_ref,
    key_ref,
    value_ref,
    copy_sem,
):
    pairs = (
        (query_hbm, query_ref),
        (key_hbm, key_ref),
        (value_hbm, value_ref),
        (res_hbm.at[0:EDGE], first_ref.at[0:EDGE]),
        (res_hbm.at[FR - EDGE : FR], last_ref.at[0:EDGE]),
        (grad_hbm.at[0:16], first_ref.at[EDGE : EDGE + 16]),
        (grad_hbm.at[FR - 16 : FR], last_ref.at[EDGE : EDGE + 16]),
    )
    copies = [pltpu.make_async_copy(src, dst, copy_sem.at[i]) for i, (src, dst) in enumerate(pairs)]
    for copy in copies:
        copy.start()
    for item, ref in enumerate((query_ref, key_ref, value_ref)):
        copies[item].wait()
        for pair in range(HEADS // 2):
            turned = ref[:, 128 * pair : 128 * (pair + 1)].T
            out_ref[2 * pair, HD * item : HD * (item + 1), :] = turned[:HD]
            out_ref[2 * pair + 1, HD * item : HD * (item + 1), :] = turned[HD:]
    for copy in copies[3:]:
        copy.wait()


CHUNKS = STRETCH // BLOCK


def block_rows(block):
    if isinstance(block, int):
        return slice(block * BLOCK, (block + 1) * BLOCK)
    return pl.ds(pl.multiple_of(block * BLOCK, BLOCK), BLOCK)


def low_lanes(rows):
    return lax.broadcasted_iota(jnp.int32, (rows, 128), 1) < HD


def soft_stage(keys_ref, query_ref, value_ref, following, current):
    queries = peak = total = None
    if following is not None:
        block, next_ref = following
        queries = query_ref[block_rows(block), :]
    for chunk in range(CHUNKS):
        rows = slice(BLOCK * chunk, BLOCK * (chunk + 1))
        if following is not None:
            part = dot(queries, keys_ref[:, rows])
            next_ref[:, rows] = part
            part = jnp.maximum(part[:, :128], part[:, 128:])
            peak = part if peak is None else jnp.maximum(peak, part)
        if current is not None:
            score_ref, top = current
            weights = jnp.exp2(score_ref[:, rows] - jnp.concatenate([top, top], axis=1)).astype(bf16)
            part = dot(weights, value_ref[rows, :])
            total = part if total is None else total + part
    if peak is not None:
        peak = jnp.broadcast_to(jnp.max(peak, axis=1, keepdims=True), (BLOCK, 128))
    return peak, total


def store_attended(total, peak, nat_ref, rows, turned_ref, log_ref, place):
    norm = jnp.broadcast_to(total[:, HD : HD + 1], (BLOCK, 128))
    attended = (total / norm).astype(bf16).astype(f32)
    low = low_lanes(BLOCK)
    nat_ref[rows, :] = jnp.where(low, attended, pltpu.roll(attended, HD, 1)).astype(bf16)
    turned = jnp.where(low, attended, peak + jnp.log2(norm)).T
    turned_ref[place] = turned[:HD].astype(bf16)
    log_ref[place] = turned[HD : HD + 8]


def edge_forward_kernel(
    qkv_ref,
    keys_ref,
    query_ref,
    value_ref,
    nat_ref,
    turned_ref,
    log_ref,
    first_ref,
    last_ref,
    score_ref,
    other_ref,
):
    pad_rows = lax.broadcasted_iota(jnp.int32, (HD, FR), 0)
    ones = jnp.where(pad_rows == 0, 1.0, 0.0).astype(bf16)
    for source in range(HEADS):
        span = slice(FR * source, FR * (source + 1))
        key_block = qkv_ref[source, HD : 2 * HD, :]
        keys_ref[0:HD, span] = key_block
        keys_ref[HD : 2 * HD, span] = key_block
        high, low = two_parts(qkv_ref[source, 0:HD, :].astype(f32) * (SCALE * LOG2E))
        query_ref[span, :] = jnp.concatenate([high, low], axis=0).T
        value_ref[span, :] = jnp.concatenate([qkv_ref[source, 2 * HD : 3 * HD, :], ones], axis=0).T
    stage = lambda *pair: soft_stage(keys_ref, query_ref, value_ref, *pair)
    top, _ = stage((0, score_ref), None)
    final_top, total = stage((CHUNKS - 1, other_ref), (score_ref, top))
    store_attended(total, top, nat_ref, slice(0, BLOCK), turned_ref, log_ref, 0)
    _, total = stage(None, (other_ref, final_top))
    store_attended(total, final_top, nat_ref, slice(BLOCK, 2 * BLOCK), turned_ref, log_ref, 1)
    first_ref[...] = nat_ref[0:EDGE, :]
    last_ref[...] = nat_ref[2 * BLOCK - EDGE : 2 * BLOCK, :]


def middle_forward_kernel(
    keys_ref, query_ref, value_ref, nat_ref, turned_ref, log_ref, score_ref, other_ref
):
    stage = lambda *pair: soft_stage(keys_ref, query_ref, value_ref, *pair)

    def store(total, top, place):
        store_attended(total, top, nat_ref, block_rows(place), turned_ref, log_ref, place)

    def two(index, top):
        place = 2 * index
        next_top, total = stage((place + 2, other_ref), (score_ref, top))
        store(total, top, place)
        last_top, total = stage((place + 3, score_ref), (other_ref, next_top))
        store(total, next_top, place + 1)
        return last_top

    top, _ = stage((1, score_ref), None)
    top = lax.fori_loop(0, 2, two, top)
    next_top, total = stage((6, other_ref), (score_ref, top))
    store(total, top, 4)
    _, total = stage(None, (other_ref, next_top))
    store(total, next_top, 5)


def assemble_kernel(edge_ref, middle_ref, before_ref, after_ref, out_ref):
    def frames(begin, count):
        if begin < 0:
            return before_ref[...]
        if begin >= STRETCH:
            return after_ref[...]
        if begin < BLOCK:
            return edge_ref[begin : begin + count, :]
        if begin < STRETCH - BLOCK:
            return middle_ref[begin - BLOCK : begin - BLOCK + count, :]
        begin -= STRETCH - 2 * BLOCK
        return edge_ref[begin : begin + count, :]

    for dest in range(HEADS):
        begin = FR * dest
        low = low_lanes(64)
        out_ref[dest, 0:64, :] = jnp.where(
            low, frames(begin, 64).astype(f32), frames(begin + 64, 64).astype(f32)
        ).astype(bf16)
        low = low_lanes(EDGE)
        out_ref[dest, 64 : 64 + EDGE, :] = jnp.where(
            low, frames(begin - EDGE, EDGE).astype(f32), frames(begin + FR, EDGE).astype(f32)
        ).astype(bf16)


def middle_kernel(
    att_ref,
    residual_ref,
    before_ref,
    after_ref,
    gain_ref,
    weight_hbm,
    taps_ref,
    vec_ref,
    grad_ref,
    skip_ref,
    stream_ref,
    payload_ref,
    weight_ref,
    normed_ref,
    low_ref,
    linear_ref,
    gate_ref,
    glu_ref,
    grad_ext_ref,
    sums_ref,
    proj_ref,
    hat_ref,
    copy_sem,
):
    def fetch(column):
        return pltpu.make_async_copy(weight_hbm.at[:, column], weight_ref.at[:, column], copy_sem.at[column])

    for part in range(8):
        fetch(part).start()
        fetch(part + 8).start()
    lanes = low_lanes(64 + EDGE)
    for pair in range(HEADS // 2):
        cols = slice(128 * pair, 128 * (pair + 1))
        even = att_ref[2 * pair].astype(f32)
        odd = att_ref[2 * pair + 1].astype(f32)
        low = jnp.where(lanes, even, pltpu.roll(odd, HD, 1))
        high = jnp.where(lanes, pltpu.roll(even, HD, 1), odd)
        normed_ref[0:EDGE, cols] = low[64:] + before_ref[0:EDGE, cols].astype(f32)
        normed_ref[EDGE : EDGE + 64, cols] = low[:64] + residual_ref[0:64, cols].astype(f32)
        normed_ref[EDGE + 64 : EDGE + FR, cols] = high[:64] + residual_ref[64:FR, cols].astype(f32)
        normed_ref[EDGE + FR :, cols] = high[64:] + after_ref[0:EDGE, cols].astype(f32)
    stream = normed_ref[...]
    centred = stream - jnp.mean(stream, axis=1, keepdims=True)
    inv_std = lax.rsqrt(jnp.mean(centred * centred, axis=1, keepdims=True) + epsilon)
    normed = centred * inv_std
    normed_ref[...] = normed
    inv_own = inv_std[EDGE : EDGE + FR]
    low_ref[...] = (normed * gain_ref[...]).astype(bf16)
    sums_ref[...] = jnp.zeros_like(sums_ref)
    for part in range(8):
        fetch(part).wait()
        fetch(part + 8).wait()
        weights = jnp.concatenate(
            [weight_ref[:, part].reshape(D, 128), weight_ref[:, part + 8].reshape(D, 128)], axis=1
        )
        projected = dot(low_ref[...], weights)
        linear = projected[:, :128]
        gate = jax.nn.sigmoid(projected[:, 128:])
        linear_ref[part] = linear[EDGE : EDGE + FR]
        gate_ref[part] = gate[EDGE : EDGE + FR]
        glu_ref[part] = (linear * gate).astype(bf16).astype(f32)
    for part in range(8):
        cols = slice(128 * part, 128 * (part + 1))

        def put(row, total):
            place = (row % 4) * 8 + part
            sums_ref[row // 4, place : place + 1, :] = total

        conv = jnp.zeros((WIDE, 128), f32)
        for tap in range(KW):
            conv = conv + taps_ref[tap : tap + 1, cols] * glu_ref[part, tap + 1 : tap + 1 + WIDE, :]
        gamma = vec_ref[0:1, cols]
        inv_scale = lax.rsqrt(vec_ref[3:4, cols] + epsilon)
        zhat = (conv - vec_ref[2:3, cols]) * inv_scale
        shifted = gamma * zhat + vec_ref[1:2, cols]
        sig = jax.nn.sigmoid(shifted)
        grads = jnp.concatenate(
            [before_ref[EDGE:, cols], grad_ref[:, cols], after_ref[EDGE:, cols]], axis=0
        ).astype(f32)
        grad_shift = grads * sig * (1.0 + shifted * (1.0 - sig))
        grad_ext_ref[...] = (grad_shift * (gamma * inv_scale)).astype(bf16).astype(f32)
        own = slice(EDGE // 2, EDGE // 2 + FR)
        conv, zhat, grad_shift = conv[own], zhat[own], grad_shift[own]
        for row, value in enumerate((grad_shift * zhat, grad_shift, conv, conv * conv)):
            total = jnp.sum(value, axis=0, keepdims=True)
            put(KW + row, total)
            put(KW + 4 + row, total - total.astype(bf16).astype(f32))
        grad_own = grad_ext_ref[own, :]
        for tap in range(KW):
            begin = EDGE + tap - HALF
            put(tap, jnp.sum(grad_own * glu_ref[part, begin : begin + FR, :], axis=0, keepdims=True))
        grad_glu = jnp.zeros((FR, 128), f32)
        for tap in range(KW):
            begin = EDGE // 2 + HALF - tap
            grad_glu = grad_glu + taps_ref[tap : tap + 1, cols] * grad_ext_ref[begin : begin + FR, :]
        gate = gate_ref[part]
        half = grad_glu * gate
        proj_ref[:, cols] = half.astype(bf16)
        proj_ref[:, D + 128 * part : D + 128 * (part + 1)] = (half * linear_ref[part] * (1.0 - gate)).astype(bf16)
    payload_ref[:, 0:PART_ROWS, :] = sums_ref[...].astype(bf16)
    proj = proj_ref[...]
    for part in range(4):
        cols = slice(256 * part, 256 * (part + 1))
        columns = [weight_ref[2 * part : 2 * (part + 1), s].reshape(256, 128) for s in range(16)]
        hat_ref[:, cols] = dot_nt(proj, jnp.concatenate(columns, axis=1)) * gain_ref[:, cols]
    hat = hat_ref[...]
    normed = normed_ref[EDGE : EDGE + FR, :]
    mean = jnp.mean(hat, axis=1, keepdims=True)
    mean_normed = jnp.mean(hat * normed, axis=1, keepdims=True)
    centre = inv_own * (hat - mean - normed * mean_normed)
    stream = (centre + skip_ref[...].astype(f32)).astype(bf16)
    stream_ref[...] = stream
    for pair in range(HEADS // 2):
        turned = stream[:, 128 * pair : 128 * (pair + 1)].T
        payload_ref[2 * pair, PART_ROWS:, :] = turned[:HD]
        payload_ref[2 * pair + 1, PART_ROWS:, :] = turned[HD:]


def spread_kernel(payload_ref, out_ref):
    total = jnp.sum(payload_ref[...].astype(f32), axis=0)
    out_ref[...] = jnp.broadcast_to(total[None], out_ref.shape)


def backward_kernel(
    qkv_ref,
    edge_att_ref,
    mid_att_ref,
    edge_log_ref,
    mid_log_ref,
    payload_ref,
    out_ref,
    keys_ref,
    values_ref,
    query_ref,
    grad_ref,
    query_rows_ref,
    grad_rows_ref,
    turned_ref,
    total_ref,
):
    pad_rows = lax.broadcasted_iota(jnp.int32, (HD, FR), 0)
    ones = jnp.where(pad_rows < 3, 1.0, 0.0).astype(bf16)
    for source in range(HEADS):
        span = slice(FR * source, FR * (source + 1))
        key_block = qkv_ref[source, HD : 2 * HD, :]
        turned_ref[:, span] = key_block
        keys_ref[span, :] = jnp.concatenate([key_block, ones], axis=0).T
        values_ref[span, :] = jnp.concatenate([qkv_ref[source, 2 * HD : 3 * HD, :], ones], axis=0).T
        grads = payload_ref[source, PART_ROWS:, :]
        block, side = divmod(source, 2)
        if 0 < block < CHUNKS - 1:
            att, log, block = mid_att_ref, mid_log_ref, block - 1
        else:
            att, log, block = edge_att_ref, edge_log_ref, min(block, 1)
        lanes = slice(FR * side, FR * (side + 1))
        delta = jnp.sum(grads.astype(f32) * att[block, :, lanes].astype(f32), axis=0, keepdims=True)
        logs = log[block, 0:1, lanes] * (1.0 / (SCALE * LOG2E))
        for ref, rows_ref, body, row in (
            (query_ref, query_rows_ref, qkv_ref[source, 0:HD, :], logs),
            (grad_ref, grad_rows_ref, grads, delta),
        ):
            parts = three_parts(jnp.broadcast_to(-row, (HD, FR)))
            tail = jnp.zeros((HD, FR), f32)
            for place in range(3):
                tail = jnp.where(pad_rows == place, parts[place].astype(f32), tail)
            both = jnp.concatenate([body, tail.astype(bf16)], axis=0)
            ref[:, span] = both
            rows_ref[span, :] = both.T
    total_ref[...] = jnp.zeros_like(total_ref)

    def step(block, carry):
        rows = block_rows(block)
        keys, values, turned = keys_ref[rows, :], values_ref[rows, :], turned_ref[:, rows]

        def products(chunk):
            cols = block_rows(chunk)
            return dot(keys, query_ref[:, cols]), dot(values, grad_ref[:, cols])

        key_total = jnp.zeros((BLOCK, 128), f32)
        value_total = jnp.zeros((BLOCK, 128), f32)
        ready = products(0)
        for chunk in range(CHUNKS):
            cols = block_rows(chunk)
            scores, grad_probs = ready
            if chunk + 1 < CHUNKS:
                ready = products(chunk + 1)
            probs = jnp.exp2(scores * (SCALE * LOG2E))
            grad_scores = (probs * grad_probs).astype(bf16)
            value_total = value_total + dot(probs.astype(bf16), grad_rows_ref[cols, :])
            key_total = key_total + dot(grad_scores, query_rows_ref[cols, :])
            total_ref[:, cols] += dot(turned, grad_scores)
        for place, total in ((1, key_total * SCALE), (2, value_total)):
            turned_total = total.T[:HD].astype(bf16)
            out_ref[2 * block, HD * place : HD * (place + 1), :] = turned_total[:, :FR]
            out_ref[2 * block + 1, HD * place : HD * (place + 1), :] = turned_total[:, FR:]
        return carry

    lax.fori_loop(0, CHUNKS, step, 0)
    for source in range(HEADS):
        span = slice(FR * source, FR * (source + 1))
        out_ref[source, 0:HD, :] = (total_ref[:, span] * SCALE).astype(bf16)


def finish_kernel(parts_ref, payload_ref, out_ref):
    total = jnp.sum(parts_ref[...], axis=0).astype(bf16)
    out_ref[...] = jnp.broadcast_to(total[None], out_ref.shape)


def unpack_kernel(frame_total, back_ref, query_ref, key_ref, value_ref, taps_ref, affine_ref, moments_ref):
    for item, ref in enumerate((query_ref, key_ref, value_ref)):
        for pair in range(HEADS // 2):
            turned = back_ref[2 * pair : 2 * pair + 2, HD * item : HD * (item + 1), :].reshape(128, FR)
            ref[:, 128 * pair : 128 * (pair + 1)] = turned.T
    totals = [back_ref[source, 3 * HD :, :].astype(f32) for source in range(10)]

    def fetch(row, part):
        place = (row % 4) * 8 + part
        return totals[row // 4][place : place + 1]

    for part in range(8):
        cols = slice(128 * part, 128 * (part + 1))
        for row in range(KW):
            taps_ref[row : row + 1, cols] = fetch(row, part)
        for row in range(4):
            ref, factor = (affine_ref, 1.0) if row < 2 else (moments_ref, 1.0 / frame_total)
            total = fetch(KW + row, part) + fetch(KW + 4 + row, part)
            ref[row % 2 : row % 2 + 1, cols] = total * factor


def call(kernel, out_shape, *args, scratch=(), gflops=0, **extra):
    if gflops:
        extra["cost_estimate"] = pl.CostEstimate(
            flops=gflops * 10**9, bytes_accessed=4 * 2**20, transcendentals=STRETCH * STRETCH
        )
    return pl.pallas_call(
        kernel, out_shape=out_shape, scratch_shapes=list(scratch), compiler_params=params(), **extra
    )(*args)


def shape(dims, dtype):
    return jax.ShapeDtypeStruct(dims, dtype)


def in_high_memory(array):
    return pltpu.with_memory_space_constraint(array, pltpu.HBM)


def whole(*dims):
    return pl.BlockSpec(dims, lambda i: (0,) * len(dims))


def weight_chunk():
    place = lax.axis_index("tm")
    return (place // 8) * 2 + lax.rem(place, 2)


def gather_weights(rows):
    peers = [[8 * x + 2 * low + core for x in range(4) for core in range(2)] for low in range(4)]
    return lax.all_gather(rows, "tm", axis=0, axis_index_groups=peers)


def neighbours(axes, first, last):
    size = lax.axis_size(axes)
    up = [(i, i + 1) for i in range(size - 1)]
    down = [(i + 1, i) for i in range(size - 1)]
    return lax.ppermute(last, axes, up), lax.ppermute(first, axes, down)


def local(
    query_in,
    key_in,
    value_in,
    residual,
    layer_gain,
    proj_weight,
    conv_kernel,
    batch_gamma,
    batch_beta,
    stale_mean,
    stale_variance,
    grad_conv,
    grad_stream_in,
):
    groups = lax.axis_size("tm")
    frame_total = FR * groups * lax.axis_size("seq")
    gain = layer_gain.reshape(1, D)
    vectors = jnp.stack([batch_gamma, batch_beta, stale_mean, stale_variance])
    in_hbm = pl.BlockSpec(memory_space=pltpu.HBM)
    in_vmem = pl.BlockSpec(memory_space=pltpu.VMEM)

    edge_rows = EDGE + EDGE // 2
    block = pltpu.VMEM((FR, D), bf16)
    chunks = call(
        chunk_kernel,
        shape((HEADS, 128, 128), bf16),
        weight_chunk().reshape(1),
        in_high_memory(proj_weight),
        in_specs=[pl.BlockSpec(memory_space=pltpu.SMEM), in_hbm],
        scratch=(pltpu.VMEM((128, 128), bf16), pltpu.SemaphoreType.DMA(())),
    )
    weight_rows = lax.all_to_all(chunks, "seq", 0, 0, tiled=True)
    packed, first, last = call(
        pack_kernel,
        (shape((HEADS, 3 * HD, FR), bf16), shape((edge_rows, D), bf16), shape((edge_rows, D), bf16)),
        *map(in_high_memory, (query_in, key_in, value_in, residual, grad_conv)),
        in_specs=[in_hbm] * 5,
        scratch=(block, block, block, pltpu.SemaphoreType.DMA((7,))),
    )
    packed, weight_rows = lax.optimization_barrier((packed, weight_rows))
    weights = gather_weights(weight_rows)
    qkv = lax.all_to_all(packed, "seq", 0, 0, tiled=True)
    before, after = neighbours(("tm", "seq"), first, last)
    square = shape((STRETCH, 128), bf16)
    scores = [pltpu.VMEM((BLOCK, STRETCH), f32)] * 2
    keys, queries, values, edge_nat, edge_att, edge_log, first, last = call(
        edge_forward_kernel,
        (
            shape((128, STRETCH), bf16),
            square,
            square,
            shape((2 * BLOCK, 128), bf16),
            shape((2, HD, BLOCK), bf16),
            shape((2, 8, BLOCK), f32),
            shape((EDGE, 128), bf16),
            shape((EDGE, 128), bf16),
        ),
        qkv,
        scratch=scores,
    )
    edge_before, edge_after = neighbours("tm", first, last)
    mid_nat, mid_att, mid_log = call(
        middle_forward_kernel,
        (
            shape((STRETCH - 2 * BLOCK, 128), bf16),
            shape((CHUNKS - 2, HD, BLOCK), bf16),
            shape((CHUNKS - 2, 8, BLOCK), f32),
        ),
        keys,
        queries,
        values,
        scratch=scores,
        gflops=6,
    )
    att_payload = call(
        assemble_kernel,
        shape((HEADS, 64 + EDGE, 128), bf16),
        edge_nat,
        mid_nat,
        edge_before,
        edge_after,
    )
    att_payload, before, after = lax.optimization_barrier((att_payload, before, after))
    att_rows = lax.all_to_all(att_payload, "seq", 0, 0, tiled=True)
    grad_stream, payload = call(
        middle_kernel,
        (shape((FR, D), bf16), shape((HEADS, PART_ROWS + HD, FR), bf16)),
        att_rows,
        residual,
        before,
        after,
        gain,
        in_high_memory(weights),
        conv_kernel,
        vectors,
        grad_conv,
        grad_stream_in,
        in_specs=[in_vmem] * 5 + [in_hbm] + [in_vmem] * 4,
        scratch=(
            pltpu.VMEM((8, HEADS, 128, 128), bf16),
            pltpu.VMEM((ROWS, D), f32),
            pltpu.VMEM((ROWS, D), bf16),
            pltpu.VMEM((8, FR, 128), f32),
            pltpu.VMEM((8, FR, 128), f32),
            pltpu.VMEM((8, ROWS, 128), f32),
            pltpu.VMEM((WIDE, 128), f32),
            pltpu.VMEM((HEADS, PART_ROWS, 128), f32),
            pltpu.VMEM((FR, 2 * D), bf16),
            pltpu.VMEM((FR, D), f32),
            pltpu.SemaphoreType.DMA((HEADS,)),
        ),
    )
    payload = lax.all_to_all(payload, "seq", 0, 0, tiled=True)
    spread = call(
        spread_kernel,
        shape((groups, PART_ROWS, 128), f32),
        payload,
        grid=(1,),
        in_specs=[whole(HEADS, PART_ROWS, 128)],
        out_specs=whole(groups, PART_ROWS, 128),
    )
    totals = lax.all_to_all(spread, "tm", 0, 0, tiled=True)
    tall = pltpu.VMEM((STRETCH, 128), bf16)
    flat = pltpu.VMEM((128, STRETCH), bf16)
    back = call(
        backward_kernel,
        shape((HEADS, 3 * HD + PART_ROWS, FR), bf16),
        qkv,
        edge_att,
        mid_att,
        edge_log,
        mid_log,
        payload,
        gflops=12,
        scratch=(
            tall,
            tall,
            flat,
            flat,
            tall,
            tall,
            pltpu.VMEM((HD, STRETCH), bf16),
            pltpu.VMEM((HD, STRETCH), f32),
        ),
    )
    back = call(
        finish_kernel,
        shape(back.shape, bf16),
        totals,
        back,
        grid=(1,),
        in_specs=[whole(groups, PART_ROWS, 128), pl.BlockSpec(memory_space=pl.ANY)],
        out_specs=pl.BlockSpec((HEADS, PART_ROWS, 128), lambda i: (0, 6, 0)),
        input_output_aliases={1: 0},
    )
    back = lax.all_to_all(back, "seq", 0, 0, tiled=True)
    narrow = shape((FR, D), bf16)
    query_grad, key_grad, value_grad, kernel_sum, affine_sum, moments = call(
        lambda *refs: unpack_kernel(frame_total, *refs),
        (narrow, narrow, narrow, shape((KW, D), f32), shape((2, D), f32), shape((2, D), f32)),
        back,
    )
    return (query_grad, key_grad, value_grad, grad_stream, kernel_sum, affine_sum, moments)


def solution(mesh):
    rows = P(("tm", "seq"), None)
    in_specs = (rows, rows, rows, rows, P(), P(None, "seq"), P(), P(), P(), P(), P(), rows, rows)
    out_specs = (rows, rows, rows, rows, P(), P(), P())
    return jax.shard_map(local, mesh=mesh, in_specs=in_specs, out_specs=out_specs, check_vma=False)
```

```python
import math

import jax
import jax.numpy as jnp
from jax import lax
from jax.experimental import pallas as pl
from jax.experimental.pallas import tpu as pltpu
from jax.sharding import PartitionSpec as P

HEADS = 16
HD = 64
D = 1024
FR = 128
KW = 31
HALF = KW // 2
STRETCH = FR * HEADS
epsilon = 1e-05
LOG2E = math.log2(math.e)
SCALE = HD ** (-0.5)
BLOCK = 256
PART_ROWS = 32
EDGE = 32
ROWS = FR + 2 * EDGE
WIDE = FR + EDGE

f32 = jnp.float32
bf16 = jnp.bfloat16
NT = (((1,), (1,)), ((), ()))


def params(megabytes=48):
    return pltpu.CompilerParams(vmem_limit_bytes=megabytes * 1024 * 1024)


def dot(left, right):
    return jnp.dot(left, right, preferred_element_type=f32)


def dot_nt(left, right):
    return lax.dot_general(left, right, NT, preferred_element_type=f32)


def two_parts(value):
    high = value.astype(bf16)
    low = (value - high.astype(f32)).astype(bf16)
    return high, low


def three_parts(value):
    high = value.astype(bf16)
    rest = value - high.astype(f32)
    mid = rest.astype(bf16)
    low = (rest - mid.astype(f32)).astype(bf16)
    return high, mid, low


def rows_kernel(res_hbm, grad_hbm, first_ref, last_ref, copy_sem):
    pairs = (
        (res_hbm.at[0:EDGE], first_ref.at[0:EDGE]),
        (res_hbm.at[FR - EDGE : FR], last_ref.at[0:EDGE]),
        (grad_hbm.at[0:16], first_ref.at[EDGE : EDGE + 16]),
        (grad_hbm.at[FR - 16 : FR], last_ref.at[EDGE : EDGE + 16]),
    )
    copies = [pltpu.make_async_copy(src, dst, copy_sem.at[i]) for i, (src, dst) in enumerate(pairs)]
    for copy in copies:
        copy.start()
    for copy in copies:
        copy.wait()


def pack_kernel(
    chunk_ref,
    query_hbm,
    key_hbm,
    value_hbm,
    weight_hbm,
    out_ref,
    query_ref,
    key_ref,
    value_ref,
    weight_ref,
    copy_sem,
):
    weight_rows = weight_hbm.at[pl.ds(pl.multiple_of(chunk_ref[0] * 128, 128), 128)]
    pairs = ((query_hbm, query_ref), (key_hbm, key_ref), (value_hbm, value_ref), (weight_rows, weight_ref))
    copies = [pltpu.make_async_copy(src, dst, copy_sem.at[i]) for i, (src, dst) in enumerate(pairs)]
    for copy in copies:
        copy.start()
    for item, ref in enumerate((query_ref, key_ref, value_ref)):
        copies[item].wait()
        for pair in range(HEADS // 2):
            turned = ref[:, 128 * pair : 128 * (pair + 1)].T
            out_ref[2 * pair, HD * item : HD * (item + 1), :] = turned[:HD]
            out_ref[2 * pair + 1, HD * item : HD * (item + 1), :] = turned[HD:]
    copies[3].wait()
    for dest in range(HEADS):
        out_ref[dest, 3 * HD :, :] = weight_ref[...]


CHUNKS = STRETCH // BLOCK


def block_rows(block):
    if isinstance(block, int):
        return slice(block * BLOCK, (block + 1) * BLOCK)
    return pl.ds(pl.multiple_of(block * BLOCK, BLOCK), BLOCK)


def low_lanes(rows):
    return lax.broadcasted_iota(jnp.int32, (rows, 128), 1) < HD


def soft_stage(keys_ref, query_ref, value_ref, following, current):
    queries = peak = total = None
    if following is not None:
        block, next_ref = following
        queries = query_ref[block_rows(block), :]
    for chunk in range(CHUNKS):
        rows = slice(BLOCK * chunk, BLOCK * (chunk + 1))
        if following is not None:
            part = dot(queries, keys_ref[:, rows])
            next_ref[:, rows] = part
            part = jnp.maximum(part[:, :128], part[:, 128:])
            peak = part if peak is None else jnp.maximum(peak, part)
        if current is not None:
            score_ref, top = current
            weights = jnp.exp2(score_ref[:, rows] - jnp.concatenate([top, top], axis=1)).astype(bf16)
            part = dot(weights, value_ref[rows, :])
            total = part if total is None else total + part
    if peak is not None:
        peak = jnp.broadcast_to(jnp.max(peak, axis=1, keepdims=True), (BLOCK, 128))
    return peak, total


def store_attended(total, peak, nat_ref, rows, turned_ref, log_ref, place):
    norm = jnp.broadcast_to(total[:, HD : HD + 1], (BLOCK, 128))
    attended = (total / norm).astype(bf16).astype(f32)
    low = low_lanes(BLOCK)
    nat_ref[rows, :] = jnp.where(low, attended, pltpu.roll(attended, HD, 1)).astype(bf16)
    turned = jnp.where(low, attended, peak + jnp.log2(norm)).T
    turned_ref[place] = turned[:HD].astype(bf16)
    log_ref[place] = turned[HD : HD + 8]


def edge_forward_kernel(
    qkv_ref,
    keys_ref,
    query_ref,
    value_ref,
    nat_ref,
    turned_ref,
    log_ref,
    first_ref,
    last_ref,
    score_ref,
    other_ref,
):
    pad_rows = lax.broadcasted_iota(jnp.int32, (HD, FR), 0)
    ones = jnp.where(pad_rows == 0, 1.0, 0.0).astype(bf16)
    for source in range(HEADS):
        span = slice(FR * source, FR * (source + 1))
        key_block = qkv_ref[source, HD : 2 * HD, :]
        keys_ref[0:HD, span] = key_block
        keys_ref[HD : 2 * HD, span] = key_block
        high, low = two_parts(qkv_ref[source, 0:HD, :].astype(f32) * (SCALE * LOG2E))
        query_ref[span, :] = jnp.concatenate([high, low], axis=0).T
        value_ref[span, :] = jnp.concatenate([qkv_ref[source, 2 * HD : 3 * HD, :], ones], axis=0).T
    stage = lambda *pair: soft_stage(keys_ref, query_ref, value_ref, *pair)
    top, _ = stage((0, score_ref), None)
    final_top, total = stage((CHUNKS - 1, other_ref), (score_ref, top))
    store_attended(total, top, nat_ref, slice(0, BLOCK), turned_ref, log_ref, 0)
    _, total = stage(None, (other_ref, final_top))
    store_attended(total, final_top, nat_ref, slice(BLOCK, 2 * BLOCK), turned_ref, log_ref, 1)
    first_ref[...] = nat_ref[0:EDGE, :]
    last_ref[...] = nat_ref[2 * BLOCK - EDGE : 2 * BLOCK, :]


def middle_forward_kernel(
    keys_ref, query_ref, value_ref, nat_ref, turned_ref, log_ref, score_ref, other_ref
):
    stage = lambda *pair: soft_stage(keys_ref, query_ref, value_ref, *pair)

    def store(total, top, place):
        store_attended(total, top, nat_ref, block_rows(place), turned_ref, log_ref, place)

    def two(index, top):
        place = 2 * index
        next_top, total = stage((place + 2, other_ref), (score_ref, top))
        store(total, top, place)
        last_top, total = stage((place + 3, score_ref), (other_ref, next_top))
        store(total, next_top, place + 1)
        return last_top

    top, _ = stage((1, score_ref), None)
    top = lax.fori_loop(0, 2, two, top)
    next_top, total = stage((6, other_ref), (score_ref, top))
    store(total, top, 4)
    _, total = stage(None, (other_ref, next_top))
    store(total, next_top, 5)


def assemble_kernel(edge_ref, middle_ref, before_ref, after_ref, out_ref):
    def frames(begin, count):
        if begin < 0:
            return before_ref[...]
        if begin >= STRETCH:
            return after_ref[...]
        if begin < BLOCK:
            return edge_ref[begin : begin + count, :]
        if begin < STRETCH - BLOCK:
            return middle_ref[begin - BLOCK : begin - BLOCK + count, :]
        begin -= STRETCH - 2 * BLOCK
        return edge_ref[begin : begin + count, :]

    for dest in range(HEADS):
        begin = FR * dest
        low = low_lanes(64)
        out_ref[dest, 0:64, :] = jnp.where(
            low, frames(begin, 64).astype(f32), frames(begin + 64, 64).astype(f32)
        ).astype(bf16)
        low = low_lanes(EDGE)
        out_ref[dest, 64 : 64 + EDGE, :] = jnp.where(
            low, frames(begin - EDGE, EDGE).astype(f32), frames(begin + FR, EDGE).astype(f32)
        ).astype(bf16)


def middle_kernel(
    att_ref,
    residual_ref,
    before_ref,
    after_ref,
    gain_ref,
    weight_hbm,
    taps_ref,
    vec_ref,
    grad_ref,
    skip_ref,
    stream_ref,
    payload_ref,
    weight_ref,
    normed_ref,
    low_ref,
    linear_ref,
    gate_ref,
    glu_ref,
    grad_ext_ref,
    sums_ref,
    proj_ref,
    hat_ref,
    copy_sem,
):
    def fetch(column):
        return pltpu.make_async_copy(weight_hbm.at[:, column], weight_ref.at[:, column], copy_sem.at[column])

    for part in range(8):
        fetch(part).start()
        fetch(part + 8).start()
    lanes = low_lanes(64 + EDGE)
    for pair in range(HEADS // 2):
        cols = slice(128 * pair, 128 * (pair + 1))
        even = att_ref[2 * pair].astype(f32)
        odd = att_ref[2 * pair + 1].astype(f32)
        low = jnp.where(lanes, even, pltpu.roll(odd, HD, 1))
        high = jnp.where(lanes, pltpu.roll(even, HD, 1), odd)
        normed_ref[0:EDGE, cols] = low[64:] + before_ref[0:EDGE, cols].astype(f32)
        normed_ref[EDGE : EDGE + 64, cols] = low[:64] + residual_ref[0:64, cols].astype(f32)
        normed_ref[EDGE + 64 : EDGE + FR, cols] = high[:64] + residual_ref[64:FR, cols].astype(f32)
        normed_ref[EDGE + FR :, cols] = high[64:] + after_ref[0:EDGE, cols].astype(f32)
    stream = normed_ref[...]
    centred = stream - jnp.mean(stream, axis=1, keepdims=True)
    inv_std = lax.rsqrt(jnp.mean(centred * centred, axis=1, keepdims=True) + epsilon)
    normed = centred * inv_std
    normed_ref[...] = normed
    inv_own = inv_std[EDGE : EDGE + FR]
    low_ref[...] = (normed * gain_ref[...]).astype(bf16)
    sums_ref[...] = jnp.zeros_like(sums_ref)
    for part in range(8):
        fetch(part).wait()
        fetch(part + 8).wait()
        weights = jnp.concatenate(
            [weight_ref[:, part].reshape(D, 128), weight_ref[:, part + 8].reshape(D, 128)], axis=1
        )
        projected = dot(low_ref[...], weights)
        linear = projected[:, :128]
        gate = jax.nn.sigmoid(projected[:, 128:])
        linear_ref[part] = linear[EDGE : EDGE + FR]
        gate_ref[part] = gate[EDGE : EDGE + FR]
        glu_ref[part] = (linear * gate).astype(bf16).astype(f32)
    for part in range(8):
        cols = slice(128 * part, 128 * (part + 1))

        def put(row, total):
            place = (row % 4) * 8 + part
            sums_ref[row // 4, place : place + 1, :] = total

        conv = jnp.zeros((WIDE, 128), f32)
        for tap in range(KW):
            conv = conv + taps_ref[tap : tap + 1, cols] * glu_ref[part, tap + 1 : tap + 1 + WIDE, :]
        gamma = vec_ref[0:1, cols]
        inv_scale = lax.rsqrt(vec_ref[3:4, cols] + epsilon)
        zhat = (conv - vec_ref[2:3, cols]) * inv_scale
        shifted = gamma * zhat + vec_ref[1:2, cols]
        sig = jax.nn.sigmoid(shifted)
        grads = jnp.concatenate(
            [before_ref[EDGE:, cols], grad_ref[:, cols], after_ref[EDGE:, cols]], axis=0
        ).astype(f32)
        grad_shift = grads * sig * (1.0 + shifted * (1.0 - sig))
        grad_ext_ref[...] = (grad_shift * (gamma * inv_scale)).astype(bf16).astype(f32)
        own = slice(EDGE // 2, EDGE // 2 + FR)
        conv, zhat, grad_shift = conv[own], zhat[own], grad_shift[own]
        for row, value in enumerate((grad_shift * zhat, grad_shift, conv, conv * conv)):
            total = jnp.sum(value, axis=0, keepdims=True)
            put(KW + row, total)
            put(KW + 4 + row, total - total.astype(bf16).astype(f32))
        grad_own = grad_ext_ref[own, :]
        for tap in range(KW):
            begin = EDGE + tap - HALF
            put(tap, jnp.sum(grad_own * glu_ref[part, begin : begin + FR, :], axis=0, keepdims=True))
        grad_glu = jnp.zeros((FR, 128), f32)
        for tap in range(KW):
            begin = EDGE // 2 + HALF - tap
            grad_glu = grad_glu + taps_ref[tap : tap + 1, cols] * grad_ext_ref[begin : begin + FR, :]
        gate = gate_ref[part]
        half = grad_glu * gate
        proj_ref[:, cols] = half.astype(bf16)
        proj_ref[:, D + 128 * part : D + 128 * (part + 1)] = (half * linear_ref[part] * (1.0 - gate)).astype(bf16)
    payload_ref[:, 0:PART_ROWS, :] = sums_ref[...].astype(bf16)
    proj = proj_ref[...]
    for part in range(4):
        cols = slice(256 * part, 256 * (part + 1))
        columns = [weight_ref[2 * part : 2 * (part + 1), s].reshape(256, 128) for s in range(16)]
        hat_ref[:, cols] = dot_nt(proj, jnp.concatenate(columns, axis=1)) * gain_ref[:, cols]
    hat = hat_ref[...]
    normed = normed_ref[EDGE : EDGE + FR, :]
    mean = jnp.mean(hat, axis=1, keepdims=True)
    mean_normed = jnp.mean(hat * normed, axis=1, keepdims=True)
    centre = inv_own * (hat - mean - normed * mean_normed)
    stream = (centre + skip_ref[...].astype(f32)).astype(bf16)
    stream_ref[...] = stream
    for pair in range(HEADS // 2):
        turned = stream[:, 128 * pair : 128 * (pair + 1)].T
        payload_ref[2 * pair, PART_ROWS:, :] = turned[:HD]
        payload_ref[2 * pair + 1, PART_ROWS:, :] = turned[HD:]


def spread_kernel(payload_ref, out_ref):
    total = jnp.sum(payload_ref[...].astype(f32), axis=0).astype(bf16)
    out_ref[...] = jnp.broadcast_to(total[None], out_ref.shape)


def backward_kernel(
    qkv_ref,
    edge_att_ref,
    mid_att_ref,
    edge_log_ref,
    mid_log_ref,
    payload_ref,
    out_ref,
    keys_ref,
    values_ref,
    query_ref,
    grad_ref,
    query_rows_ref,
    grad_rows_ref,
    turned_ref,
    total_ref,
):
    pad_rows = lax.broadcasted_iota(jnp.int32, (HD, FR), 0)
    ones = jnp.where(pad_rows < 3, 1.0, 0.0).astype(bf16)
    for source in range(HEADS):
        span = slice(FR * source, FR * (source + 1))
        key_block = qkv_ref[source, HD : 2 * HD, :]
        turned_ref[:, span] = key_block
        keys_ref[span, :] = jnp.concatenate([key_block, ones], axis=0).T
        values_ref[span, :] = jnp.concatenate([qkv_ref[source, 2 * HD : 3 * HD, :], ones], axis=0).T
        grads = payload_ref[source, PART_ROWS:, :]
        block, side = divmod(source, 2)
        if 0 < block < CHUNKS - 1:
            att, log, block = mid_att_ref, mid_log_ref, block - 1
        else:
            att, log, block = edge_att_ref, edge_log_ref, min(block, 1)
        lanes = slice(FR * side, FR * (side + 1))
        delta = jnp.sum(grads.astype(f32) * att[block, :, lanes].astype(f32), axis=0, keepdims=True)
        logs = log[block, 0:1, lanes] * (1.0 / (SCALE * LOG2E))
        for ref, rows_ref, body, row in (
            (query_ref, query_rows_ref, qkv_ref[source, 0:HD, :], logs),
            (grad_ref, grad_rows_ref, grads, delta),
        ):
            parts = three_parts(jnp.broadcast_to(-row, (HD, FR)))
            tail = jnp.zeros((HD, FR), f32)
            for place in range(3):
                tail = jnp.where(pad_rows == place, parts[place].astype(f32), tail)
            both = jnp.concatenate([body, tail.astype(bf16)], axis=0)
            ref[:, span] = both
            rows_ref[span, :] = both.T
    total_ref[...] = jnp.zeros_like(total_ref)

    def step(block, carry):
        rows = block_rows(block)
        keys, values, turned = keys_ref[rows, :], values_ref[rows, :], turned_ref[:, rows]

        def products(chunk):
            cols = block_rows(chunk)
            return dot(keys, query_ref[:, cols]), dot(values, grad_ref[:, cols])

        key_total = jnp.zeros((BLOCK, 128), f32)
        value_total = jnp.zeros((BLOCK, 128), f32)
        ready = products(0)
        for chunk in range(CHUNKS):
            cols = block_rows(chunk)
            scores, grad_probs = ready
            if chunk + 1 < CHUNKS:
                ready = products(chunk + 1)
            probs = jnp.exp2(scores * (SCALE * LOG2E))
            grad_scores = (probs * grad_probs).astype(bf16)
            value_total = value_total + dot(probs.astype(bf16), grad_rows_ref[cols, :])
            key_total = key_total + dot(grad_scores, query_rows_ref[cols, :])
            total_ref[:, cols] += dot(turned, grad_scores)
        for place, total in ((1, key_total * SCALE), (2, value_total)):
            turned_total = total.T[:HD].astype(bf16)
            out_ref[2 * block, HD * place : HD * (place + 1), :] = turned_total[:, :FR]
            out_ref[2 * block + 1, HD * place : HD * (place + 1), :] = turned_total[:, FR:]
        return carry

    lax.fori_loop(0, CHUNKS, step, 0)
    for source in range(HEADS):
        span = slice(FR * source, FR * (source + 1))
        out_ref[source, 0:HD, :] = (total_ref[:, span] * SCALE).astype(bf16)


def finish_kernel(parts_ref, payload_ref, out_ref):
    total = jnp.sum(parts_ref[...].astype(f32), axis=0).astype(bf16)
    out_ref[...] = jnp.broadcast_to(total[None], out_ref.shape)


def unpack_kernel(frame_total, back_ref, query_ref, key_ref, value_ref, taps_ref, affine_ref, moments_ref):
    for item, ref in enumerate((query_ref, key_ref, value_ref)):
        for pair in range(HEADS // 2):
            turned = back_ref[2 * pair : 2 * pair + 2, HD * item : HD * (item + 1), :].reshape(128, FR)
            ref[:, 128 * pair : 128 * (pair + 1)] = turned.T
    totals = [back_ref[source, 3 * HD :, :].astype(f32) for source in range(10)]

    def fetch(row, part):
        place = (row % 4) * 8 + part
        return totals[row // 4][place : place + 1]

    for part in range(8):
        cols = slice(128 * part, 128 * (part + 1))
        for row in range(KW):
            taps_ref[row : row + 1, cols] = fetch(row, part)
        for row in range(4):
            ref, factor = (affine_ref, 1.0) if row < 2 else (moments_ref, 1.0 / frame_total)
            total = fetch(KW + row, part) + fetch(KW + 4 + row, part)
            ref[row % 2 : row % 2 + 1, cols] = total * factor


def call(kernel, out_shape, *args, scratch=(), gflops=0, **extra):
    if gflops:
        extra["cost_estimate"] = pl.CostEstimate(
            flops=gflops * 10**9, bytes_accessed=4 * 2**20, transcendentals=STRETCH * STRETCH
        )
    return pl.pallas_call(
        kernel, out_shape=out_shape, scratch_shapes=list(scratch), compiler_params=params(), **extra
    )(*args)


def shape(dims, dtype):
    return jax.ShapeDtypeStruct(dims, dtype)


def in_high_memory(array):
    return pltpu.with_memory_space_constraint(array, pltpu.HBM)


def whole(*dims):
    return pl.BlockSpec(dims, lambda i: (0,) * len(dims))


def weight_chunk():
    place = lax.axis_index("tm")
    return (place // 8) * 2 + lax.rem(place, 2)


def gather_weights(rows):
    peers = [[8 * x + 2 * low + core for x in range(4) for core in range(2)] for low in range(4)]
    return lax.all_gather(rows, "tm", axis=0, axis_index_groups=peers)


def neighbours(axes, first, last):
    size = lax.axis_size(axes)
    up = [(i, i + 1) for i in range(size - 1)]
    down = [(i + 1, i) for i in range(size - 1)]
    return lax.ppermute(last, axes, up), lax.ppermute(first, axes, down)


def local(
    query_in,
    key_in,
    value_in,
    residual,
    layer_gain,
    proj_weight,
    conv_kernel,
    batch_gamma,
    batch_beta,
    stale_mean,
    stale_variance,
    grad_conv,
    grad_stream_in,
):
    groups = lax.axis_size("tm")
    frame_total = FR * groups * lax.axis_size("seq")
    gain = layer_gain.reshape(1, D)
    vectors = jnp.stack([batch_gamma, batch_beta, stale_mean, stale_variance])
    in_hbm = pl.BlockSpec(memory_space=pltpu.HBM)
    in_vmem = pl.BlockSpec(memory_space=pltpu.VMEM)

    edge_rows = EDGE + EDGE // 2
    block = pltpu.VMEM((FR, D), bf16)
    first, last = call(
        rows_kernel,
        (shape((edge_rows, D), bf16), shape((edge_rows, D), bf16)),
        in_high_memory(residual),
        in_high_memory(grad_conv),
        in_specs=[in_hbm] * 2,
        scratch=(pltpu.SemaphoreType.DMA((4,)),),
    )
    before, after = neighbours(("tm", "seq"), first, last)
    packed = call(
        pack_kernel,
        shape((HEADS, 3 * HD + 128, FR), bf16),
        weight_chunk().reshape(1),
        *map(in_high_memory, (query_in, key_in, value_in, proj_weight)),
        in_specs=[pl.BlockSpec(memory_space=pltpu.SMEM)] + [in_hbm] * 4,
        scratch=(block, block, block, pltpu.VMEM((128, 128), bf16), pltpu.SemaphoreType.DMA((4,))),
    )
    packed, before, after = lax.optimization_barrier((packed, before, after))
    qkv = lax.all_to_all(packed, "seq", 0, 0, tiled=True)
    weights = gather_weights(qkv[:, 3 * HD :])
    square = shape((STRETCH, 128), bf16)
    scores = [pltpu.VMEM((BLOCK, STRETCH), f32)] * 2
    keys, queries, values, edge_nat, edge_att, edge_log, first, last = call(
        edge_forward_kernel,
        (
            shape((128, STRETCH), bf16),
            square,
            square,
            shape((2 * BLOCK, 128), bf16),
            shape((2, HD, BLOCK), bf16),
            shape((2, 8, BLOCK), f32),
            shape((EDGE, 128), bf16),
            shape((EDGE, 128), bf16),
        ),
        qkv,
        scratch=scores,
    )
    edge_before, edge_after = neighbours("tm", first, last)
    mid_nat, mid_att, mid_log = call(
        middle_forward_kernel,
        (
            shape((STRETCH - 2 * BLOCK, 128), bf16),
            shape((CHUNKS - 2, HD, BLOCK), bf16),
            shape((CHUNKS - 2, 8, BLOCK), f32),
        ),
        keys,
        queries,
        values,
        scratch=scores,
        gflops=6,
    )
    att_payload = call(
        assemble_kernel,
        shape((HEADS, 64 + EDGE, 128), bf16),
        edge_nat,
        mid_nat,
        edge_before,
        edge_after,
    )
    att_rows = lax.all_to_all(att_payload, "seq", 0, 0, tiled=True)
    grad_stream, payload = call(
        middle_kernel,
        (shape((FR, D), bf16), shape((HEADS, PART_ROWS + HD, FR), bf16)),
        att_rows,
        residual,
        before,
        after,
        gain,
        in_high_memory(weights),
        conv_kernel,
        vectors,
        grad_conv,
        grad_stream_in,
        in_specs=[in_vmem] * 5 + [in_hbm] + [in_vmem] * 4,
        scratch=(
            pltpu.VMEM((8, HEADS, 128, 128), bf16),
            pltpu.VMEM((ROWS, D), f32),
            pltpu.VMEM((ROWS, D), bf16),
            pltpu.VMEM((8, FR, 128), f32),
            pltpu.VMEM((8, FR, 128), f32),
            pltpu.VMEM((8, ROWS, 128), f32),
            pltpu.VMEM((WIDE, 128), f32),
            pltpu.VMEM((HEADS, PART_ROWS, 128), f32),
            pltpu.VMEM((FR, 2 * D), bf16),
            pltpu.VMEM((FR, D), f32),
            pltpu.SemaphoreType.DMA((HEADS,)),
        ),
    )
    payload = lax.all_to_all(payload, "seq", 0, 0, tiled=True)
    spread = call(
        spread_kernel,
        shape((groups, PART_ROWS, 128), bf16),
        payload,
        grid=(1,),
        in_specs=[whole(HEADS, PART_ROWS, 128)],
        out_specs=whole(groups, PART_ROWS, 128),
    )
    totals = lax.all_to_all(spread, "tm", 0, 0, tiled=True)
    tall = pltpu.VMEM((STRETCH, 128), bf16)
    flat = pltpu.VMEM((128, STRETCH), bf16)
    back = call(
        backward_kernel,
        shape((HEADS, 3 * HD + PART_ROWS, FR), bf16),
        qkv,
        edge_att,
        mid_att,
        edge_log,
        mid_log,
        payload,
        gflops=12,
        scratch=(
            tall,
            tall,
            flat,
            flat,
            tall,
            tall,
            pltpu.VMEM((HD, STRETCH), bf16),
            pltpu.VMEM((HD, STRETCH), f32),
        ),
    )
    back = call(
        finish_kernel,
        shape(back.shape, bf16),
        totals,
        back,
        grid=(1,),
        in_specs=[whole(groups, PART_ROWS, 128), pl.BlockSpec(memory_space=pl.ANY)],
        out_specs=pl.BlockSpec((HEADS, PART_ROWS, 128), lambda i: (0, 6, 0)),
        input_output_aliases={1: 0},
    )
    back = lax.all_to_all(back, "seq", 0, 0, tiled=True)
    narrow = shape((FR, D), bf16)
    query_grad, key_grad, value_grad, kernel_sum, affine_sum, moments = call(
        lambda *refs: unpack_kernel(frame_total, *refs),
        (narrow, narrow, narrow, shape((KW, D), f32), shape((2, D), f32), shape((2, D), f32)),
        back,
    )
    return (query_grad, key_grad, value_grad, grad_stream, kernel_sum, affine_sum, moments)


def solution(mesh):
    rows = P(("tm", "seq"), None)
    in_specs = (rows, rows, rows, rows, P(), P(None, "seq"), P(), P(), P(), P(), P(), rows, rows)
    out_specs = (rows, rows, rows, rows, P(), P(), P())
    return jax.shard_map(local, mesh=mesh, in_specs=in_specs, out_specs=out_specs, check_vma=False)
```

```python
import math

import jax
import jax.numpy as jnp
from jax import lax
from jax.experimental import pallas as pl
from jax.experimental.pallas import tpu as pltpu
from jax.sharding import PartitionSpec as P

HEADS = 16
HD = 64
D = 1024
FR = 128
KW = 31
HALF = KW // 2
STRETCH = FR * HEADS
epsilon = 1e-05
LOG2E = math.log2(math.e)
SCALE = HD ** (-0.5)
BLOCK = 256
TALL = 512
PART_ROWS = 32
EDGE = 32
ROWS = FR + 2 * EDGE
WIDE = FR + EDGE

f32 = jnp.float32
bf16 = jnp.bfloat16
NT = (((1,), (1,)), ((), ()))


def params(megabytes=48):
    return pltpu.CompilerParams(vmem_limit_bytes=megabytes * 1024 * 1024)


def dot(left, right):
    return jnp.dot(left, right, preferred_element_type=f32)


def dot_nt(left, right):
    return lax.dot_general(left, right, NT, preferred_element_type=f32)


def two_parts(value):
    high = value.astype(bf16)
    low = (value - high.astype(f32)).astype(bf16)
    return high, low


def three_parts(value):
    high = value.astype(bf16)
    rest = value - high.astype(f32)
    mid = rest.astype(bf16)
    low = (rest - mid.astype(f32)).astype(bf16)
    return high, mid, low


def row_copies(res_hbm, grad_hbm, first_ref, last_ref, copy_sem):
    pairs = (
        (res_hbm.at[0:EDGE], first_ref.at[0:EDGE]),
        (res_hbm.at[FR - EDGE : FR], last_ref.at[0:EDGE]),
        (grad_hbm.at[0:16], first_ref.at[EDGE : EDGE + 16]),
        (grad_hbm.at[FR - 16 : FR], last_ref.at[EDGE : EDGE + 16]),
    )
    return [pltpu.make_async_copy(src, dst, copy_sem.at[i]) for i, (src, dst) in enumerate(pairs)]


def pack_kernel(
    chunk_ref,
    query_hbm,
    key_hbm,
    value_hbm,
    weight_hbm,
    out_ref,
    query_ref,
    key_ref,
    value_ref,
    weight_ref,
    copy_sem,
):
    weight_rows = weight_hbm.at[pl.ds(pl.multiple_of(chunk_ref[0] * 128, 128), 128)]
    pairs = ((query_hbm, query_ref), (key_hbm, key_ref), (value_hbm, value_ref), (weight_rows, weight_ref))
    copies = [pltpu.make_async_copy(src, dst, copy_sem.at[i]) for i, (src, dst) in enumerate(pairs)]
    for copy in copies:
        copy.start()
    for item, ref in enumerate((query_ref, key_ref, value_ref)):
        copies[item].wait()
        for pair in range(HEADS // 2):
            turned = ref[:, 128 * pair : 128 * (pair + 1)].T
            out_ref[2 * pair, HD * item : HD * (item + 1), :] = turned[:HD]
            out_ref[2 * pair + 1, HD * item : HD * (item + 1), :] = turned[HD:]
    copies[3].wait()
    for dest in range(HEADS):
        out_ref[dest, 3 * HD :, :] = weight_ref[...]


CHUNKS = STRETCH // BLOCK


TALLS = STRETCH // TALL
PER_TALL = TALL // FR


def block_rows(block, size=BLOCK):
    if isinstance(block, int):
        return slice(block * size, (block + 1) * size)
    return pl.ds(pl.multiple_of(block * size, size), size)


def low_lanes(rows):
    return lax.broadcasted_iota(jnp.int32, (rows, 128), 1) < HD


def soft_stage(keys_ref, query_ref, value_ref, following, current):
    queries = peak = total = None
    if following is not None:
        block, next_ref = following
        queries = query_ref[block_rows(block, TALL), :]
    for chunk in range(CHUNKS):
        rows = slice(BLOCK * chunk, BLOCK * (chunk + 1))
        if following is not None:
            part = dot(queries, keys_ref[:, rows])
            next_ref[:, rows] = part
            part = jnp.maximum(part[:, :128], part[:, 128:])
            peak = part if peak is None else jnp.maximum(peak, part)
        if current is not None:
            score_ref, top = current
            weights = jnp.exp2(score_ref[:, rows] - jnp.concatenate([top, top], axis=1)).astype(bf16)
            part = dot(weights, value_ref[rows, :])
            total = part if total is None else total + part
    if peak is not None:
        peak = jnp.broadcast_to(jnp.max(peak, axis=1, keepdims=True), (TALL, 128))
    return peak, total


def store_attended(total, peak, nat_ref, rows, turned_ref, log_ref, place):
    norm = jnp.broadcast_to(total[:, HD : HD + 1], (TALL, 128))
    attended = (total / norm).astype(bf16).astype(f32)
    low = low_lanes(TALL)
    nat_ref[rows, :] = jnp.where(low, attended, pltpu.roll(attended, HD, 1)).astype(bf16)
    turned = jnp.where(low, attended, peak + jnp.log2(norm)).T
    turned_ref[place] = turned[:HD].astype(bf16)
    log_ref[place] = turned[HD : HD + 8]


def edge_forward_kernel(
    qkv_ref,
    res_hbm,
    grad_hbm,
    keys_ref,
    query_ref,
    value_ref,
    nat_ref,
    turned_ref,
    log_ref,
    first_ref,
    last_ref,
    row_first_ref,
    row_last_ref,
    score_ref,
    other_ref,
    copy_sem,
):
    copies = row_copies(res_hbm, grad_hbm, row_first_ref, row_last_ref, copy_sem)
    for copy in copies:
        copy.start()
    pad_rows = lax.broadcasted_iota(jnp.int32, (HD, FR), 0)
    ones = jnp.where(pad_rows == 0, 1.0, 0.0).astype(bf16)
    for source in range(HEADS):
        span = slice(FR * source, FR * (source + 1))
        key_block = qkv_ref[source, HD : 2 * HD, :]
        keys_ref[0:HD, span] = key_block
        keys_ref[HD : 2 * HD, span] = key_block
        high, low = two_parts(qkv_ref[source, 0:HD, :].astype(f32) * (SCALE * LOG2E))
        query_ref[span, :] = jnp.concatenate([high, low], axis=0).T
        value_ref[span, :] = jnp.concatenate([qkv_ref[source, 2 * HD : 3 * HD, :], ones], axis=0).T
    stage = lambda *pair: soft_stage(keys_ref, query_ref, value_ref, *pair)
    top, _ = stage((0, score_ref), None)
    final_top, total = stage((TALLS - 1, other_ref), (score_ref, top))
    store_attended(total, top, nat_ref, slice(0, TALL), turned_ref, log_ref, 0)
    _, total = stage(None, (other_ref, final_top))
    store_attended(total, final_top, nat_ref, slice(TALL, 2 * TALL), turned_ref, log_ref, 1)
    first_ref[...] = nat_ref[0:EDGE, :]
    last_ref[...] = nat_ref[2 * TALL - EDGE : 2 * TALL, :]
    for copy in copies:
        copy.wait()


def middle_forward_kernel(
    keys_ref, query_ref, value_ref, nat_ref, turned_ref, log_ref, score_ref, other_ref
):
    stage = lambda *pair: soft_stage(keys_ref, query_ref, value_ref, *pair)

    top, _ = stage((1, score_ref), None)
    next_top, total = stage((2, other_ref), (score_ref, top))
    store_attended(total, top, nat_ref, slice(0, TALL), turned_ref, log_ref, 0)
    _, total = stage(None, (other_ref, next_top))
    store_attended(total, next_top, nat_ref, slice(TALL, 2 * TALL), turned_ref, log_ref, 1)


def assemble_kernel(edge_ref, middle_ref, before_ref, after_ref, out_ref):
    def frames(begin, count):
        if begin < 0:
            return before_ref[...]
        if begin >= STRETCH:
            return after_ref[...]
        if begin < TALL:
            return edge_ref[begin : begin + count, :]
        if begin < STRETCH - TALL:
            return middle_ref[begin - TALL : begin - TALL + count, :]
        begin -= STRETCH - 2 * TALL
        return edge_ref[begin : begin + count, :]

    for dest in range(HEADS):
        begin = FR * dest
        low = low_lanes(64)
        out_ref[dest, 0:64, :] = jnp.where(
            low, frames(begin, 64).astype(f32), frames(begin + 64, 64).astype(f32)
        ).astype(bf16)
        low = low_lanes(EDGE)
        out_ref[dest, 64 : 64 + EDGE, :] = jnp.where(
            low, frames(begin - EDGE, EDGE).astype(f32), frames(begin + FR, EDGE).astype(f32)
        ).astype(bf16)


def middle_kernel(
    att_ref,
    residual_ref,
    before_ref,
    after_ref,
    gain_ref,
    weight_hbm,
    taps_ref,
    vec_ref,
    grad_ref,
    skip_ref,
    stream_ref,
    payload_ref,
    weight_ref,
    normed_ref,
    low_ref,
    linear_ref,
    gate_ref,
    glu_ref,
    grad_ext_ref,
    sums_ref,
    proj_ref,
    hat_ref,
    copy_sem,
):
    def fetch(column):
        return pltpu.make_async_copy(weight_hbm.at[:, column], weight_ref.at[:, column], copy_sem.at[column])

    for part in range(8):
        fetch(part).start()
        fetch(part + 8).start()
    lanes = low_lanes(64 + EDGE)
    for pair in range(HEADS // 2):
        cols = slice(128 * pair, 128 * (pair + 1))
        even = att_ref[2 * pair].astype(f32)
        odd = att_ref[2 * pair + 1].astype(f32)
        low = jnp.where(lanes, even, pltpu.roll(odd, HD, 1))
        high = jnp.where(lanes, pltpu.roll(even, HD, 1), odd)
        normed_ref[0:EDGE, cols] = low[64:] + before_ref[0:EDGE, cols].astype(f32)
        normed_ref[EDGE : EDGE + 64, cols] = low[:64] + residual_ref[0:64, cols].astype(f32)
        normed_ref[EDGE + 64 : EDGE + FR, cols] = high[:64] + residual_ref[64:FR, cols].astype(f32)
        normed_ref[EDGE + FR :, cols] = high[64:] + after_ref[0:EDGE, cols].astype(f32)
    stream = normed_ref[...]
    centred = stream - jnp.mean(stream, axis=1, keepdims=True)
    inv_std = lax.rsqrt(jnp.mean(centred * centred, axis=1, keepdims=True) + epsilon)
    normed = centred * inv_std
    normed_ref[...] = normed
    inv_own = inv_std[EDGE : EDGE + FR]
    low_ref[...] = (normed * gain_ref[...]).astype(bf16)
    sums_ref[...] = jnp.zeros_like(sums_ref)
    for part in range(8):
        fetch(part).wait()
        fetch(part + 8).wait()
        weights = jnp.concatenate(
            [weight_ref[:, part].reshape(D, 128), weight_ref[:, part + 8].reshape(D, 128)], axis=1
        )
        projected = dot(low_ref[...], weights)
        linear = projected[:, :128]
        gate = jax.nn.sigmoid(projected[:, 128:])
        linear_ref[part] = linear[EDGE : EDGE + FR]
        gate_ref[part] = gate[EDGE : EDGE + FR]
        glu_ref[part] = (linear * gate).astype(bf16).astype(f32)
    for part in range(8):
        cols = slice(128 * part, 128 * (part + 1))

        def put(row, total):
            place = (row % 4) * 8 + part
            sums_ref[row // 4, place : place + 1, :] = total

        conv = jnp.zeros((WIDE, 128), f32)
        for tap in range(KW):
            conv = conv + taps_ref[tap : tap + 1, cols] * glu_ref[part, tap + 1 : tap + 1 + WIDE, :]
        gamma = vec_ref[0:1, cols]
        inv_scale = lax.rsqrt(vec_ref[3:4, cols] + epsilon)
        zhat = (conv - vec_ref[2:3, cols]) * inv_scale
        shifted = gamma * zhat + vec_ref[1:2, cols]
        sig = jax.nn.sigmoid(shifted)
        grads = jnp.concatenate(
            [before_ref[EDGE:, cols], grad_ref[:, cols], after_ref[EDGE:, cols]], axis=0
        ).astype(f32)
        grad_shift = grads * sig * (1.0 + shifted * (1.0 - sig))
        grad_ext_ref[...] = (grad_shift * (gamma * inv_scale)).astype(bf16).astype(f32)
        own = slice(EDGE // 2, EDGE // 2 + FR)
        conv, zhat, grad_shift = conv[own], zhat[own], grad_shift[own]
        for row, value in enumerate((grad_shift * zhat, grad_shift, conv, conv * conv)):
            total = jnp.sum(value, axis=0, keepdims=True)
            put(KW + row, total)
            put(KW + 4 + row, total - total.astype(bf16).astype(f32))
        grad_own = grad_ext_ref[own, :]
        for tap in range(KW):
            begin = EDGE + tap - HALF
            put(tap, jnp.sum(grad_own * glu_ref[part, begin : begin + FR, :], axis=0, keepdims=True))
        grad_glu = jnp.zeros((FR, 128), f32)
        for tap in range(KW):
            begin = EDGE // 2 + HALF - tap
            grad_glu = grad_glu + taps_ref[tap : tap + 1, cols] * grad_ext_ref[begin : begin + FR, :]
        gate = gate_ref[part]
        half = grad_glu * gate
        proj_ref[:, cols] = half.astype(bf16)
        proj_ref[:, D + 128 * part : D + 128 * (part + 1)] = (half * linear_ref[part] * (1.0 - gate)).astype(bf16)
    payload_ref[:, 0:PART_ROWS, :] = sums_ref[...].astype(bf16)
    proj = proj_ref[...]
    for part in range(4):
        cols = slice(256 * part, 256 * (part + 1))
        columns = [weight_ref[2 * part : 2 * (part + 1), s].reshape(256, 128) for s in range(16)]
        hat_ref[:, cols] = dot_nt(proj, jnp.concatenate(columns, axis=1)) * gain_ref[:, cols]
    hat = hat_ref[...]
    normed = normed_ref[EDGE : EDGE + FR, :]
    mean = jnp.mean(hat, axis=1, keepdims=True)
    mean_normed = jnp.mean(hat * normed, axis=1, keepdims=True)
    centre = inv_own * (hat - mean - normed * mean_normed)
    stream = (centre + skip_ref[...].astype(f32)).astype(bf16)
    stream_ref[...] = stream
    for pair in range(HEADS // 2):
        turned = stream[:, 128 * pair : 128 * (pair + 1)].T
        payload_ref[2 * pair, PART_ROWS:, :] = turned[:HD]
        payload_ref[2 * pair + 1, PART_ROWS:, :] = turned[HD:]


def spread_kernel(payload_ref, out_ref):
    total = jnp.sum(payload_ref[...].astype(f32), axis=0).astype(bf16)
    out_ref[...] = jnp.broadcast_to(total[None], out_ref.shape)


def backward_kernel(
    qkv_ref,
    edge_att_ref,
    mid_att_ref,
    edge_log_ref,
    mid_log_ref,
    payload_ref,
    out_ref,
    keys_ref,
    values_ref,
    query_ref,
    grad_ref,
    query_rows_ref,
    grad_rows_ref,
    turned_ref,
    total_ref,
):
    pad_rows = lax.broadcasted_iota(jnp.int32, (HD, FR), 0)
    ones = jnp.where(pad_rows < 3, 1.0, 0.0).astype(bf16)
    for source in range(HEADS):
        span = slice(FR * source, FR * (source + 1))
        key_block = qkv_ref[source, HD : 2 * HD, :]
        turned_ref[:, span] = key_block
        keys_ref[span, :] = jnp.concatenate([key_block, ones], axis=0).T
        values_ref[span, :] = jnp.concatenate([qkv_ref[source, 2 * HD : 3 * HD, :], ones], axis=0).T
        grads = payload_ref[source, PART_ROWS:, :]
        block, side = divmod(source, PER_TALL)
        if 0 < block < TALLS - 1:
            att, log, block = mid_att_ref, mid_log_ref, block - 1
        else:
            att, log, block = edge_att_ref, edge_log_ref, min(block, 1)
        lanes = slice(FR * side, FR * (side + 1))
        delta = jnp.sum(grads.astype(f32) * att[block, :, lanes].astype(f32), axis=0, keepdims=True)
        logs = log[block, 0:1, lanes] * (1.0 / (SCALE * LOG2E))
        for ref, rows_ref, body, row in (
            (query_ref, query_rows_ref, qkv_ref[source, 0:HD, :], logs),
            (grad_ref, grad_rows_ref, grads, delta),
        ):
            parts = three_parts(jnp.broadcast_to(-row, (HD, FR)))
            tail = jnp.zeros((HD, FR), f32)
            for place in range(3):
                tail = jnp.where(pad_rows == place, parts[place].astype(f32), tail)
            both = jnp.concatenate([body, tail.astype(bf16)], axis=0)
            ref[:, span] = both
            rows_ref[span, :] = both.T
    total_ref[...] = jnp.zeros_like(total_ref)

    def step(block, carry):
        rows = block_rows(block, TALL)
        keys, values, turned = keys_ref[rows, :], values_ref[rows, :], turned_ref[:, rows]

        def products(chunk):
            cols = block_rows(chunk)
            return dot(keys, query_ref[:, cols]), dot(values, grad_ref[:, cols])

        key_total = jnp.zeros((TALL, 128), f32)
        value_total = jnp.zeros((TALL, 128), f32)
        ready = products(0)
        for chunk in range(CHUNKS):
            cols = block_rows(chunk)
            scores, grad_probs = ready
            if chunk + 1 < CHUNKS:
                ready = products(chunk + 1)
            probs = jnp.exp2(scores * (SCALE * LOG2E))
            grad_scores = (probs * grad_probs).astype(bf16)
            value_total = value_total + dot(probs.astype(bf16), grad_rows_ref[cols, :])
            key_total = key_total + dot(grad_scores, query_rows_ref[cols, :])
            total_ref[:, cols] += dot(turned, grad_scores)
        for place, total in ((1, key_total * SCALE), (2, value_total)):
            turned_total = total.T[:HD].astype(bf16)
            for side in range(PER_TALL):
                out_ref[PER_TALL * block + side, HD * place : HD * (place + 1), :] = turned_total[
                    :, FR * side : FR * (side + 1)
                ]
        return carry

    lax.fori_loop(0, TALLS, step, 0)
    for source in range(HEADS):
        span = slice(FR * source, FR * (source + 1))
        out_ref[source, 0:HD, :] = (total_ref[:, span] * SCALE).astype(bf16)


def finish_kernel(parts_ref, payload_ref, out_ref):
    total = jnp.sum(parts_ref[...].astype(f32), axis=0).astype(bf16)
    out_ref[...] = jnp.broadcast_to(total[None], out_ref.shape)


def unpack_kernel(frame_total, back_ref, query_ref, key_ref, value_ref, taps_ref, affine_ref, moments_ref):
    for item, ref in enumerate((query_ref, key_ref, value_ref)):
        for pair in range(HEADS // 2):
            turned = back_ref[2 * pair : 2 * pair + 2, HD * item : HD * (item + 1), :].reshape(128, FR)
            ref[:, 128 * pair : 128 * (pair + 1)] = turned.T
    totals = [back_ref[source, 3 * HD :, :].astype(f32) for source in range(10)]

    def fetch(row, part):
        place = (row % 4) * 8 + part
        return totals[row // 4][place : place + 1]

    for part in range(8):
        cols = slice(128 * part, 128 * (part + 1))
        for row in range(KW):
            taps_ref[row : row + 1, cols] = fetch(row, part)
        for row in range(4):
            ref, factor = (affine_ref, 1.0) if row < 2 else (moments_ref, 1.0 / frame_total)
            total = fetch(KW + row, part) + fetch(KW + 4 + row, part)
            ref[row % 2 : row % 2 + 1, cols] = total * factor


def call(kernel, out_shape, *args, scratch=(), gflops=0, **extra):
    if gflops:
        extra["cost_estimate"] = pl.CostEstimate(
            flops=gflops * 10**9, bytes_accessed=4 * 2**20, transcendentals=STRETCH * STRETCH
        )
    return pl.pallas_call(
        kernel, out_shape=out_shape, scratch_shapes=list(scratch), compiler_params=params(), **extra
    )(*args)


def shape(dims, dtype):
    return jax.ShapeDtypeStruct(dims, dtype)


def in_high_memory(array):
    return pltpu.with_memory_space_constraint(array, pltpu.HBM)


def whole(*dims):
    return pl.BlockSpec(dims, lambda i: (0,) * len(dims))


def weight_chunk():
    place = lax.axis_index("tm")
    return (place // 8) * 2 + lax.rem(place, 2)


def gather_weights(rows):
    peers = [[8 * x + 2 * low + core for x in range(4) for core in range(2)] for low in range(4)]
    return lax.all_gather(rows, "tm", axis=0, axis_index_groups=peers)


def neighbours(axes, first, last):
    size = lax.axis_size(axes)
    up = [(i, i + 1) for i in range(size - 1)]
    down = [(i + 1, i) for i in range(size - 1)]
    return lax.ppermute(last, axes, up), lax.ppermute(first, axes, down)


def local(
    query_in,
    key_in,
    value_in,
    residual,
    layer_gain,
    proj_weight,
    conv_kernel,
    batch_gamma,
    batch_beta,
    stale_mean,
    stale_variance,
    grad_conv,
    grad_stream_in,
):
    groups = lax.axis_size("tm")
    frame_total = FR * groups * lax.axis_size("seq")
    gain = layer_gain.reshape(1, D)
    vectors = jnp.stack([batch_gamma, batch_beta, stale_mean, stale_variance])
    in_hbm = pl.BlockSpec(memory_space=pltpu.HBM)
    in_vmem = pl.BlockSpec(memory_space=pltpu.VMEM)

    edge_rows = EDGE + EDGE // 2
    block = pltpu.VMEM((FR, D), bf16)
    packed = call(
        pack_kernel,
        shape((HEADS, 3 * HD + 128, FR), bf16),
        weight_chunk().reshape(1),
        *map(in_high_memory, (query_in, key_in, value_in, proj_weight)),
        in_specs=[pl.BlockSpec(memory_space=pltpu.SMEM)] + [in_hbm] * 4,
        scratch=(block, block, block, pltpu.VMEM((128, 128), bf16), pltpu.SemaphoreType.DMA((4,))),
    )
    qkv = lax.all_to_all(packed, "seq", 0, 0, tiled=True)
    weights = gather_weights(qkv[:, 3 * HD :])
    square = shape((STRETCH, 128), bf16)
    scores = [pltpu.VMEM((TALL, STRETCH), f32)] * 2
    keys, queries, values, edge_nat, edge_att, edge_log, first, last, row_first, row_last = call(
        edge_forward_kernel,
        (
            shape((128, STRETCH), bf16),
            square,
            square,
            shape((2 * TALL, 128), bf16),
            shape((2, HD, TALL), bf16),
            shape((2, 8, TALL), f32),
            shape((EDGE, 128), bf16),
            shape((EDGE, 128), bf16),
            shape((edge_rows, D), bf16),
            shape((edge_rows, D), bf16),
        ),
        qkv,
        in_high_memory(residual),
        in_high_memory(grad_conv),
        in_specs=[in_vmem, in_hbm, in_hbm],
        scratch=(*scores, pltpu.SemaphoreType.DMA((4,))),
    )
    edge_before, edge_after = neighbours("tm", first, last)
    before, after = neighbours(("tm", "seq"), row_first, row_last)
    mid_nat, mid_att, mid_log = call(
        middle_forward_kernel,
        (
            shape((STRETCH - 2 * TALL, 128), bf16),
            shape((TALLS - 2, HD, TALL), bf16),
            shape((TALLS - 2, 8, TALL), f32),
        ),
        keys,
        queries,
        values,
        scratch=scores,
        gflops=6,
    )
    att_payload = call(
        assemble_kernel,
        shape((HEADS, 64 + EDGE, 128), bf16),
        edge_nat,
        mid_nat,
        edge_before,
        edge_after,
    )
    att_payload, before, after = lax.optimization_barrier((att_payload, before, after))
    att_rows = lax.all_to_all(att_payload, "seq", 0, 0, tiled=True)
    grad_stream, payload = call(
        middle_kernel,
        (shape((FR, D), bf16), shape((HEADS, PART_ROWS + HD, FR), bf16)),
        att_rows,
        residual,
        before,
        after,
        gain,
        in_high_memory(weights),
        conv_kernel,
        vectors,
        grad_conv,
        grad_stream_in,
        in_specs=[in_vmem] * 5 + [in_hbm] + [in_vmem] * 4,
        scratch=(
            pltpu.VMEM((8, HEADS, 128, 128), bf16),
            pltpu.VMEM((ROWS, D), f32),
            pltpu.VMEM((ROWS, D), bf16),
            pltpu.VMEM((8, FR, 128), f32),
            pltpu.VMEM((8, FR, 128), f32),
            pltpu.VMEM((8, ROWS, 128), f32),
            pltpu.VMEM((WIDE, 128), f32),
            pltpu.VMEM((HEADS, PART_ROWS, 128), f32),
            pltpu.VMEM((FR, 2 * D), bf16),
            pltpu.VMEM((FR, D), f32),
            pltpu.SemaphoreType.DMA((HEADS,)),
        ),
    )
    payload = lax.all_to_all(payload, "seq", 0, 0, tiled=True)
    spread = call(
        spread_kernel,
        shape((groups, PART_ROWS, 128), bf16),
        payload,
        grid=(1,),
        in_specs=[whole(HEADS, PART_ROWS, 128)],
        out_specs=whole(groups, PART_ROWS, 128),
    )
    totals = lax.all_to_all(spread, "tm", 0, 0, tiled=True)
    tall = pltpu.VMEM((STRETCH, 128), bf16)
    flat = pltpu.VMEM((128, STRETCH), bf16)
    back = call(
        backward_kernel,
        shape((HEADS, 3 * HD + PART_ROWS, FR), bf16),
        qkv,
        edge_att,
        mid_att,
        edge_log,
        mid_log,
        payload,
        gflops=12,
        scratch=(
            tall,
            tall,
            flat,
            flat,
            tall,
            tall,
            pltpu.VMEM((HD, STRETCH), bf16),
            pltpu.VMEM((HD, STRETCH), f32),
        ),
    )
    back = call(
        finish_kernel,
        shape(back.shape, bf16),
        totals,
        back,
        grid=(1,),
        in_specs=[whole(groups, PART_ROWS, 128), pl.BlockSpec(memory_space=pl.ANY)],
        out_specs=pl.BlockSpec((HEADS, PART_ROWS, 128), lambda i: (0, 6, 0)),
        input_output_aliases={1: 0},
    )
    back = lax.all_to_all(back, "seq", 0, 0, tiled=True)
    narrow = shape((FR, D), bf16)
    query_grad, key_grad, value_grad, kernel_sum, affine_sum, moments = call(
        lambda *refs: unpack_kernel(frame_total, *refs),
        (narrow, narrow, narrow, shape((KW, D), f32), shape((2, D), f32), shape((2, D), f32)),
        back,
    )
    return (query_grad, key_grad, value_grad, grad_stream, kernel_sum, affine_sum, moments)


def solution(mesh):
    rows = P(("tm", "seq"), None)
    in_specs = (rows, rows, rows, rows, P(), P(None, "seq"), P(), P(), P(), P(), P(), rows, rows)
    out_specs = (rows, rows, rows, rows, P(), P(), P())
    return jax.shard_map(local, mesh=mesh, in_specs=in_specs, out_specs=out_specs, check_vma=False)
```

```python
import math

import jax
import jax.numpy as jnp
from jax import lax
from jax.experimental import pallas as pl
from jax.experimental.pallas import tpu as pltpu
from jax.sharding import PartitionSpec as P

HEADS = 16
HD = 64
D = 1024
FR = 128
KW = 31
HALF = KW // 2
STRETCH = FR * HEADS
epsilon = 1e-05
LOG2E = math.log2(math.e)
SCALE = HD ** (-0.5)
BLOCK = 256
TALL = 512
BACK = 1024
PART_ROWS = 32
EDGE = 32
ROWS = FR + 2 * EDGE
WIDE = FR + EDGE

f32 = jnp.float32
bf16 = jnp.bfloat16
NT = (((1,), (1,)), ((), ()))


def params(megabytes=48):
    return pltpu.CompilerParams(vmem_limit_bytes=megabytes * 1024 * 1024)


def dot(left, right):
    return jnp.dot(left, right, preferred_element_type=f32)


def dot_nt(left, right):
    return lax.dot_general(left, right, NT, preferred_element_type=f32)


def two_parts(value):
    high = value.astype(bf16)
    low = (value - high.astype(f32)).astype(bf16)
    return high, low


def three_parts(value):
    high = value.astype(bf16)
    rest = value - high.astype(f32)
    mid = rest.astype(bf16)
    low = (rest - mid.astype(f32)).astype(bf16)
    return high, mid, low


def rows_kernel(res_hbm, grad_hbm, first_ref, last_ref, copy_sem):
    pairs = (
        (res_hbm.at[0:EDGE], first_ref.at[0:EDGE]),
        (res_hbm.at[FR - EDGE : FR], last_ref.at[0:EDGE]),
        (grad_hbm.at[0:16], first_ref.at[EDGE : EDGE + 16]),
        (grad_hbm.at[FR - 16 : FR], last_ref.at[EDGE : EDGE + 16]),
    )
    copies = [pltpu.make_async_copy(src, dst, copy_sem.at[i]) for i, (src, dst) in enumerate(pairs)]
    for copy in copies:
        copy.start()
    for copy in copies:
        copy.wait()


def pack_kernel(
    chunk_ref,
    query_hbm,
    key_hbm,
    value_hbm,
    weight_hbm,
    out_ref,
    query_ref,
    key_ref,
    value_ref,
    weight_ref,
    copy_sem,
):
    weight_rows = weight_hbm.at[pl.ds(pl.multiple_of(chunk_ref[0] * 128, 128), 128)]
    pairs = ((query_hbm, query_ref), (key_hbm, key_ref), (value_hbm, value_ref), (weight_rows, weight_ref))
    copies = [pltpu.make_async_copy(src, dst, copy_sem.at[i]) for i, (src, dst) in enumerate(pairs)]
    for copy in copies:
        copy.start()
    for item, ref in enumerate((query_ref, key_ref, value_ref)):
        copies[item].wait()
        for pair in range(HEADS // 2):
            turned = ref[:, 128 * pair : 128 * (pair + 1)].T
            out_ref[2 * pair, HD * item : HD * (item + 1), :] = turned[:HD]
            out_ref[2 * pair + 1, HD * item : HD * (item + 1), :] = turned[HD:]
    copies[3].wait()
    for dest in range(HEADS):
        out_ref[dest, 3 * HD :, :] = weight_ref[...]


CHUNKS = STRETCH // BLOCK


TALLS = STRETCH // TALL
PER_TALL = TALL // FR


def block_rows(block, size=BLOCK):
    if isinstance(block, int):
        return slice(block * size, (block + 1) * size)
    return pl.ds(pl.multiple_of(block * size, size), size)


def low_lanes(rows):
    return lax.broadcasted_iota(jnp.int32, (rows, 128), 1) < HD


def soft_stage(keys_ref, query_ref, value_ref, following, current):
    queries = peak = total = None
    if following is not None:
        block, next_ref = following
        queries = query_ref[block_rows(block, TALL), :]
    for chunk in range(CHUNKS):
        rows = slice(BLOCK * chunk, BLOCK * (chunk + 1))
        if following is not None:
            part = dot(queries, keys_ref[:, rows])
            next_ref[:, rows] = part
            part = jnp.maximum(part[:, :128], part[:, 128:])
            peak = part if peak is None else jnp.maximum(peak, part)
        if current is not None:
            score_ref, top = current
            weights = jnp.exp2(score_ref[:, rows] - jnp.concatenate([top, top], axis=1)).astype(bf16)
            part = dot(weights, value_ref[rows, :])
            total = part if total is None else total + part
    if peak is not None:
        peak = jnp.broadcast_to(jnp.max(peak, axis=1, keepdims=True), (TALL, 128))
    return peak, total


def store_attended(total, peak, nat_ref, rows, turned_ref, log_ref, place):
    norm = jnp.broadcast_to(total[:, HD : HD + 1], (TALL, 128))
    attended = (total / norm).astype(bf16).astype(f32)
    low = low_lanes(TALL)
    nat_ref[rows, :] = jnp.where(low, attended, pltpu.roll(attended, HD, 1)).astype(bf16)
    turned = jnp.where(low, attended, peak + jnp.log2(norm)).T
    turned_ref[place] = turned[:HD].astype(bf16)
    log_ref[place] = turned[HD : HD + 8]


def edge_forward_kernel(
    qkv_ref,
    keys_ref,
    query_ref,
    value_ref,
    nat_ref,
    turned_ref,
    log_ref,
    first_ref,
    last_ref,
    score_ref,
    other_ref,
):
    pad_rows = lax.broadcasted_iota(jnp.int32, (HD, FR), 0)
    ones = jnp.where(pad_rows == 0, 1.0, 0.0).astype(bf16)
    for source in range(HEADS):
        span = slice(FR * source, FR * (source + 1))
        key_block = qkv_ref[source, HD : 2 * HD, :]
        keys_ref[0:HD, span] = key_block
        keys_ref[HD : 2 * HD, span] = key_block
        high, low = two_parts(qkv_ref[source, 0:HD, :].astype(f32) * (SCALE * LOG2E))
        query_ref[span, :] = jnp.concatenate([high, low], axis=0).T
        value_ref[span, :] = jnp.concatenate([qkv_ref[source, 2 * HD : 3 * HD, :], ones], axis=0).T
    stage = lambda *pair: soft_stage(keys_ref, query_ref, value_ref, *pair)
    top, _ = stage((0, score_ref), None)
    final_top, total = stage((TALLS - 1, other_ref), (score_ref, top))
    store_attended(total, top, nat_ref, slice(0, TALL), turned_ref, log_ref, 0)
    _, total = stage(None, (other_ref, final_top))
    store_attended(total, final_top, nat_ref, slice(TALL, 2 * TALL), turned_ref, log_ref, 1)
    first_ref[...] = nat_ref[0:EDGE, :]
    last_ref[...] = nat_ref[2 * TALL - EDGE : 2 * TALL, :]


def middle_forward_kernel(
    keys_ref, query_ref, value_ref, nat_ref, turned_ref, log_ref, score_ref, other_ref
):
    stage = lambda *pair: soft_stage(keys_ref, query_ref, value_ref, *pair)

    top, _ = stage((1, score_ref), None)
    next_top, total = stage((2, other_ref), (score_ref, top))
    store_attended(total, top, nat_ref, slice(0, TALL), turned_ref, log_ref, 0)
    _, total = stage(None, (other_ref, next_top))
    store_attended(total, next_top, nat_ref, slice(TALL, 2 * TALL), turned_ref, log_ref, 1)


def assemble_kernel(edge_ref, middle_ref, before_ref, after_ref, out_ref):
    def frames(begin, count):
        if begin < 0:
            return before_ref[...]
        if begin >= STRETCH:
            return after_ref[...]
        if begin < TALL:
            return edge_ref[begin : begin + count, :]
        if begin < STRETCH - TALL:
            return middle_ref[begin - TALL : begin - TALL + count, :]
        begin -= STRETCH - 2 * TALL
        return edge_ref[begin : begin + count, :]

    for dest in range(HEADS):
        begin = FR * dest
        low = low_lanes(64)
        out_ref[dest, 0:64, :] = jnp.where(
            low, frames(begin, 64).astype(f32), frames(begin + 64, 64).astype(f32)
        ).astype(bf16)
        low = low_lanes(EDGE)
        out_ref[dest, 64 : 64 + EDGE, :] = jnp.where(
            low, frames(begin - EDGE, EDGE).astype(f32), frames(begin + FR, EDGE).astype(f32)
        ).astype(bf16)


def middle_kernel(
    att_ref,
    residual_ref,
    before_ref,
    after_ref,
    gain_ref,
    weight_hbm,
    taps_ref,
    vec_ref,
    grad_ref,
    skip_ref,
    stream_ref,
    payload_ref,
    weight_ref,
    normed_ref,
    low_ref,
    linear_ref,
    gate_ref,
    glu_ref,
    grad_ext_ref,
    sums_ref,
    proj_ref,
    hat_ref,
    copy_sem,
):
    def fetch(column):
        return pltpu.make_async_copy(weight_hbm.at[:, column], weight_ref.at[:, column], copy_sem.at[column])

    for part in range(8):
        fetch(part).start()
        fetch(part + 8).start()
    lanes = low_lanes(64 + EDGE)
    for pair in range(HEADS // 2):
        cols = slice(128 * pair, 128 * (pair + 1))
        even = att_ref[2 * pair].astype(f32)
        odd = att_ref[2 * pair + 1].astype(f32)
        low = jnp.where(lanes, even, pltpu.roll(odd, HD, 1))
        high = jnp.where(lanes, pltpu.roll(even, HD, 1), odd)
        normed_ref[0:EDGE, cols] = low[64:] + before_ref[0:EDGE, cols].astype(f32)
        normed_ref[EDGE : EDGE + 64, cols] = low[:64] + residual_ref[0:64, cols].astype(f32)
        normed_ref[EDGE + 64 : EDGE + FR, cols] = high[:64] + residual_ref[64:FR, cols].astype(f32)
        normed_ref[EDGE + FR :, cols] = high[64:] + after_ref[0:EDGE, cols].astype(f32)
    stream = normed_ref[...]
    centred = stream - jnp.mean(stream, axis=1, keepdims=True)
    inv_std = lax.rsqrt(jnp.mean(centred * centred, axis=1, keepdims=True) + epsilon)
    normed = centred * inv_std
    normed_ref[...] = normed
    inv_own = inv_std[EDGE : EDGE + FR]
    low_ref[...] = (normed * gain_ref[...]).astype(bf16)
    sums_ref[...] = jnp.zeros_like(sums_ref)
    for part in range(8):
        fetch(part).wait()
        fetch(part + 8).wait()
        weights = jnp.concatenate(
            [weight_ref[:, part].reshape(D, 128), weight_ref[:, part + 8].reshape(D, 128)], axis=1
        )
        projected = dot(low_ref[...], weights)
        linear = projected[:, :128]
        gate = jax.nn.sigmoid(projected[:, 128:])
        linear_ref[part] = linear[EDGE : EDGE + FR]
        gate_ref[part] = gate[EDGE : EDGE + FR]
        glu_ref[part] = (linear * gate).astype(bf16).astype(f32)
    for part in range(8):
        cols = slice(128 * part, 128 * (part + 1))

        def put(row, total):
            place = (row % 4) * 8 + part
            sums_ref[row // 4, place : place + 1, :] = total

        conv = jnp.zeros((WIDE, 128), f32)
        for tap in range(KW):
            conv = conv + taps_ref[tap : tap + 1, cols] * glu_ref[part, tap + 1 : tap + 1 + WIDE, :]
        gamma = vec_ref[0:1, cols]
        inv_scale = lax.rsqrt(vec_ref[3:4, cols] + epsilon)
        zhat = (conv - vec_ref[2:3, cols]) * inv_scale
        shifted = gamma * zhat + vec_ref[1:2, cols]
        sig = jax.nn.sigmoid(shifted)
        grads = jnp.concatenate(
            [before_ref[EDGE:, cols], grad_ref[:, cols], after_ref[EDGE:, cols]], axis=0
        ).astype(f32)
        grad_shift = grads * sig * (1.0 + shifted * (1.0 - sig))
        grad_ext_ref[...] = (grad_shift * (gamma * inv_scale)).astype(bf16).astype(f32)
        own = slice(EDGE // 2, EDGE // 2 + FR)
        conv, zhat, grad_shift = conv[own], zhat[own], grad_shift[own]
        for row, value in enumerate((grad_shift * zhat, grad_shift, conv, conv * conv)):
            total = jnp.sum(value, axis=0, keepdims=True)
            put(KW + row, total)
            put(KW + 4 + row, total - total.astype(bf16).astype(f32))
        grad_own = grad_ext_ref[own, :]
        for tap in range(KW):
            begin = EDGE + tap - HALF
            put(tap, jnp.sum(grad_own * glu_ref[part, begin : begin + FR, :], axis=0, keepdims=True))
        grad_glu = jnp.zeros((FR, 128), f32)
        for tap in range(KW):
            begin = EDGE // 2 + HALF - tap
            grad_glu = grad_glu + taps_ref[tap : tap + 1, cols] * grad_ext_ref[begin : begin + FR, :]
        gate = gate_ref[part]
        half = grad_glu * gate
        proj_ref[:, cols] = half.astype(bf16)
        proj_ref[:, D + 128 * part : D + 128 * (part + 1)] = (half * linear_ref[part] * (1.0 - gate)).astype(bf16)
    payload_ref[:, 0:PART_ROWS, :] = sums_ref[...].astype(bf16)
    proj = proj_ref[...]
    for part in range(4):
        cols = slice(256 * part, 256 * (part + 1))
        columns = [weight_ref[2 * part : 2 * (part + 1), s].reshape(256, 128) for s in range(16)]
        hat_ref[:, cols] = dot_nt(proj, jnp.concatenate(columns, axis=1)) * gain_ref[:, cols]
    hat = hat_ref[...]
    normed = normed_ref[EDGE : EDGE + FR, :]
    mean = jnp.mean(hat, axis=1, keepdims=True)
    mean_normed = jnp.mean(hat * normed, axis=1, keepdims=True)
    centre = inv_own * (hat - mean - normed * mean_normed)
    stream = (centre + skip_ref[...].astype(f32)).astype(bf16)
    stream_ref[...] = stream
    for pair in range(HEADS // 2):
        turned = stream[:, 128 * pair : 128 * (pair + 1)].T
        payload_ref[2 * pair, PART_ROWS:, :] = turned[:HD]
        payload_ref[2 * pair + 1, PART_ROWS:, :] = turned[HD:]


def spread_kernel(payload_ref, out_ref):
    total = jnp.sum(payload_ref[...].astype(f32), axis=0).astype(bf16)
    out_ref[...] = jnp.broadcast_to(total[None], out_ref.shape)


def backward_kernel(
    qkv_ref,
    edge_att_ref,
    mid_att_ref,
    edge_log_ref,
    mid_log_ref,
    payload_ref,
    out_ref,
    keys_ref,
    values_ref,
    query_ref,
    grad_ref,
    query_rows_ref,
    grad_rows_ref,
    turned_ref,
    total_ref,
):
    pad_rows = lax.broadcasted_iota(jnp.int32, (HD, FR), 0)
    ones = jnp.where(pad_rows < 3, 1.0, 0.0).astype(bf16)
    for source in range(HEADS):
        span = slice(FR * source, FR * (source + 1))
        key_block = qkv_ref[source, HD : 2 * HD, :]
        turned_ref[:, span] = key_block
        keys_ref[span, :] = jnp.concatenate([key_block, ones], axis=0).T
        values_ref[span, :] = jnp.concatenate([qkv_ref[source, 2 * HD : 3 * HD, :], ones], axis=0).T
        grads = payload_ref[source, PART_ROWS:, :]
        block, side = divmod(source, PER_TALL)
        if 0 < block < TALLS - 1:
            att, log, block = mid_att_ref, mid_log_ref, block - 1
        else:
            att, log, block = edge_att_ref, edge_log_ref, min(block, 1)
        lanes = slice(FR * side, FR * (side + 1))
        delta = jnp.sum(grads.astype(f32) * att[block, :, lanes].astype(f32), axis=0, keepdims=True)
        logs = log[block, 0:1, lanes] * (1.0 / (SCALE * LOG2E))
        for ref, rows_ref, body, row in (
            (query_ref, query_rows_ref, qkv_ref[source, 0:HD, :], logs),
            (grad_ref, grad_rows_ref, grads, delta),
        ):
            parts = three_parts(jnp.broadcast_to(-row, (HD, FR)))
            tail = jnp.zeros((HD, FR), f32)
            for place in range(3):
                tail = jnp.where(pad_rows == place, parts[place].astype(f32), tail)
            both = jnp.concatenate([body, tail.astype(bf16)], axis=0)
            ref[:, span] = both
            rows_ref[span, :] = both.T
    total_ref[...] = jnp.zeros_like(total_ref)

    def step(block, carry):
        rows = block_rows(block, BACK)
        keys, values, turned = keys_ref[rows, :], values_ref[rows, :], turned_ref[:, rows]

        def products(chunk):
            cols = block_rows(chunk)
            return dot(keys, query_ref[:, cols]), dot(values, grad_ref[:, cols])

        key_total = jnp.zeros((BACK, 128), f32)
        value_total = jnp.zeros((BACK, 128), f32)
        ready = products(0)
        for chunk in range(CHUNKS):
            cols = block_rows(chunk)
            scores, grad_probs = ready
            if chunk + 1 < CHUNKS:
                ready = products(chunk + 1)
            probs = jnp.exp2(scores * (SCALE * LOG2E))
            grad_scores = (probs * grad_probs).astype(bf16)
            value_total = value_total + dot(probs.astype(bf16), grad_rows_ref[cols, :])
            key_total = key_total + dot(grad_scores, query_rows_ref[cols, :])
            total_ref[:, cols] += dot(turned, grad_scores)
        for place, total in ((1, key_total * SCALE), (2, value_total)):
            turned_total = total.T[:HD].astype(bf16)
            for side in range(BACK // FR):
                out_ref[BACK // FR * block + side, HD * place : HD * (place + 1), :] = turned_total[
                    :, FR * side : FR * (side + 1)
                ]
        return carry

    lax.fori_loop(0, STRETCH // BACK, step, 0)
    for source in range(HEADS):
        span = slice(FR * source, FR * (source + 1))
        out_ref[source, 0:HD, :] = (total_ref[:, span] * SCALE).astype(bf16)


def finish_kernel(parts_ref, payload_ref, out_ref):
    total = jnp.sum(parts_ref[...].astype(f32), axis=0).astype(bf16)
    out_ref[...] = jnp.broadcast_to(total[None], out_ref.shape)


def unpack_kernel(frame_total, back_ref, query_ref, key_ref, value_ref, taps_ref, affine_ref, moments_ref):
    for item, ref in enumerate((query_ref, key_ref, value_ref)):
        for pair in range(HEADS // 2):
            turned = back_ref[2 * pair : 2 * pair + 2, HD * item : HD * (item + 1), :].reshape(128, FR)
            ref[:, 128 * pair : 128 * (pair + 1)] = turned.T
    totals = [back_ref[source, 3 * HD :, :].astype(f32) for source in range(10)]

    def fetch(row, part):
        place = (row % 4) * 8 + part
        return totals[row // 4][place : place + 1]

    for part in range(8):
        cols = slice(128 * part, 128 * (part + 1))
        for row in range(KW):
            taps_ref[row : row + 1, cols] = fetch(row, part)
        for row in range(4):
            ref, factor = (affine_ref, 1.0) if row < 2 else (moments_ref, 1.0 / frame_total)
            total = fetch(KW + row, part) + fetch(KW + 4 + row, part)
            ref[row % 2 : row % 2 + 1, cols] = total * factor


def call(kernel, out_shape, *args, scratch=(), gflops=0, **extra):
    if gflops:
        extra["cost_estimate"] = pl.CostEstimate(
            flops=gflops * 10**9, bytes_accessed=4 * 2**20, transcendentals=STRETCH * STRETCH
        )
    return pl.pallas_call(
        kernel, out_shape=out_shape, scratch_shapes=list(scratch), compiler_params=params(), **extra
    )(*args)


def shape(dims, dtype):
    return jax.ShapeDtypeStruct(dims, dtype)


def in_high_memory(array):
    return pltpu.with_memory_space_constraint(array, pltpu.HBM)


def whole(*dims):
    return pl.BlockSpec(dims, lambda i: (0,) * len(dims))


def weight_chunk():
    place = lax.axis_index("tm")
    return (place // 8) * 2 + lax.rem(place, 2)


def gather_weights(rows):
    peers = [[8 * x + 2 * low + core for x in range(4) for core in range(2)] for low in range(4)]
    return lax.all_gather(rows, "tm", axis=0, axis_index_groups=peers)


def neighbours(axes, first, last):
    size = lax.axis_size(axes)
    up = [(i, i + 1) for i in range(size - 1)]
    down = [(i + 1, i) for i in range(size - 1)]
    return lax.ppermute(last, axes, up), lax.ppermute(first, axes, down)


def local(
    query_in,
    key_in,
    value_in,
    residual,
    layer_gain,
    proj_weight,
    conv_kernel,
    batch_gamma,
    batch_beta,
    stale_mean,
    stale_variance,
    grad_conv,
    grad_stream_in,
):
    groups = lax.axis_size("tm")
    frame_total = FR * groups * lax.axis_size("seq")
    gain = layer_gain.reshape(1, D)
    vectors = jnp.stack([batch_gamma, batch_beta, stale_mean, stale_variance])
    in_hbm = pl.BlockSpec(memory_space=pltpu.HBM)
    in_vmem = pl.BlockSpec(memory_space=pltpu.VMEM)

    edge_rows = EDGE + EDGE // 2
    block = pltpu.VMEM((FR, D), bf16)
    packed = call(
        pack_kernel,
        shape((HEADS, 3 * HD + 128, FR), bf16),
        weight_chunk().reshape(1),
        *map(in_high_memory, (query_in, key_in, value_in, proj_weight)),
        in_specs=[pl.BlockSpec(memory_space=pltpu.SMEM)] + [in_hbm] * 4,
        scratch=(block, block, block, pltpu.VMEM((128, 128), bf16), pltpu.SemaphoreType.DMA((4,))),
    )
    row_first, row_last = call(
        rows_kernel,
        (shape((edge_rows, D), bf16), shape((edge_rows, D), bf16)),
        in_high_memory(residual),
        in_high_memory(grad_conv),
        in_specs=[in_hbm] * 2,
        scratch=(pltpu.SemaphoreType.DMA((4,)),),
    )
    before, after = neighbours(("tm", "seq"), row_first, row_last)
    qkv = lax.all_to_all(packed, "seq", 0, 0, tiled=True)
    weights = gather_weights(qkv[:, 3 * HD :])
    square = shape((STRETCH, 128), bf16)
    scores = [pltpu.VMEM((TALL, STRETCH), f32)] * 2
    keys, queries, values, edge_nat, edge_att, edge_log, first, last = call(
        edge_forward_kernel,
        (
            shape((128, STRETCH), bf16),
            square,
            square,
            shape((2 * TALL, 128), bf16),
            shape((2, HD, TALL), bf16),
            shape((2, 8, TALL), f32),
            shape((EDGE, 128), bf16),
            shape((EDGE, 128), bf16),
        ),
        qkv,
        scratch=scores,
    )
    edge_before, edge_after = neighbours("tm", first, last)
    mid_nat, mid_att, mid_log = call(
        middle_forward_kernel,
        (
            shape((STRETCH - 2 * TALL, 128), bf16),
            shape((TALLS - 2, HD, TALL), bf16),
            shape((TALLS - 2, 8, TALL), f32),
        ),
        keys,
        queries,
        values,
        scratch=scores,
        gflops=6,
    )
    att_payload = call(
        assemble_kernel,
        shape((HEADS, 64 + EDGE, 128), bf16),
        edge_nat,
        mid_nat,
        edge_before,
        edge_after,
    )
    att_payload, before, after = lax.optimization_barrier((att_payload, before, after))
    att_rows = lax.all_to_all(att_payload, "seq", 0, 0, tiled=True)
    grad_stream, payload = call(
        middle_kernel,
        (shape((FR, D), bf16), shape((HEADS, PART_ROWS + HD, FR), bf16)),
        att_rows,
        residual,
        before,
        after,
        gain,
        in_high_memory(weights),
        conv_kernel,
        vectors,
        grad_conv,
        grad_stream_in,
        in_specs=[in_vmem] * 5 + [in_hbm] + [in_vmem] * 4,
        scratch=(
            pltpu.VMEM((8, HEADS, 128, 128), bf16),
            pltpu.VMEM((ROWS, D), f32),
            pltpu.VMEM((ROWS, D), bf16),
            pltpu.VMEM((8, FR, 128), f32),
            pltpu.VMEM((8, FR, 128), f32),
            pltpu.VMEM((8, ROWS, 128), f32),
            pltpu.VMEM((WIDE, 128), f32),
            pltpu.VMEM((HEADS, PART_ROWS, 128), f32),
            pltpu.VMEM((FR, 2 * D), bf16),
            pltpu.VMEM((FR, D), f32),
            pltpu.SemaphoreType.DMA((HEADS,)),
        ),
    )
    payload = lax.all_to_all(payload, "seq", 0, 0, tiled=True)
    spread = call(
        spread_kernel,
        shape((groups, PART_ROWS, 128), bf16),
        payload,
        grid=(1,),
        in_specs=[whole(HEADS, PART_ROWS, 128)],
        out_specs=whole(groups, PART_ROWS, 128),
    )
    totals = lax.all_to_all(spread, "tm", 0, 0, tiled=True)
    tall = pltpu.VMEM((STRETCH, 128), bf16)
    flat = pltpu.VMEM((128, STRETCH), bf16)
    back = call(
        backward_kernel,
        shape((HEADS, 3 * HD + PART_ROWS, FR), bf16),
        qkv,
        edge_att,
        mid_att,
        edge_log,
        mid_log,
        payload,
        gflops=12,
        scratch=(
            tall,
            tall,
            flat,
            flat,
            tall,
            tall,
            pltpu.VMEM((HD, STRETCH), bf16),
            pltpu.VMEM((HD, STRETCH), f32),
        ),
    )
    back = call(
        finish_kernel,
        shape(back.shape, bf16),
        totals,
        back,
        grid=(1,),
        in_specs=[whole(groups, PART_ROWS, 128), pl.BlockSpec(memory_space=pl.ANY)],
        out_specs=pl.BlockSpec((HEADS, PART_ROWS, 128), lambda i: (0, 6, 0)),
        input_output_aliases={1: 0},
    )
    back = lax.all_to_all(back, "seq", 0, 0, tiled=True)
    narrow = shape((FR, D), bf16)
    query_grad, key_grad, value_grad, kernel_sum, affine_sum, moments = call(
        lambda *refs: unpack_kernel(frame_total, *refs),
        (narrow, narrow, narrow, shape((KW, D), f32), shape((2, D), f32), shape((2, D), f32)),
        back,
    )
    return (query_grad, key_grad, value_grad, grad_stream, kernel_sum, affine_sum, moments)


def solution(mesh):
    rows = P(("tm", "seq"), None)
    in_specs = (rows, rows, rows, rows, P(), P(None, "seq"), P(), P(), P(), P(), P(), rows, rows)
    out_specs = (rows, rows, rows, rows, P(), P(), P())
    return jax.shard_map(local, mesh=mesh, in_specs=in_specs, out_specs=out_specs, check_vma=False)
```

```python
import math

import jax
import jax.numpy as jnp
from jax import lax
from jax.experimental import pallas as pl
from jax.experimental.pallas import tpu as pltpu
from jax.sharding import PartitionSpec as P

HEADS = 16
HD = 64
D = 1024
FR = 128
KW = 31
HALF = KW // 2
STRETCH = FR * HEADS
epsilon = 1e-05
LOG2E = math.log2(math.e)
SCALE = HD ** (-0.5)
BLOCK = 256
TALL = 512
BACK = 1024
PART_ROWS = 32
EDGE = 32
ROWS = FR + 2 * EDGE
WIDE = FR + EDGE

f32 = jnp.float32
bf16 = jnp.bfloat16
NT = (((1,), (1,)), ((), ()))


def params(megabytes=48):
    return pltpu.CompilerParams(vmem_limit_bytes=megabytes * 1024 * 1024)


def dot(left, right):
    return jnp.dot(left, right, preferred_element_type=f32)


def dot_nt(left, right):
    return lax.dot_general(left, right, NT, preferred_element_type=f32)


def two_parts(value):
    high = value.astype(bf16)
    low = (value - high.astype(f32)).astype(bf16)
    return high, low


def three_parts(value):
    high = value.astype(bf16)
    rest = value - high.astype(f32)
    mid = rest.astype(bf16)
    low = (rest - mid.astype(f32)).astype(bf16)
    return high, mid, low


def pack_kernel(
    chunk_ref,
    query_hbm,
    key_hbm,
    value_hbm,
    weight_hbm,
    res_hbm,
    grad_hbm,
    out_ref,
    first_ref,
    last_ref,
    query_ref,
    key_ref,
    value_ref,
    weight_ref,
    copy_sem,
):
    weight_rows = weight_hbm.at[pl.ds(pl.multiple_of(chunk_ref[0] * 128, 128), 128)]
    pairs = (
        (query_hbm, query_ref),
        (key_hbm, key_ref),
        (value_hbm, value_ref),
        (weight_rows, weight_ref),
        (res_hbm.at[0:EDGE], first_ref.at[0:EDGE]),
        (res_hbm.at[FR - EDGE : FR], last_ref.at[0:EDGE]),
        (grad_hbm.at[0:16], first_ref.at[EDGE : EDGE + 16]),
        (grad_hbm.at[FR - 16 : FR], last_ref.at[EDGE : EDGE + 16]),
    )
    copies = [pltpu.make_async_copy(src, dst, copy_sem.at[i]) for i, (src, dst) in enumerate(pairs)]
    for copy in copies:
        copy.start()
    for item, ref in enumerate((query_ref, key_ref, value_ref)):
        copies[item].wait()
        for pair in range(HEADS // 2):
            turned = ref[:, 128 * pair : 128 * (pair + 1)].T
            out_ref[2 * pair, HD * item : HD * (item + 1), :] = turned[:HD]
            out_ref[2 * pair + 1, HD * item : HD * (item + 1), :] = turned[HD:]
    copies[3].wait()
    for dest in range(HEADS):
        out_ref[dest, 3 * HD :, :] = weight_ref[...]
    for copy in copies[4:]:
        copy.wait()


CHUNKS = STRETCH // BLOCK


TALLS = STRETCH // TALL
PER_TALL = TALL // FR


def block_rows(block, size=BLOCK):
    if isinstance(block, int):
        return slice(block * size, (block + 1) * size)
    return pl.ds(pl.multiple_of(block * size, size), size)


def low_lanes(rows):
    return lax.broadcasted_iota(jnp.int32, (rows, 128), 1) < HD


def soft_stage(keys_ref, query_ref, value_ref, following, current):
    queries = peak = total = None
    if following is not None:
        block, next_ref = following
        queries = query_ref[block_rows(block, TALL), :]
    for chunk in range(CHUNKS):
        rows = slice(BLOCK * chunk, BLOCK * (chunk + 1))
        if following is not None:
            part = dot(queries, keys_ref[:, rows])
            next_ref[:, rows] = part
            part = jnp.maximum(part[:, :128], part[:, 128:])
            peak = part if peak is None else jnp.maximum(peak, part)
        if current is not None:
            score_ref, top = current
            weights = jnp.exp2(score_ref[:, rows] - jnp.concatenate([top, top], axis=1)).astype(bf16)
            part = dot(weights, value_ref[rows, :])
            total = part if total is None else total + part
    if peak is not None:
        peak = jnp.broadcast_to(jnp.max(peak, axis=1, keepdims=True), (TALL, 128))
    return peak, total


def store_attended(total, peak, nat_ref, rows, turned_ref, log_ref, place):
    norm = jnp.broadcast_to(total[:, HD : HD + 1], (TALL, 128))
    attended = (total / norm).astype(bf16).astype(f32)
    low = low_lanes(TALL)
    nat_ref[rows, :] = jnp.where(low, attended, pltpu.roll(attended, HD, 1)).astype(bf16)
    turned = jnp.where(low, attended, peak + jnp.log2(norm)).T
    turned_ref[place] = turned[:HD].astype(bf16)
    log_ref[place] = turned[HD : HD + 8]


def edge_forward_kernel(
    qkv_ref,
    keys_ref,
    query_ref,
    value_ref,
    nat_ref,
    turned_ref,
    log_ref,
    first_ref,
    last_ref,
    score_ref,
    other_ref,
):
    pad_rows = lax.broadcasted_iota(jnp.int32, (HD, FR), 0)
    ones = jnp.where(pad_rows == 0, 1.0, 0.0).astype(bf16)
    for source in range(HEADS):
        span = slice(FR * source, FR * (source + 1))
        key_block = qkv_ref[source, HD : 2 * HD, :]
        keys_ref[0:HD, span] = key_block
        keys_ref[HD : 2 * HD, span] = key_block
        high, low = two_parts(qkv_ref[source, 0:HD, :].astype(f32) * (SCALE * LOG2E))
        query_ref[span, :] = jnp.concatenate([high, low], axis=0).T
        value_ref[span, :] = jnp.concatenate([qkv_ref[source, 2 * HD : 3 * HD, :], ones], axis=0).T
    stage = lambda *pair: soft_stage(keys_ref, query_ref, value_ref, *pair)
    top, _ = stage((0, score_ref), None)
    final_top, total = stage((TALLS - 1, other_ref), (score_ref, top))
    store_attended(total, top, nat_ref, slice(0, TALL), turned_ref, log_ref, 0)
    _, total = stage(None, (other_ref, final_top))
    store_attended(total, final_top, nat_ref, slice(TALL, 2 * TALL), turned_ref, log_ref, 1)
    first_ref[...] = nat_ref[0:EDGE, :]
    last_ref[...] = nat_ref[2 * TALL - EDGE : 2 * TALL, :]


def middle_forward_kernel(
    keys_ref, query_ref, value_ref, nat_ref, turned_ref, log_ref, score_ref, other_ref
):
    stage = lambda *pair: soft_stage(keys_ref, query_ref, value_ref, *pair)

    top, _ = stage((1, score_ref), None)
    next_top, total = stage((2, other_ref), (score_ref, top))
    store_attended(total, top, nat_ref, slice(0, TALL), turned_ref, log_ref, 0)
    _, total = stage(None, (other_ref, next_top))
    store_attended(total, next_top, nat_ref, slice(TALL, 2 * TALL), turned_ref, log_ref, 1)


def assemble_kernel(edge_ref, middle_ref, before_ref, after_ref, out_ref):
    def frames(begin, count):
        if begin < 0:
            return before_ref[...]
        if begin >= STRETCH:
            return after_ref[...]
        if begin < TALL:
            return edge_ref[begin : begin + count, :]
        if begin < STRETCH - TALL:
            return middle_ref[begin - TALL : begin - TALL + count, :]
        begin -= STRETCH - 2 * TALL
        return edge_ref[begin : begin + count, :]

    for dest in range(HEADS):
        begin = FR * dest
        low = low_lanes(64)
        out_ref[dest, 0:64, :] = jnp.where(
            low, frames(begin, 64).astype(f32), frames(begin + 64, 64).astype(f32)
        ).astype(bf16)
        low = low_lanes(EDGE)
        out_ref[dest, 64 : 64 + EDGE, :] = jnp.where(
            low, frames(begin - EDGE, EDGE).astype(f32), frames(begin + FR, EDGE).astype(f32)
        ).astype(bf16)


def middle_kernel(
    att_ref,
    residual_ref,
    before_ref,
    after_ref,
    gain_ref,
    weight_hbm,
    taps_ref,
    vec_ref,
    grad_ref,
    skip_ref,
    stream_ref,
    payload_ref,
    weight_ref,
    normed_ref,
    low_ref,
    linear_ref,
    gate_ref,
    glu_ref,
    grad_ext_ref,
    sums_ref,
    proj_ref,
    hat_ref,
    copy_sem,
):
    def fetch(column):
        return pltpu.make_async_copy(weight_hbm.at[:, column], weight_ref.at[:, column], copy_sem.at[column])

    for part in range(8):
        fetch(part).start()
        fetch(part + 8).start()
    lanes = low_lanes(64 + EDGE)
    for pair in range(HEADS // 2):
        cols = slice(128 * pair, 128 * (pair + 1))
        even = att_ref[2 * pair].astype(f32)
        odd = att_ref[2 * pair + 1].astype(f32)
        low = jnp.where(lanes, even, pltpu.roll(odd, HD, 1))
        high = jnp.where(lanes, pltpu.roll(even, HD, 1), odd)
        normed_ref[0:EDGE, cols] = low[64:] + before_ref[0:EDGE, cols].astype(f32)
        normed_ref[EDGE : EDGE + 64, cols] = low[:64] + residual_ref[0:64, cols].astype(f32)
        normed_ref[EDGE + 64 : EDGE + FR, cols] = high[:64] + residual_ref[64:FR, cols].astype(f32)
        normed_ref[EDGE + FR :, cols] = high[64:] + after_ref[0:EDGE, cols].astype(f32)
    stream = normed_ref[...]
    centred = stream - jnp.mean(stream, axis=1, keepdims=True)
    inv_std = lax.rsqrt(jnp.mean(centred * centred, axis=1, keepdims=True) + epsilon)
    normed = centred * inv_std
    normed_ref[...] = normed
    inv_own = inv_std[EDGE : EDGE + FR]
    low_ref[...] = (normed * gain_ref[...]).astype(bf16)
    sums_ref[...] = jnp.zeros_like(sums_ref)
    for part in range(8):
        fetch(part).wait()
        fetch(part + 8).wait()
        weights = jnp.concatenate(
            [weight_ref[:, part].reshape(D, 128), weight_ref[:, part + 8].reshape(D, 128)], axis=1
        )
        projected = dot(low_ref[...], weights)
        linear = projected[:, :128]
        gate = jax.nn.sigmoid(projected[:, 128:])
        linear_ref[part] = linear[EDGE : EDGE + FR]
        gate_ref[part] = gate[EDGE : EDGE + FR]
        glu_ref[part] = (linear * gate).astype(bf16).astype(f32)
    for part in range(8):
        cols = slice(128 * part, 128 * (part + 1))

        def put(row, total):
            place = (row % 4) * 8 + part
            sums_ref[row // 4, place : place + 1, :] = total

        conv = jnp.zeros((WIDE, 128), f32)
        for tap in range(KW):
            conv = conv + taps_ref[tap : tap + 1, cols] * glu_ref[part, tap + 1 : tap + 1 + WIDE, :]
        gamma = vec_ref[0:1, cols]
        inv_scale = lax.rsqrt(vec_ref[3:4, cols] + epsilon)
        zhat = (conv - vec_ref[2:3, cols]) * inv_scale
        shifted = gamma * zhat + vec_ref[1:2, cols]
        sig = jax.nn.sigmoid(shifted)
        grads = jnp.concatenate(
            [before_ref[EDGE:, cols], grad_ref[:, cols], after_ref[EDGE:, cols]], axis=0
        ).astype(f32)
        grad_shift = grads * sig * (1.0 + shifted * (1.0 - sig))
        grad_ext_ref[...] = (grad_shift * (gamma * inv_scale)).astype(bf16).astype(f32)
        own = slice(EDGE // 2, EDGE // 2 + FR)
        conv, zhat, grad_shift = conv[own], zhat[own], grad_shift[own]
        for row, value in enumerate((grad_shift * zhat, grad_shift, conv, conv * conv)):
            total = jnp.sum(value, axis=0, keepdims=True)
            put(KW + row, total)
            put(KW + 4 + row, total - total.astype(bf16).astype(f32))
        grad_own = grad_ext_ref[own, :]
        for tap in range(KW):
            begin = EDGE + tap - HALF
            put(tap, jnp.sum(grad_own * glu_ref[part, begin : begin + FR, :], axis=0, keepdims=True))
        grad_glu = jnp.zeros((FR, 128), f32)
        for tap in range(KW):
            begin = EDGE // 2 + HALF - tap
            grad_glu = grad_glu + taps_ref[tap : tap + 1, cols] * grad_ext_ref[begin : begin + FR, :]
        gate = gate_ref[part]
        half = grad_glu * gate
        proj_ref[:, cols] = half.astype(bf16)
        proj_ref[:, D + 128 * part : D + 128 * (part + 1)] = (half * linear_ref[part] * (1.0 - gate)).astype(bf16)
    payload_ref[:, 0:PART_ROWS, :] = sums_ref[...].astype(bf16)
    proj = proj_ref[...]
    for part in range(4):
        cols = slice(256 * part, 256 * (part + 1))
        columns = [weight_ref[2 * part : 2 * (part + 1), s].reshape(256, 128) for s in range(16)]
        hat_ref[:, cols] = dot_nt(proj, jnp.concatenate(columns, axis=1)) * gain_ref[:, cols]
    hat = hat_ref[...]
    normed = normed_ref[EDGE : EDGE + FR, :]
    mean = jnp.mean(hat, axis=1, keepdims=True)
    mean_normed = jnp.mean(hat * normed, axis=1, keepdims=True)
    centre = inv_own * (hat - mean - normed * mean_normed)
    stream = (centre + skip_ref[...].astype(f32)).astype(bf16)
    stream_ref[...] = stream
    for pair in range(HEADS // 2):
        turned = stream[:, 128 * pair : 128 * (pair + 1)].T
        payload_ref[2 * pair, PART_ROWS:, :] = turned[:HD]
        payload_ref[2 * pair + 1, PART_ROWS:, :] = turned[HD:]


def spread_kernel(payload_ref, out_ref):
    total = jnp.sum(payload_ref[...].astype(f32), axis=0).astype(bf16)
    out_ref[...] = jnp.broadcast_to(total[None], out_ref.shape)


def backward_kernel(
    qkv_ref,
    edge_att_ref,
    mid_att_ref,
    edge_log_ref,
    mid_log_ref,
    payload_ref,
    out_ref,
    keys_ref,
    values_ref,
    query_ref,
    grad_ref,
    query_rows_ref,
    grad_rows_ref,
    turned_ref,
    total_ref,
):
    pad_rows = lax.broadcasted_iota(jnp.int32, (HD, FR), 0)
    ones = jnp.where(pad_rows < 3, 1.0, 0.0).astype(bf16)
    for source in range(HEADS):
        span = slice(FR * source, FR * (source + 1))
        key_block = qkv_ref[source, HD : 2 * HD, :]
        turned_ref[:, span] = key_block
        keys_ref[span, :] = jnp.concatenate([key_block, ones], axis=0).T
        values_ref[span, :] = jnp.concatenate([qkv_ref[source, 2 * HD : 3 * HD, :], ones], axis=0).T
        grads = payload_ref[source, PART_ROWS:, :]
        block, side = divmod(source, PER_TALL)
        if 0 < block < TALLS - 1:
            att, log, block = mid_att_ref, mid_log_ref, block - 1
        else:
            att, log, block = edge_att_ref, edge_log_ref, min(block, 1)
        lanes = slice(FR * side, FR * (side + 1))
        delta = jnp.sum(grads.astype(f32) * att[block, :, lanes].astype(f32), axis=0, keepdims=True)
        logs = log[block, 0:1, lanes] * (1.0 / (SCALE * LOG2E))
        for ref, rows_ref, body, row in (
            (query_ref, query_rows_ref, qkv_ref[source, 0:HD, :], logs),
            (grad_ref, grad_rows_ref, grads, delta),
        ):
            parts = three_parts(jnp.broadcast_to(-row, (HD, FR)))
            tail = jnp.zeros((HD, FR), f32)
            for place in range(3):
                tail = jnp.where(pad_rows == place, parts[place].astype(f32), tail)
            both = jnp.concatenate([body, tail.astype(bf16)], axis=0)
            ref[:, span] = both
            rows_ref[span, :] = both.T
    total_ref[...] = jnp.zeros_like(total_ref)

    def step(block, carry):
        rows = block_rows(block, BACK)
        keys, values, turned = keys_ref[rows, :], values_ref[rows, :], turned_ref[:, rows]

        def products(chunk):
            cols = block_rows(chunk)
            return dot(keys, query_ref[:, cols]), dot(values, grad_ref[:, cols])

        key_total = jnp.zeros((BACK, 128), f32)
        value_total = jnp.zeros((BACK, 128), f32)
        ready = products(0)
        for chunk in range(CHUNKS):
            cols = block_rows(chunk)
            scores, grad_probs = ready
            if chunk + 1 < CHUNKS:
                ready = products(chunk + 1)
            probs = jnp.exp2(scores * (SCALE * LOG2E))
            grad_scores = (probs * grad_probs).astype(bf16)
            value_total = value_total + dot(probs.astype(bf16), grad_rows_ref[cols, :])
            key_total = key_total + dot(grad_scores, query_rows_ref[cols, :])
            total_ref[:, cols] += dot(turned, grad_scores)
        for place, total in ((1, key_total * SCALE), (2, value_total)):
            turned_total = total.T[:HD].astype(bf16)
            for side in range(BACK // FR):
                out_ref[BACK // FR * block + side, HD * place : HD * (place + 1), :] = turned_total[
                    :, FR * side : FR * (side + 1)
                ]
        return carry

    lax.fori_loop(0, STRETCH // BACK, step, 0)
    for source in range(HEADS):
        span = slice(FR * source, FR * (source + 1))
        out_ref[source, 0:HD, :] = (total_ref[:, span] * SCALE).astype(bf16)


def finish_kernel(parts_ref, payload_ref, out_ref):
    total = jnp.sum(parts_ref[...].astype(f32), axis=0).astype(bf16)
    out_ref[...] = jnp.broadcast_to(total[None], out_ref.shape)


def unpack_kernel(frame_total, back_ref, query_ref, key_ref, value_ref, taps_ref, affine_ref, moments_ref):
    for item, ref in enumerate((query_ref, key_ref, value_ref)):
        for pair in range(HEADS // 2):
            turned = back_ref[2 * pair : 2 * pair + 2, HD * item : HD * (item + 1), :].reshape(128, FR)
            ref[:, 128 * pair : 128 * (pair + 1)] = turned.T
    totals = [back_ref[source, 3 * HD :, :].astype(f32) for source in range(10)]

    def fetch(row, part):
        place = (row % 4) * 8 + part
        return totals[row // 4][place : place + 1]

    for part in range(8):
        cols = slice(128 * part, 128 * (part + 1))
        for row in range(KW):
            taps_ref[row : row + 1, cols] = fetch(row, part)
        for row in range(4):
            ref, factor = (affine_ref, 1.0) if row < 2 else (moments_ref, 1.0 / frame_total)
            total = fetch(KW + row, part) + fetch(KW + 4 + row, part)
            ref[row % 2 : row % 2 + 1, cols] = total * factor


def call(kernel, out_shape, *args, scratch=(), gflops=0, **extra):
    if gflops:
        extra["cost_estimate"] = pl.CostEstimate(
            flops=gflops * 10**9, bytes_accessed=4 * 2**20, transcendentals=STRETCH * STRETCH
        )
    return pl.pallas_call(
        kernel, out_shape=out_shape, scratch_shapes=list(scratch), compiler_params=params(), **extra
    )(*args)


def shape(dims, dtype):
    return jax.ShapeDtypeStruct(dims, dtype)


def in_high_memory(array):
    return pltpu.with_memory_space_constraint(array, pltpu.HBM)


def whole(*dims):
    return pl.BlockSpec(dims, lambda i: (0,) * len(dims))


def weight_chunk():
    place = lax.axis_index("tm")
    return (place // 8) * 2 + lax.rem(place, 2)


def gather_weights(rows):
    peers = [[8 * x + 2 * low + core for x in range(4) for core in range(2)] for low in range(4)]
    return lax.all_gather(rows, "tm", axis=0, axis_index_groups=peers)


def neighbours(axes, first, last):
    size = lax.axis_size(axes)
    up = [(i, i + 1) for i in range(size - 1)]
    down = [(i + 1, i) for i in range(size - 1)]
    return lax.ppermute(last, axes, up), lax.ppermute(first, axes, down)


def local(
    query_in,
    key_in,
    value_in,
    residual,
    layer_gain,
    proj_weight,
    conv_kernel,
    batch_gamma,
    batch_beta,
    stale_mean,
    stale_variance,
    grad_conv,
    grad_stream_in,
):
    groups = lax.axis_size("tm")
    frame_total = FR * groups * lax.axis_size("seq")
    gain = layer_gain.reshape(1, D)
    vectors = jnp.stack([batch_gamma, batch_beta, stale_mean, stale_variance])
    in_hbm = pl.BlockSpec(memory_space=pltpu.HBM)
    in_vmem = pl.BlockSpec(memory_space=pltpu.VMEM)

    edge_rows = EDGE + EDGE // 2
    block = pltpu.VMEM((FR, D), bf16)
    packed, row_first, row_last = call(
        pack_kernel,
        (shape((HEADS, 3 * HD + 128, FR), bf16), shape((edge_rows, D), bf16), shape((edge_rows, D), bf16)),
        weight_chunk().reshape(1),
        *map(in_high_memory, (query_in, key_in, value_in, proj_weight, residual, grad_conv)),
        in_specs=[pl.BlockSpec(memory_space=pltpu.SMEM)] + [in_hbm] * 6,
        scratch=(block, block, block, pltpu.VMEM((128, 128), bf16), pltpu.SemaphoreType.DMA((8,))),
    )
    before, after = neighbours(("tm", "seq"), row_first, row_last)
    qkv = lax.all_to_all(packed, "seq", 0, 0, tiled=True)
    weights = gather_weights(qkv[:, 3 * HD :])
    square = shape((STRETCH, 128), bf16)
    scores = [pltpu.VMEM((TALL, STRETCH), f32)] * 2
    keys, queries, values, edge_nat, edge_att, edge_log, first, last = call(
        edge_forward_kernel,
        (
            shape((128, STRETCH), bf16),
            square,
            square,
            shape((2 * TALL, 128), bf16),
            shape((2, HD, TALL), bf16),
            shape((2, 8, TALL), f32),
            shape((EDGE, 128), bf16),
            shape((EDGE, 128), bf16),
        ),
        qkv,
        scratch=scores,
    )
    edge_before, edge_after = neighbours("tm", first, last)
    mid_nat, mid_att, mid_log = call(
        middle_forward_kernel,
        (
            shape((STRETCH - 2 * TALL, 128), bf16),
            shape((TALLS - 2, HD, TALL), bf16),
            shape((TALLS - 2, 8, TALL), f32),
        ),
        keys,
        queries,
        values,
        scratch=scores,
        gflops=6,
    )
    att_payload = call(
        assemble_kernel,
        shape((HEADS, 64 + EDGE, 128), bf16),
        edge_nat,
        mid_nat,
        edge_before,
        edge_after,
    )
    att_payload, before, after = lax.optimization_barrier((att_payload, before, after))
    att_rows = lax.all_to_all(att_payload, "seq", 0, 0, tiled=True)
    grad_stream, payload = call(
        middle_kernel,
        (shape((FR, D), bf16), shape((HEADS, PART_ROWS + HD, FR), bf16)),
        att_rows,
        residual,
        before,
        after,
        gain,
        in_high_memory(weights),
        conv_kernel,
        vectors,
        grad_conv,
        grad_stream_in,
        in_specs=[in_vmem] * 5 + [in_hbm] + [in_vmem] * 4,
        scratch=(
            pltpu.VMEM((8, HEADS, 128, 128), bf16),
            pltpu.VMEM((ROWS, D), f32),
            pltpu.VMEM((ROWS, D), bf16),
            pltpu.VMEM((8, FR, 128), f32),
            pltpu.VMEM((8, FR, 128), f32),
            pltpu.VMEM((8, ROWS, 128), f32),
            pltpu.VMEM((WIDE, 128), f32),
            pltpu.VMEM((HEADS, PART_ROWS, 128), f32),
            pltpu.VMEM((FR, 2 * D), bf16),
            pltpu.VMEM((FR, D), f32),
            pltpu.SemaphoreType.DMA((HEADS,)),
        ),
    )
    payload = lax.all_to_all(payload, "seq", 0, 0, tiled=True)
    spread = call(
        spread_kernel,
        shape((groups, PART_ROWS, 128), bf16),
        payload,
        grid=(1,),
        in_specs=[whole(HEADS, PART_ROWS, 128)],
        out_specs=whole(groups, PART_ROWS, 128),
    )
    totals = lax.all_to_all(spread, "tm", 0, 0, tiled=True)
    tall = pltpu.VMEM((STRETCH, 128), bf16)
    flat = pltpu.VMEM((128, STRETCH), bf16)
    back = call(
        backward_kernel,
        shape((HEADS, 3 * HD + PART_ROWS, FR), bf16),
        qkv,
        edge_att,
        mid_att,
        edge_log,
        mid_log,
        payload,
        gflops=12,
        scratch=(
            tall,
            tall,
            flat,
            flat,
            tall,
            tall,
            pltpu.VMEM((HD, STRETCH), bf16),
            pltpu.VMEM((HD, STRETCH), f32),
        ),
    )
    back = call(
        finish_kernel,
        shape(back.shape, bf16),
        totals,
        back,
        grid=(1,),
        in_specs=[whole(groups, PART_ROWS, 128), pl.BlockSpec(memory_space=pl.ANY)],
        out_specs=pl.BlockSpec((HEADS, PART_ROWS, 128), lambda i: (0, 6, 0)),
        input_output_aliases={1: 0},
    )
    back = lax.all_to_all(back, "seq", 0, 0, tiled=True)
    narrow = shape((FR, D), bf16)
    query_grad, key_grad, value_grad, kernel_sum, affine_sum, moments = call(
        lambda *refs: unpack_kernel(frame_total, *refs),
        (narrow, narrow, narrow, shape((KW, D), f32), shape((2, D), f32), shape((2, D), f32)),
        back,
    )
    return (query_grad, key_grad, value_grad, grad_stream, kernel_sum, affine_sum, moments)


def solution(mesh):
    rows = P(("tm", "seq"), None)
    in_specs = (rows, rows, rows, rows, P(), P(None, "seq"), P(), P(), P(), P(), P(), rows, rows)
    out_specs = (rows, rows, rows, rows, P(), P(), P())
    return jax.shard_map(local, mesh=mesh, in_specs=in_specs, out_specs=out_specs, check_vma=False)
```
